32 devices in a mesh: dp: 8 (over z, y), head: 4 (over x, core).
Axes of the slice: x: 2, y: 2, z: 4, core: 2. Of those that a mesh axis runs over, the one named last changes fastest.
Arguments:
- cell_input: bfloat16 [24576, 512], P(('dp', 'head')), may hold values from -6 to 6
- lengths: int32 [96], P(('dp', 'head')), may hold values from 0 to 256, as said below
- pair_ids: int32 [96], P(('dp', 'head')), may hold values from 0 to 3, as said below
- cotangent: bfloat16 [24576, 512], P(('dp', 'head')), may hold values from -6 to 6
- norm_gains: bfloat16 [4, 512], replicated, may hold values from 0.5 to 1.5
- wide_gain: bfloat16 [2048], replicated, may hold values from 0.5 to 1.5
- w_glu: bfloat16 [512, 1024], replicated, may hold values from -0.25 to 0.25
- w_left: bfloat16 [512, 2048], replicated, may hold values from -0.25 to 0.25
- w_conv3: bfloat16 [3, 512, 256], replicated, may hold values from -0.15625 to 0.15625
- w_depth: bfloat16 [9, 2048], replicated, may hold values from -2 to 2
- w_point: bfloat16 [2048, 256], replicated, may hold values from -0.125 to 0.125
- w_qkv: bfloat16 [512, 1536], replicated, may hold values from -0.25 to 0.25
- w_out: bfloat16 [512, 512], replicated, may hold values from -1 to 1
- w_up: bfloat16 [512, 2048], replicated, may hold values from -0.25 to 0.25
- w_down: bfloat16 [2048, 512], replicated, may hold values from -0.125 to 0.125
Outputs:
- cell_output: bfloat16 [24576, 512], P(('dp', 'head'))
- input_grad: float32 [24576, 512], P(('dp', 'head'))
- grad_norm_gains: float32 [4, 512], replicated
- grad_wide_gain: float32 [2048], replicated
- grad_glu: float32 [512, 1024], P('dp')
- grad_left: float32 [512, 2048], P('dp')
- grad_conv3: float32 [3, 512, 256], P(None, 'dp')
- grad_depth: float32 [9, 2048], replicated
- grad_point: float32 [2048, 256], P('dp')
- grad_qkv: float32 [512, 1536], P('dp')
- grad_out: float32 [512, 512], P('dp')
- grad_up: float32 [512, 2048], P('dp')
- grad_down: float32 [2048, 512], P('dp')
The draws below stay inside these ranges and needn't reach their ends.
Inputs may be any that keep to these rules, and one draw needn't show every extreme that they name: `lengths`: dead sentences have length 0 and stand after the live ones of their device; each device's first sentence is live with length 256; live sentences have 256 // 4 to 256 tokens. `pair_ids`: the first sentence of the device of flat index i (dp major) has pair id i modulo 4.
All inputs are finite; a program needn't handle non-finite values.
Results may differ from the reference program's by a relative error of at most 0.02.
Values may be sent and summed in bfloat16 or wider, within the bound.
A program may use at most 320 MiB of HBM per device.

```python
import math
import jax
import jax.numpy as jnp
from jax import lax

D = 512
HEADS = 8
DH = 64
FF = 2048
SEQ = 256
PAIRS = 4
SENT_DEV = 3
HALF = 256
SENTENCES = 96
TOKENS = 24576


def draw_lengths(key, part):
    key = jax.random.fold_in(key, 11)
    device_total = SENTENCES // SENT_DEV
    index = jnp.arange(SENTENCES, dtype=jnp.int32)
    owner = index // SENT_DEV
    slot_index = index % SENT_DEV
    live_count = 1 + (SENT_DEV - 1) * owner // max(device_total - 1, 1)
    drawn = jax.random.randint(key, (SENTENCES,), SEQ // 4, SEQ + 1)
    drawn = jnp.where(slot_index == 0, SEQ, drawn)
    return jnp.where(slot_index < live_count, drawn, 0).astype(jnp.int32)


def draw_pair_ids(key, part):
    key = jax.random.fold_in(key, 23)
    drawn = jax.random.randint(key, (SENTENCES,), 0, PAIRS)
    index = jnp.arange(SENTENCES, dtype=jnp.int32)
    return jnp.where(index % SENT_DEV == 0, index // SENT_DEV % PAIRS, drawn).astype(jnp.int32)


def level_of(key, shape, split, least, largest):
    loudness = 1.0
    for dim, shards_of in split:
        steps = jax.random.uniform(jax.random.fold_in(jax.random.fold_in(key, 6), dim), (shards_of,), jnp.float32, least / len(split), largest / len(split))
        loudness = loudness * jnp.repeat(jnp.exp(steps), shape[dim] // shards_of).reshape((-1,) + (1,) * (len(shape) - 1 - dim))
    return loudness


def bell_draw(key, dims, spread, limit, split=(), kind=jnp.bfloat16):
    array = jax.random.normal(key, dims, jnp.float32) * spread
    if len(split) > 0:
        array = level_of(key, dims, split, -0.22, 0.18) * array
    return jnp.clip(array, min=-limit, max=limit).astype(kind)


def setup_inputs(seed: int = 0) -> dict:
    seeds = jax.random.split(jax.random.key(seed), 16)
    return {
        "cell_input": bell_draw(seeds[0], (TOKENS, D), 1.0, 6.0, ((0, 32),)),
        "lengths": draw_lengths(jax.random.fold_in(seeds[15], 71), 0),
        "pair_ids": draw_pair_ids(jax.random.fold_in(seeds[15], 71), 0),
        "cotangent": bell_draw(seeds[3], (TOKENS, D), 1.0, 6.0, ((0, 32),)),
        "norm_gains": jnp.clip(1.0 + 0.1 * jax.random.normal(seeds[4], (4, D), jnp.float32), 0.5, 1.5).astype(jnp.bfloat16),
        "wide_gain": jnp.clip(1.0 + 0.1 * jax.random.normal(seeds[5], (FF,), jnp.float32), 0.5, 1.5).astype(jnp.bfloat16),
        "w_glu": bell_draw(seeds[6], (D, 2 * D), D ** -0.5, 0.25),
        "w_left": bell_draw(seeds[7], (D, FF), D ** -0.5, 0.25),
        "w_conv3": bell_draw(seeds[8], (3, D, HALF), (3 * D) ** -0.5, 0.15625),
        "w_depth": bell_draw(seeds[9], (9, FF), 9 ** -0.5, 2.0),
        "w_point": bell_draw(seeds[10], (FF, HALF), FF ** -0.5, 0.125),
        "w_qkv": bell_draw(seeds[11], (D, 3 * D), D ** -0.5, 0.25),
        "w_out": bell_draw(seeds[12], (D, D), (D // 16) ** -0.5, 1.0),
        "w_up": bell_draw(seeds[13], (D, FF), D ** -0.5, 0.25),
        "w_down": bell_draw(seeds[14], (FF, D), FF ** -0.5, 0.125),
    }


@jax.custom_vjp
def low(v):
    return lax.optimization_barrier(v.astype(jnp.bfloat16)).astype(jnp.float32)

@jax.custom_vjp
def low_back(v):
    return v

def low_keep(v):
    return (low(v), None)

def low_pass(kept, grad):
    return (grad,)

def back_keep(v):
    return (v, None)

def back_low(kept, grad):
    return (low(grad),)
low.defvjp(low_keep, low_pass)
low_back.defvjp(back_keep, back_low)
epsilon = 1e-05
highest_mode = lax.Precision.HIGHEST

def layer_norm(values, scaling):
    centred = values - lax.optimization_barrier(jnp.mean(values, axis=-1, keepdims=True))
    variance = lax.optimization_barrier(jnp.mean(centred * centred, axis=-1, keepdims=True))
    return centred * lax.rsqrt(variance + epsilon) * scaling

def project(values, weights):
    return jnp.einsum('std,de->ste', values, weights, precision=highest_mode)

def shift_seq(values, offset):
    length_now = values.shape[1]
    padded = jnp.pad(values, ((0, 0), (4, 4), (0, 0)))
    return padded[:, 4 + offset:4 + offset + length_now]

def cell(inputs, sent_lengths, norm_gains, wide_gain, w_glu, w_left, w_conv3, w_depth, w_point, w_qkv, w_out, w_up, w_down):
    sent_count = inputs.shape[0]
    model_width = inputs.shape[-1]
    half_width = w_point.shape[1]
    wide_width = w_left.shape[1]
    position = lax.broadcasted_iota(jnp.int32, (sent_count, SEQ), 1)
    live = (position < sent_lengths[:, None]).astype(jnp.float32)[..., None]
    valid_keys = position < jnp.maximum(sent_lengths, 1)[:, None]
    normed_a = low(layer_norm(inputs, norm_gains[0]))
    glu_pre = low_back(project(normed_a, w_glu))
    after_glu = inputs + glu_pre[..., :model_width] * jax.nn.sigmoid(glu_pre[..., model_width:])
    normed_b = low(layer_norm(after_glu, norm_gains[1]) * live)
    left_part = jax.nn.gelu(low_back(project(normed_b, w_left)))
    stacked = jnp.concatenate([shift_seq(normed_b, -1), normed_b, shift_seq(normed_b, 1)], axis=-1)
    right_part = jax.nn.gelu(low_back(project(stacked, w_conv3.reshape(3 * model_width, half_width))))
    hidden = left_part + jnp.pad(right_part, ((0, 0), (0, 0), (0, wide_width - half_width)))
    masked_c = layer_norm(hidden, wide_gain) * live
    depth = masked_c * w_depth[4]
    for offset in range(-4, 5):
        if offset != 0:
            depth = depth + shift_seq(masked_c, offset) * w_depth[offset + 4]
    sep = low_back(project(low(depth), w_point))
    after_conv = after_glu + jnp.pad(sep, ((0, 0), (0, 0), (0, model_width - half_width)))
    normed_e = low(layer_norm(after_conv, norm_gains[2]))
    qkv = low(low_back(project(normed_e, w_qkv))).reshape(sent_count, SEQ, HEADS, 3 * DH)
    queries = qkv[..., :DH]
    key_rows = qkv[..., DH:2 * DH]
    value_rows = qkv[..., 2 * DH:]
    raw_scores = jnp.einsum('bshe,bthe->bhst', queries, key_rows, precision=highest_mode) * DH ** (-0.5)
    scores = jnp.where(valid_keys[:, None, None, :], low_back(raw_scores), -1e+30)
    attn_probs = low(jax.nn.softmax(scores, axis=-1))
    mixed = jnp.einsum('bhst,bthe->bshe', attn_probs, value_rows, precision=highest_mode)
    mixed = low(low_back(mixed)).reshape(sent_count, SEQ, model_width)
    after_attn = after_conv + low_back(project(mixed, w_out))
    normed_f = low(layer_norm(after_attn, norm_gains[3]))
    up_low = low(jax.nn.gelu(low_back(project(normed_f, w_up))))
    return after_attn + low_back(project(up_low, w_down))

def reference(cell_input, lengths, pair_ids, cotangent, norm_gains, wide_gain, w_glu, w_left, w_conv3, w_depth, w_point, w_qkv, w_out, w_up, w_down):
    sent_total = lengths.shape[0]
    model_width = cell_input.shape[-1]
    onehot = (pair_ids[:, None] == jnp.arange(PAIRS, dtype=jnp.int32)[None, :]).astype(jnp.float32)
    counts = lax.optimization_barrier(jnp.sum(onehot * lengths[:, None].astype(jnp.float32), axis=0))
    live_total = jnp.sum(counts)
    factor = live_total / (PAIRS * lax.optimization_barrier(jnp.sum(onehot * counts[None, :], axis=1)))
    position = lax.broadcasted_iota(jnp.int32, (sent_total, SEQ), 1)
    live = (position < lengths[:, None]).astype(jnp.float32)
    row_weight = live * factor[:, None]
    block_size = math.gcd(sent_total, max(1, 4096 // SEQ))
    block_count = sent_total // block_size
    inputs = cell_input.astype(jnp.float32).reshape(block_count, block_size, SEQ, model_width)
    upstream = (cotangent.astype(jnp.float32).reshape(sent_total, SEQ, model_width) * row_weight[..., None]).reshape(block_count, block_size, SEQ, model_width)
    length_blocks = lengths.reshape(block_count, block_size)
    params = tuple((p_arg.astype(jnp.float32) for p_arg in (norm_gains, wide_gain, w_glu, w_left, w_conv3, w_depth, w_point, w_qkv, w_out, w_up, w_down)))

    def step(carry, pieces):
        block_in, block_len, block_up = pieces

        def apply_cell(values, *weights):
            return cell(values, block_len, *weights)
        result, pull_back = jax.vjp(apply_cell, block_in, *params)
        grads = pull_back(block_up)
        summed = tuple((c_old + g_new for c_old, g_new in zip(carry, grads[1:])))
        return (summed, (result.astype(jnp.bfloat16), grads[0]))
    zero_grads = tuple((jnp.zeros_like(p_arg) for p_arg in params))
    sums, (results, input_grads) = lax.scan(step, zero_grads, (inputs, length_blocks, upstream))
    tokens_all = sent_total * SEQ
    return (results.reshape(tokens_all, model_width), input_grads.reshape(tokens_all, model_width), sums[0], sums[1], sums[2], sums[3], sums[4], sums[5], sums[6], sums[7], sums[8], sums[9], sums[10])
```

```python
import functools

import jax
import jax.numpy as jnp
from jax import lax
from jax.experimental import pallas as pl
from jax.experimental.pallas import tpu as pltpu
from jax.sharding import PartitionSpec as P

HEADS = 8
DH = 64
SEQ = 256
PAIRS = 4
D = 512
FF = 2048
HALF = 256
PAD = SEQ + 16
EPS = 1e-05
MESH = pl.DeviceIdType.MESH
bf = jnp.bfloat16
f32 = jnp.float32
GELU_A = 0.7978845608028654
GELU_B = 0.7978845608028654 * 0.044715
CH = 32


def nn(a, b):
    return lax.dot_general(a, b, (((1,), (0,)), ((), ())), preferred_element_type=f32)


def nt(a, b):
    return lax.dot_general(a, b, (((1,), (1,)), ((), ())), preferred_element_type=f32)


def tn(a, b):
    return lax.dot_general(a, b, (((0,), (0,)), ((), ())), preferred_element_type=f32)


def gelu_both(v):
    square = v * v
    t = jnp.tanh(v * (GELU_A + GELU_B * square))
    half = 0.5 + 0.5 * t
    slope = half + (0.5 * v) * (1.0 - t * t) * (GELU_A + (3.0 * GELU_B) * square)
    return v * half, slope


def sigmoid(v):
    return 0.5 + 0.5 * jnp.tanh(0.5 * v)


def fold8(v):
    total = v[0:8]
    for i in range(1, v.shape[0] // 8):
        total = total + v[8 * i : 8 * i + 8]
    return total


def norm(v):
    centred = v - jnp.mean(v, axis=-1, keepdims=True)
    rstd = lax.rsqrt(jnp.mean(centred * centred, axis=-1, keepdims=True) + EPS)
    return centred, rstd


def norm_back(g, low, gain, inverse, rstd):
    gy = g * gain
    m1 = jnp.mean(gy, axis=-1, keepdims=True)
    m2 = jnp.mean(g * low, axis=-1, keepdims=True)
    return rstd * (gy - m1 - (low * inverse) * m2)


def at(s, first, size):
    return pl.ds(pl.multiple_of(s * SEQ + first, size), size)


def row_of(first, size):
    return first + lax.broadcasted_iota(jnp.int32, (size, 1), 0)


KEPT = (
    "a", "b", "e", "f", "rstd", "sig", "u", "dgl", "dgr", "m",
    "depth", "qkvt", "pt", "mixt", "up", "gup", "ga", "gmixt", "gain_f",
)


def kept_shapes(sents):
    rows = sents * SEQ
    shape = jax.ShapeDtypeStruct
    return {
        "a": shape((rows, D), bf),
        "b": shape((rows, D), bf),
        "e": shape((rows, D), bf),
        "f": shape((rows, D), bf),
        "rstd": shape((rows, 8), f32),
        "sig": shape((rows, D), bf),
        "u": shape((rows, D), bf),
        "dgl": shape((rows, FF), bf),
        "dgr": shape((rows, HALF), bf),
        "m": shape((sents, 16, PAD, 128), f32),
        "depth": shape((8, sents, SEQ, 256), bf),
        "qkvt": shape((3 * D, rows), bf),
        "pt": shape((sents, HEADS, SEQ, SEQ), bf),
        "mixt": shape((D, rows), bf),
        "up": shape((rows, FF), bf),
        "gup": shape((rows, FF), bf),
        "ga": shape((rows, D), f32),
        "gmixt": shape((D, rows), bf),
        "gain_f": shape((sents * 8, D), f32),
    }


def part_of(name, s):
    if name in ("m", "pt"):
        return (s,)
    if name == "depth":
        return (slice(None), s)
    if name in ("qkvt", "mixt", "gmixt"):
        return (slice(None), pl.ds(pl.multiple_of(s * SEQ, SEQ), SEQ))
    if name == "gain_f":
        return (pl.ds(pl.multiple_of(s * 8, 8), 8),)
    return (pl.ds(pl.multiple_of(s * SEQ, SEQ), SEQ),)


def front_kernel(
    sents,
    len_ref,
    x_ref,
    cot_ref,
    gains_ref,
    wg_ref,
    wglu,
    wleft,
    wconv,
    wdepth,
    wpoint,
    wqkv,
    wout,
    wup,
    wdown,
    out_ref,
    *refs,
):
    far, refs = dict(zip(KEPT, refs)), refs[len(KEPT) :]
    near, refs = dict(zip(KEPT, refs)), refs[len(KEPT) :]
    ship_sems, wp_ref, xf_ref, bs_ref, wide_ref, sep_ref, qkv_ref = refs
    (a_ref, b_ref, e_ref, f_ref, rstd_ref, sig_ref, u_ref, dgl_ref, dgr_ref, m_ref) = [near[n] for n in KEPT[:10]]
    (depth_ref, qkvt_ref, pt_ref, mixt_ref, up_ref, gup_ref, ga_ref, gmixt_ref, gain_f_ref) = [near[n] for n in KEPT[10:]]

    def shipment(name, s):
        k = KEPT.index(name)
        where = part_of(name, s)
        return pltpu.make_async_copy(near[name].at[where], far[name].at[where], ship_sems.at[k, s])

    def ship(s, *names):
        for name in names:
            shipment(name, s).start()

    wp_ref[0:9, :] = wdepth[...].astype(f32) * wg_ref[...].astype(f32)
    gain_f_ref[...] = jnp.zeros_like(gain_f_ref)
    zero8 = jnp.zeros((8, 128), f32)

    def sentence(s, carry):
        length = len_ref[s]
        gains = gains_ref[...].astype(f32)
        rows = at(s, 0, SEQ)
        for c in range(0, SEQ, CH):
            cen, rstd = norm(x_ref[at(s, c, CH), :].astype(f32))
            a_ref[at(s, c, CH), :] = (cen * rstd * gains[0:1]).astype(bf)
            rstd_ref[at(s, c, CH), 0:1] = rstd
        a_low = a_ref[rows, :]
        for n in range(2):
            cols = slice(256 * n, 256 * n + 256)
            gcols = slice(512 + 256 * n, 768 + 256 * n)
            value = nn(a_low, wglu[:, cols])
            gate = nn(a_low, wglu[:, gcols])
            for c in range(0, SEQ, CH):
                sig = sigmoid(gate[c : c + CH])
                mixed = value[c : c + CH] * sig
                xf_ref[c : c + CH, cols] = x_ref[at(s, c, CH), cols].astype(f32) + mixed
                sig_ref[at(s, c, CH), cols] = sig.astype(bf)
                u_ref[at(s, c, CH), cols] = (mixed * (1.0 - sig)).astype(bf)
        ship(s, "a", "sig", "u")
        for c in range(0, SEQ, CH):
            cen, rstd = norm(xf_ref[c : c + CH, :])
            rstd = jnp.where(row_of(c, CH) < length, rstd, 0.0)
            b_low = cen * rstd * gains[1:2]
            b_ref[at(s, c, CH), :] = b_low.astype(bf)
            rstd_ref[at(s, c, CH), 1:2] = rstd
            bs_ref[8 + c : 8 + c + CH, :] = b_low
        b_low = b_ref[rows, :]
        bs_ref[0:8, :] = jnp.zeros((8, D), f32)
        bs_ref[8 + SEQ : 16 + SEQ, :] = jnp.zeros((8, D), f32)
        right = (
            nn(bs_ref[7 : 7 + SEQ, :].astype(bf), wconv[0])
            + nn(b_low, wconv[1])
            + nn(bs_ref[9 : 9 + SEQ, :].astype(bf), wconv[2])
        )
        for n in range(8):
            cols = slice(256 * n, 256 * n + 256)
            left = nn(b_low, wleft[:, cols])
            for c in range(0, SEQ, CH):
                hidden, slope = gelu_both(left[c : c + CH])
                dgl_ref[at(s, c, CH), cols] = slope.astype(bf)
                if n == 0:
                    extra, slope = gelu_both(right[c : c + CH])
                    dgr_ref[at(s, c, CH), :] = slope.astype(bf)
                    hidden = hidden + extra
                wide_ref[c : c + CH, cols] = hidden
        ship(s, "b", "dgl", "dgr")
        for j in range(16):
            m_ref[s, j, 0:8, :] = zero8
            m_ref[s, j, 8 + SEQ : PAD, :] = zero8
        for c in range(0, SEQ, 8):
            mean = jnp.mean(wide_ref[c : c + 8, :], axis=-1, keepdims=True)
            cen = wide_ref[c : c + 8, :] - mean
            rstd = lax.rsqrt(jnp.mean(cen * cen, axis=-1, keepdims=True) + EPS)
            rstd = jnp.where(row_of(c, 8) < length, rstd, 0.0)
            rstd_ref[at(s, c, 8), 2:3] = rstd
            for j in range(16):
                m_ref[s, j, 8 + c : 16 + c, :] = cen[:, 128 * j : 128 * j + 128] * rstd
        for j in range(16):
            cols = slice(128 * j, 128 * j + 128)
            taps = [wp_ref[o : o + 1, cols] for o in range(9)]
            for c in range(0, SEQ, CH):
                total = m_ref[s, j, c + 4 : c + 4 + CH, :] * taps[0]
                for o in range(1, 9):
                    total = total + m_ref[s, j, c + 4 + o : c + 4 + o + CH, :] * taps[o]
                depth_ref[j // 2, s, c : c + CH, 128 * (j % 2) : 128 * (j % 2) + 128] = total.astype(bf)
        ship(s, "m", "depth")
        depth = jnp.concatenate([depth_ref[n, s] for n in range(8)], axis=1)
        sep_ref[...] = nn(depth, wpoint[...])
        for c in range(0, SEQ, CH):
            conv = xf_ref[c : c + CH, :]
            conv = jnp.concatenate([conv[:, :HALF] + sep_ref[c : c + CH, :], conv[:, HALF:]], axis=1)
            xf_ref[c : c + CH, :] = conv
            cen, rstd = norm(conv)
            e_ref[at(s, c, CH), :] = (cen * rstd * gains[2:3]).astype(bf)
            rstd_ref[at(s, c, CH), 3:4] = rstd
        e_low = e_ref[rows, :]
        for n in range(6):
            cols = slice(256 * n, 256 * n + 256)
            part = nn(e_low, wqkv[:, cols]).astype(bf)
            qkv_ref[:, cols] = part
            qkvt_ref[cols, at(s, 0, SEQ)] = part.T
        ship(s, "e", "qkvt")
        bias = jnp.where(row_of(0, SEQ) < jnp.maximum(length, 1), 0.0, -1e30)
        for h in range(HEADS):
            base = 3 * DH * h
            key = qkv_ref[:, base + DH : base + 2 * DH] * jnp.asarray(DH**-0.5, bf)
            query_t = qkvt_ref[base : base + DH, at(s, 0, SEQ)]
            value_t = qkvt_ref[base + 2 * DH : base + 3 * DH, at(s, 0, SEQ)]
            for q in range(0, SEQ, 128):
                scores = nn(key, query_t[:, q : q + 128]) + bias
                scores = jnp.exp(scores - jnp.max(scores, axis=0, keepdims=True))
                scores = scores * (1.0 / jnp.sum(scores, axis=0, keepdims=True))
                pt_ref[s, h, :, q : q + 128] = scores.astype(bf)
            mixt_ref[DH * h : DH * h + DH, at(s, 0, SEQ)] = nn(value_t, pt_ref[s, h]).astype(bf)
        ship(s, "pt", "mixt")
        for n in range(2):
            cols = slice(256 * n, 256 * n + 256)
            xf_ref[:, cols] += tn(mixt_ref[:, at(s, 0, SEQ)], wout[:, cols])
        for c in range(0, SEQ, CH):
            cen, rstd = norm(xf_ref[c : c + CH, :])
            f_ref[at(s, c, CH), :] = (cen * rstd * gains[3:4]).astype(bf)
            rstd_ref[at(s, c, CH), 4:5] = rstd
        f_low = f_ref[rows, :]
        for n in range(8):
            cols = slice(256 * n, 256 * n + 256)
            up = nn(f_low, wup[:, cols])
            for c in range(0, SEQ, CH):
                low, slope = gelu_both(up[c : c + CH])
                up_ref[at(s, c, CH), cols] = low.astype(bf)
                gup_ref[at(s, c, CH), cols] = slope.astype(bf)
        for n in range(2):
            cols = slice(256 * n, 256 * n + 256)
            down = nn(up_ref[rows, :], wdown[:, cols])
            out_ref[rows, cols] = (xf_ref[:, cols] + down).astype(bf)
        ship(s, "f", "rstd", "up")
        for c in range(0, SEQ, CH):
            live = row_of(c, CH) < length
            ga_ref[at(s, c, CH), :] = jnp.where(live, cot_ref[at(s, c, CH), :].astype(f32), 0.0)
        g_low = ga_ref[rows, :].astype(bf)
        for n in range(8):
            cols = slice(256 * n, 256 * n + 256)
            back = nt(g_low, wdown[cols, :])
            gup_ref[rows, cols] = (back * gup_ref[rows, cols].astype(f32)).astype(bf)
        ship(s, "gup")
        for n in range(2):
            cols = slice(256 * n, 256 * n + 256)
            wide_ref[:, cols] = nt(gup_ref[rows, :], wup[cols, :])
        inverse = 1.0 / gains[3:4]
        for c in range(0, SEQ, CH):
            g_f = wide_ref[c : c + CH, 0:D]
            low = f_ref[at(s, c, CH), :].astype(f32)
            gain_f_ref[pl.ds(pl.multiple_of(s * 8, 8), 8), :] += fold8(g_f * low)
            back = norm_back(g_f, low, gains[3:4], inverse, rstd_ref[at(s, c, CH), 4:5])
            ga_ref[at(s, c, CH), :] += back
        gmixt_ref[:, at(s, 0, SEQ)] = nt(wout[...], ga_ref[rows, :].astype(bf)).astype(bf)
        ship(s, "ga", "gmixt", "gain_f")
        return carry

    lax.fori_loop(0, sents, sentence, 0)

    def landed(s, carry):
        for name in KEPT:
            shipment(name, s).wait()
        return carry

    lax.fori_loop(0, sents, landed, 0)


def vmem():
    return pl.BlockSpec(memory_space=pltpu.VMEM)


def smem():
    return pl.BlockSpec(memory_space=pltpu.SMEM)


def offsets(share, wide_share):
    sizes = (
        ("up", 8 * share, True),
        ("down", 2 * wide_share, True),
        ("out", 2 * share, False),
        ("qkv", 6 * share, True),
        ("point", wide_share, True),
        ("left", 2 * share, True),
        ("left1", 2 * share, True),
        ("left2", 2 * share, True),
        ("left3", 2 * share, True),
        ("conv", 3 * share, True),
        ("glu", 2 * share, True),
        ("glu1", 2 * share, True),
    )
    first, starts, groups, begin = 0, {}, [], 0
    for name, size, ends in sizes:
        starts[name] = first
        first += size
        if ends:
            first = -(-first // 32) * 32
            groups.append((begin, first - begin))
            begin = first
    return starts, groups, first


def put(g_ref, grid, tile, first, share, wide, chunk=0):
    _, ys = grid
    for part in range(tile.shape[1] // 256):
        for k in range(512 // share):
            block = chunk * (512 // share) + k
            piece = tile[k * share : (k + 1) * share, 256 * part : 256 * part + 256]
            rows = pl.ds(pl.multiple_of(first + part * share, 16), share)
            g_ref[block // ys, block % ys, rows, :] = piece.astype(bf)


def back_kernel(
    sents,
    grid,
    xs,
    names,
    len_ref,
    pair_ref,
    cot_far,
    gains_ref,
    wg_ref,
    wglu,
    wleft,
    wconv,
    wdepth,
    wpoint,
    wqkv,
    *refs,
):
    far, refs = dict(zip(KEPT, refs)), refs[len(KEPT) :]
    xgrad_far, final_far, early_far, late_far = refs[:4]
    recv, refs = dict(zip(names, refs[4:])), refs[4 + len(names) :]
    (
        fetch_sems,
        send_sems,
        recv_sems,
        g_ref,
        final_ref,
        count_ref,
        count_got,
        early_ref,
        early_got,
        late_ref,
        late_got,
        fac_ref,
        first_wide,
        second_wide,
        gqkv_ref,
        squares,
        conv_ref,
        gl_ref,
        fs_ref,
        gas_ref,
        mixt_ref,
        gmixt_ref,
        qkvt_ref,
        dgr_ref,
        rstd_ref,
        gain_f_ref,
        m_ref,
        wp_ref,
        gqkvt_ref,
        gd_ref,
        wide_ref,
        taps_ref,
        s1_ref,
        s2_ref,
        right_ref,
        gain_ref,
    ) = refs
    e_ref = gas_ref
    gr_refs = (gl_ref.at[:, 0:HALF], gl_ref.at[:, HALF:D], fs_ref.at[:, 0:HALF])
    sep_ref = fs_ref.at[:, HALF:D]
    up_ref = gleft_ref = dgl_ref = first_wide
    gup_ref = second_wide
    a_ref, b_ref, sig_ref, u_ref = [second_wide.at[:, D * k : D * k + D] for k in range(4)]
    gg_ref = gqkv_ref
    pt_ref, depth_view = squares, squares.reshape(8, sents, SEQ, 256)
    where = dict(
        a=a_ref, b=b_ref, e=e_ref, f=fs_ref, rstd=rstd_ref, sig=sig_ref, u=u_ref, dgl=first_wide, dgr=dgr_ref,
        qkvt=qkvt_ref, mixt=mixt_ref, up=first_wide, gup=second_wide, ga=conv_ref, gmixt=gmixt_ref, gain_f=gain_f_ref,
        pt=squares, depth=depth_view, cot=gl_ref,
    )
    far["cot"] = cot_far
    order = (
        "gmixt", "qkvt", "pt", "f", "gup", "ga", "cot", "up", "gain_f", "mixt", "rstd", "dgr",
        "e", "b", "a", "sig", "u", "dgl", "depth",
    )

    def fetch(name):
        return pltpu.make_async_copy(far[name], where[name], fetch_sems.at[order.index(name)])

    def start(*names):
        for name in names:
            fetch(name).start()

    def wait(*names):
        for name in names:
            fetch(name).wait()

    def fetch_m(s):
        return pltpu.make_async_copy(far["m"].at[s], m_ref.at[s % 2], fetch_sems.at[len(order) + s % 2])

    start(*order[:12])
    fetch_m(0).start()
    if sents > 1:
        fetch_m(1).start()
    share, wide_share = 512 // (grid[0] * grid[1]), 2048 // (grid[0] * grid[1])
    starts, groups, _ = offsets(share, wide_share)
    sums = Sums(grid, xs, groups, g_ref, final_ref, recv, send_sems, recv_sems)
    sums.greet()
    lane = lax.broadcasted_iota(jnp.int32, (8, 128), 1)
    counts = jnp.zeros((8, 128), f32)
    for s in range(sents):
        counts = counts + jnp.where(lane == pair_ref[s], len_ref[s].astype(f32), 0.0)
    count_ref[3] = counts
    sums.small_send(0, 3, count_ref, count_got)

    def count_next(axis):
        sums.small_next(0, axis, count_ref, count_got)
        if axis == 0:
            counts = count_ref[4]
            total = jnp.sum(counts, axis=1, keepdims=True)
            for s in range(sents):
                mine = jnp.sum(jnp.where(lane == pair_ref[s], counts, 0.0), axis=1, keepdims=True)
                fac_ref[s] = jnp.broadcast_to(total / (PAIRS * mine), (8, 128))

    def factor_of(s):
        return fac_ref[s, 0:1, 0:1]

    def between(s, events):
        for k, steps in enumerate(events):
            pl.when(s == min(k, sents - 1))(functools.partial(sums.do, steps))

    wp_ref[0:9, :] = wdepth[...].astype(f32) * wg_ref[...].astype(f32)
    gain_ref[...] = jnp.zeros_like(gain_ref)
    taps_ref[...] = jnp.zeros_like(taps_ref)

    wait("gmixt", "qkvt", "pt")

    def attend(first, s, carry):
        rows = at(s, 0, SEQ)
        for h in range(HEADS):
            base = 3 * DH * h
            g_o = gmixt_ref[DH * h : DH * h + DH, rows]
            query_t = qkvt_ref[base : base + DH, rows]
            key_t = qkvt_ref[base + DH : base + 2 * DH, rows]
            value = qkvt_ref[base + 2 * DH : base + 3 * DH, rows].T
            probs = pt_ref[s, h]
            halves = []
            for q in range(0, SEQ, 128):
                part = probs[:, q : q + 128].astype(f32)
                back = nn(value, g_o[:, q : q + 128])
                both = part * back
                halves.append((both - part * jnp.sum(both, axis=0, keepdims=True)).astype(bf))
            g_scores = jnp.concatenate(halves, axis=1)
            gqkvt_ref[base : base + DH, :] = (nn(key_t, g_scores) * DH**-0.5).astype(bf)
            gqkvt_ref[base + DH : base + 2 * DH, :] = (nt(query_t, g_scores) * DH**-0.5).astype(bf)
            gqkvt_ref[base + 2 * DH : base + 3 * DH, :] = nt(g_o, probs).astype(bf)
            if first and h % 2:
                count_next(3 - h // 2)
        factor = factor_of(s).astype(bf)
        for n in range(6):
            cols = slice(256 * n, 256 * n + 256)
            gqkv_ref[rows, cols] = gqkvt_ref[cols, :].T * factor
        if not first:
            between(s - 1, after_attend)
        return carry

    lax.fori_loop(0, 1, functools.partial(attend, True), 0)

    wait("f", "gup", "ga", "cot", "up", "gain_f", "mixt", "rstd")

    def scale(s, carry):
        factor = factor_of(s)
        length = len_ref[s]
        for c in range(0, SEQ, CH):
            rows = at(s, c, CH)
            weight = jnp.where(row_of(c, CH) < length, factor, 0.0)
            gl_ref[rows, :] = (gl_ref[rows, :].astype(f32) * weight).astype(bf)
            fs_ref[rows, :] = (fs_ref[rows, :].astype(f32) * factor).astype(bf)
            conv_ref[rows, :] = conv_ref[rows, :] * factor
            gas_ref[rows, :] = conv_ref[rows, :].astype(bf)
        gain_ref[24:32, :] += gain_f_ref[pl.ds(pl.multiple_of(s * 8, 8), 8), :] * factor
        return carry

    lax.fori_loop(0, sents, scale, 0)

    def wide_tile(i):
        return pl.ds(pl.multiple_of(i * 512, 512), 512)

    def grad_up(i, carry):
        put(g_ref, grid, tn(fs_ref[...], gup_ref[:, wide_tile(i)]), starts["up"] + i * 2 * share, share, False)
        return carry

    lax.fori_loop(0, 4, grad_up, 0)
    start("b", "a", "sig", "u")
    sums.advance(0)

    def grad_down(i, carry):
        put(g_ref, grid, tn(up_ref[:, wide_tile(i)], gl_ref[...]), starts["down"], wide_share, True, i)
        return carry

    lax.fori_loop(0, 4, grad_down, 0)
    start("dgl")
    sums.advance(1, 0)
    put(g_ref, grid, nn(mixt_ref[...], gas_ref[...]), starts["out"], share, False)
    start("e")
    sums.advance(1)
    after_attend = (sums.claim(0), sums.claim(1))
    lax.fori_loop(1, sents, functools.partial(attend, False), 0)
    start("depth")
    wait("e")

    def grad_qkv(i, carry):
        put(g_ref, grid, tn(e_ref[...], gqkv_ref[:, wide_tile(i)]), starts["qkv"] + i * 2 * share, share, False)
        return carry

    lax.fori_loop(0, 3, grad_qkv, 0)
    sums.advance(2, 0)

    def attention_input(s, carry):
        gains = gains_ref[...].astype(f32)
        inverse = 1.0 / gains[2:3]
        rows = at(s, 0, SEQ)
        for n in range(2):
            cols = slice(256 * n, 256 * n + 256)
            wide_ref[:, cols] = nt(gqkv_ref[rows, :], wqkv[cols, :])
        for c in range(0, SEQ, CH):
            part = at(s, c, CH)
            g_e = wide_ref[c : c + CH, 0:D]
            low = e_ref[part, :].astype(f32)
            gain_ref[16:24, :] += fold8(g_e * low)
            g_conv = conv_ref[part, :] + norm_back(g_e, low, gains[2:3], inverse, rstd_ref[part, 3:4])
            conv_ref[part, :] = g_conv
            sep_ref[part, :] = g_conv[:, :HALF].astype(bf)
        return carry

    lax.fori_loop(0, sents, attention_input, 0)

    sums.advance(2, 1)
    wait("depth")

    def grad_point(i, carry):
        depth = [depth_view[2 * i + k].reshape(sents * SEQ, 256) for k in range(2)]
        put(g_ref, grid, tn(jnp.concatenate(depth, axis=1), sep_ref[...]), starts["point"], wide_share, True, i)
        return carry

    lax.fori_loop(0, 4, grad_point, 0)
    sums.advance(3, 0)

    wait("b", "a", "sig", "u", "dgr", "dgl")
    after_wide = (sums.claim(3, 1, 2, 0), sums.claim(3, 2, 1), sums.claim(3, 2))

    zero8 = jnp.zeros((8, 128), f32)

    def wide(s, carry):
        rows = at(s, 0, SEQ)
        slot = s % 2
        fetch_m(s).wait()
        for n in range(8):
            back = nt(sep_ref[rows, :], wpoint[256 * n : 256 * n + 256, :])
            for k in range(2):
                gd_ref[2 * n + k, 8 : 8 + SEQ, :] = back[:, 128 * k : 128 * k + 128]
        for j in range(16):
            gd_ref[j, 0:8, :] = zero8
            gd_ref[j, 8 + SEQ : PAD, :] = zero8
            cols = slice(128 * j, 128 * j + 128)
            taps = [wp_ref[o : o + 1, cols] for o in range(9)]
            for c in range(0, SEQ, CH):
                total = gd_ref[j, c + 12 : c + 12 + CH, :] * taps[0]
                for o in range(1, 9):
                    total = total + gd_ref[j, c + 12 - o : c + 12 - o + CH, :] * taps[o]
                wide_ref[c : c + CH, cols] = total
                mine = m_ref[slot, j, c + 8 : c + 8 + CH, :]
                if j == 0:
                    s1_ref[c : c + CH, :] = total
                    s2_ref[c : c + CH, :] = total * mine
                else:
                    s1_ref[c : c + CH, :] += total
                    s2_ref[c : c + CH, :] += total * mine
            for o in range(9):
                sums = taps_ref[o, :, cols]
                for c in range(0, SEQ, CH):
                    sums = sums + fold8(m_ref[slot, j, c + 4 + o : c + 4 + o + CH, :] * gd_ref[j, c + 8 : c + 8 + CH, :])
                taps_ref[o, :, cols] = sums
        right_ref[0:8, :] = jnp.zeros((8, HALF), f32)
        right_ref[8 + SEQ : PAD, :] = jnp.zeros((8, HALF), f32)
        for c in range(0, SEQ, CH):
            part = at(s, c, CH)
            rstd = rstd_ref[part, 2:3]
            m1 = jnp.sum(s1_ref[c : c + CH, :], axis=-1, keepdims=True) * (rstd / FF)
            m2 = jnp.sum(s2_ref[c : c + CH, :], axis=-1, keepdims=True) * (rstd / FF)
            for j in range(16):
                cols = slice(128 * j, 128 * j + 128)
                g_h = wide_ref[c : c + CH, cols] * rstd - m1 - m_ref[slot, j, c + 8 : c + 8 + CH, :] * m2
                gleft_ref[part, cols] = (g_h * dgl_ref[part, cols].astype(f32)).astype(bf)
                if j < 2:
                    right_ref[8 + c : 8 + c + CH, cols] = g_h * dgr_ref[part, cols].astype(f32)
        @pl.when(s + 2 < sents)
        def _():
            fetch_m(s + 2).start()

        for k in range(3):
            gr_refs[k][rows, :] = right_ref[9 - k : 9 - k + SEQ, :].astype(bf)
        between(s, after_wide)
        return carry

    lax.fori_loop(0, sents, wide, 0)

    for i, waiting in enumerate(((2,), (4, 3), (5,), (6, 3))):
        put(g_ref, grid, tn(b_ref[...], gleft_ref[:, 512 * i : 512 * i + 512]), starts[("left", "left1", "left2", "left3")[i]], share, False)
        sums.advance(4 + i, *waiting)
    for k in range(3):
        put(g_ref, grid, tn(b_ref[...], gr_refs[k][...]), starts["conv"] + k * share, share, False)
    sums.advance(8, 7)

    wide_gain = wg_ref[...].astype(f32)
    total = jnp.zeros((1, FF), f32)
    for o in range(9):
        lines = jnp.sum(taps_ref[o], axis=0, keepdims=True)
        total = total + lines * wdepth[o : o + 1, :].astype(f32)
        for k in range(8):
            early_ref[3, 8 * o + k : 8 * o + k + 1, :] = (lines * wide_gain)[:, 256 * k : 256 * k + 256]
    for k in range(8):
        early_ref[3, 72 + k : 73 + k, :] = total[:, 256 * k : 256 * k + 256]

    def gain_rows(ref, first, i):
        lines = jnp.sum(gain_ref[8 * i : 8 * i + 8, :], axis=0, keepdims=True) / gains_ref[i : i + 1, :].astype(f32)
        for k in range(2):
            ref[3, first + k : first + k + 1, :] = lines[:, 256 * k : 256 * k + 256]

    early_ref[3, 80:88, :] = jnp.zeros((8, 256), f32)
    gain_rows(early_ref, 80, 2)
    gain_rows(early_ref, 82, 3)
    sums.small_send(1, 3, early_ref, early_got)

    def inputs(s, carry):
        gains = gains_ref[...].astype(f32)
        rows = at(s, 0, SEQ)
        for n in range(2):
            cols = slice(256 * n, 256 * n + 256)
            g_b = nt(gleft_ref[rows, :], wleft[cols, :])
            for k in range(3):
                g_b = g_b + nt(gr_refs[k][rows, :], wconv[k, cols, :])
            wide_ref[:, cols] = g_b
        inverse = 1.0 / gains[1:2]
        for c in range(0, SEQ, CH):
            part = at(s, c, CH)
            g_b = wide_ref[c : c + CH, 0:D]
            low = b_ref[part, :].astype(f32)
            gain_ref[8:16, :] += fold8(g_b * low)
            g_glu = conv_ref[part, :] + norm_back(g_b, low, gains[1:2], inverse, rstd_ref[part, 1:2])
            conv_ref[part, :] = g_glu
            gg_ref[part, 0:D] = (g_glu * sig_ref[part, :].astype(f32)).astype(bf)
            gg_ref[part, D : 2 * D] = (g_glu * u_ref[part, :].astype(f32)).astype(bf)
        for n in range(2):
            cols = slice(256 * n, 256 * n + 256)
            wide_ref[:, cols] = nt(gg_ref[rows, 0 : 2 * D], wglu[cols, :])
        inverse = 1.0 / gains[0:1]
        for c in range(0, SEQ, CH):
            part = at(s, c, CH)
            g_a = wide_ref[c : c + CH, 0:D]
            low = a_ref[part, :].astype(f32)
            gain_ref[0:8, :] += fold8(g_a * low)
            conv_ref[part, :] += norm_back(g_a, low, gains[0:1], inverse, rstd_ref[part, 0:1])
        between(s, after_inputs)
        return carry

    after_inputs = (sums.claim(8, 4), sums.claim(5, 6), sums.claim(7, 4))
    lax.fori_loop(0, sents, inputs, 0)
    leave = pltpu.make_async_copy(conv_ref, xgrad_far, fetch_sems.at[len(order) + 2])
    leave.start()
    late_ref[3] = jnp.zeros((8, 256), f32)
    gain_rows(late_ref, 0, 0)
    gain_rows(late_ref, 2, 1)
    sums.small_send(2, 3, late_ref, late_got)
    sums.small_next(1, 3, early_ref, early_got)
    for i, waiting in enumerate(((8, 5), (9, 6))):
        put(g_ref, grid, tn(a_ref[...], gg_ref[:, 512 * i : 512 * i + 512]), starts[("glu", "glu1")[i]], share, False)
        sums.advance(9 + i, *waiting)
    rounds = 0
    while any(stage < sums.STAGES for stage in sums.stage):
        sums.advance(*range(len(groups)))
        if rounds < 3:
            sums.small_next(1, 2 - rounds, early_ref, early_got)
        if rounds < 4:
            sums.small_next(2, 3 - rounds, late_ref, late_got)
        rounds += 1
    ends = (final_ref, final_far), (early_ref.at[4], early_far), (late_ref.at[4], late_far)
    ends = [pltpu.make_async_copy(*pair, fetch_sems.at[len(order) + 3 + k]) for k, pair in enumerate(ends)]
    for copy in ends:
        copy.start()
    sums.finish()
    leave.wait()
    for copy in ends:
        copy.wait()


def coordinates(ys):
    dp, head = lax.axis_index("dp"), lax.axis_index("head")
    return dp // ys, dp % ys, head // 2, head % 2


def device(ys, z, y, x, c):
    return (z * ys + y, x * 2 + c)


def rows16(first, size):
    return pl.ds(pl.multiple_of(first, 16), size)


def split_of(size, xs):
    half = size // 2
    first = (half // (32 * xs)) * 16 * xs
    return half, first, half - first


class Sums:
    STAGES = 6

    def __init__(self, grid, xs, groups, g_ref, final_ref, recv, send_sems, recv_sems):
        self.zs, self.ys = grid
        self.xs = xs
        self.sizes = (*grid, xs, 2)
        self.groups = groups
        self.g, self.final = g_ref, final_ref
        self.recv = recv
        self.send_sems, self.recv_sems = send_sems, recv_sems
        self.place = coordinates(self.ys)
        self.stage = [-1] * len(groups)
        self.small = []

    def peers(self, axis):
        size = self.sizes[axis]
        for step in range(1, size):
            to = list(self.place)
            to[axis] = lax.rem(to[axis] + step, size)
            yield step - 1, to[axis], device(self.ys, *to)

    def greet(self):
        barrier = pltpu.get_barrier_semaphore()
        total = 0
        for axis in range(4):
            for _, _, to in self.peers(axis):
                pl.semaphore_signal(barrier, inc=1, device_id=to, device_id_type=MESH)
                total += 1
        pl.semaphore_wait(barrier, total)

    def core_first(self, i):
        return (self.groups[i][0] - (self.groups[3][0] if i > 2 else 0)) // 2

    def a_first(self, i):
        return sum(split_of(size, self.xs)[1] // self.xs for _, size in self.groups[:i])

    def b_first(self, i):
        return sum(split_of(size, self.xs)[2] for _, size in self.groups[:i])

    def rows(self, i):
        first, size = self.groups[i]
        half, na, nb = split_of(size, self.xs)
        mine = first + self.place[3] * half
        return first, half, mine, na, na // self.xs, mine + na, nb

    def plan(self, stage, i):
        z, y, x, c = self.place
        first, half, mine, na, part, b_row, nb = self.rows(i)
        g, recv, final = self.g, self.recv, self.final
        a_in, b_in = pl.ds(self.a_first(i), part), pl.ds(self.b_first(i), nb)
        a_rows, b_rows = rows16(mine + x * part, part), rows16(b_row, nb)
        axis_a, axis_b = ((None, 3), (2, 1), (1, 0), (0, 2), (2, 3), (3, None))[stage]
        copies_a, copies_b = [], []
        for slot, other, to in self.peers(axis_b) if axis_b is not None else ():
            if stage == 0:
                source = g.at[:, :, rows16(first + other * half, half), :]
                target = recv["core"].at[:, :, pl.ds(self.core_first(i), half), :]
            elif stage == 1:
                source, target = g.at[:, other, b_rows, :], recv["b1"].at[slot, :, b_in, :]
            elif stage == 2:
                source, target = g.at[other, y, b_rows, :], recv["b2"].at[slot, b_in, :]
            elif stage == 3:
                source, target = g.at[z, y, b_rows, :], recv["b3"].at[slot, b_in, :]
            else:
                source, target = final.at[b_rows, :], final.at[b_rows, :]
            copies_b.append((source, target, to))
        for slot, other, to in self.peers(axis_a) if axis_a is not None and na else ():
            if stage == 1:
                source, target = g.at[:, :, rows16(mine + other * part, part), :], recv["a1"].at[slot, :, :, a_in, :]
            elif stage == 2:
                source, target = g.at[:, other, a_rows, :], recv["a2"].at[slot, :, a_in, :]
            elif stage == 3:
                source, target = g.at[other, y, a_rows, :], recv["a3"].at[slot, a_in, :]
            else:
                rows = a_rows if stage == 4 else rows16(mine, na)
                source, target = final.at[rows, :], final.at[rows, :]
            copies_a.append((source, target, to))
        return copies_b, copies_a

    def copies(self, stage, i):
        counts = self.counts(self.sizes)
        first = i * sum(map(sum, counts)) + sum(map(sum, counts[:stage]))
        copies_b, copies_a = self.plan(stage, i)
        made = []
        for copies, extra in ((copies_b, 0), (copies_a, counts[stage][0])):
            for n, (source, target, to) in enumerate(copies):
                index = first + extra + n
                made.append(
                    pltpu.make_async_remote_copy(
                        src_ref=source,
                        dst_ref=target,
                        send_sem=self.send_sems.at[index],
                        recv_sem=self.recv_sems.at[index],
                        device_id=to,
                        device_id_type=MESH,
                    )
                )
        return made

    @staticmethod
    def counts(sizes):
        z, y, x, _ = (size - 1 for size in sizes)
        return ((1, 0), (y, x), (z, y), (x, z), (1, x), (0, 1))

    @staticmethod
    def semaphores(grid, xs, groups):
        sizes = (*grid, xs, 2)
        return len(groups) * sum(map(sum, Sums.counts(sizes))) + 12 * (max(sizes) - 1)

    def claim(self, *groups):
        steps = []
        for i in groups:
            if self.stage[i] < self.STAGES:
                steps.append((i, self.stage[i]))
                self.stage[i] += 1
        return steps

    def do(self, steps):
        for i, stage in steps:
            if stage >= 0:
                for copy in self.copies(stage, i):
                    copy.wait_recv()
                self.add(stage, i)
            if stage + 1 < self.STAGES:
                for copy in self.copies(stage + 1, i):
                    copy.start()

    def advance(self, *groups):
        self.do(self.claim(*groups))

    def over(self, i):
        return self.stage[i] == self.STAGES

    def add(self, stage, i):
        z, y, x, c = self.place
        first, half, mine, na, part, b_row, nb = self.rows(i)
        g, recv = self.g, self.recv
        a_in, b_in = pl.ds(self.a_first(i), part), pl.ds(self.b_first(i), nb)
        a_rows, b_rows = rows16(mine + x * part, part), rows16(b_row, nb)

        def total(mine, got):
            value = mine.astype(f32)
            for other in got:
                value = value + other.astype(f32)
            return value.astype(bf)

        if stage == 0:

            def core(block, carry):
                zb, yb = block // self.ys, block % self.ys
                g[zb, yb, rows16(mine, half), :] += recv["core"][zb, yb, pl.ds(self.core_first(i), half), :]
                return carry

            lax.fori_loop(0, self.zs * self.ys, core, 0)
        elif stage == 1:

            def one(zb, carry):
                got = [recv["b1"][slot, zb, b_in, :] for slot in range(self.ys - 1)]
                g[zb, y, b_rows, :] = total(g[zb, y, b_rows, :], got)
                for yb in range(self.ys) if na else ():
                    got = [recv["a1"][slot, zb, yb, a_in, :] for slot in range(self.xs - 1)]
                    g[zb, yb, a_rows, :] = total(g[zb, yb, a_rows, :], got)
                return carry

            lax.fori_loop(0, self.zs, one, 0)
        elif stage == 2:
            g[z, y, b_rows, :] = total(g[z, y, b_rows, :], [recv["b2"][slot, b_in, :] for slot in range(self.zs - 1)])
            if na:

                def two(zb, carry):
                    got = [recv["a2"][slot, zb, a_in, :] for slot in range(self.ys - 1)]
                    g[zb, y, a_rows, :] = total(g[zb, y, a_rows, :], got)
                    return carry

                lax.fori_loop(0, self.zs, two, 0)
        elif stage == 3:
            got = [recv["b3"][slot, b_in, :] for slot in range(self.xs - 1)]
            self.final[b_rows, :] = total(g[z, y, b_rows, :], got)
            if na:
                got = [recv["a3"][slot, a_in, :] for slot in range(self.zs - 1)]
                self.final[a_rows, :] = total(g[z, y, a_rows, :], got)

    def small_copies(self, k, axis, held, got):
        most = max(self.sizes) - 1
        base = len(self.groups) * sum(map(sum, self.counts(self.sizes)))
        made = []
        for slot, other, to in self.peers(axis):
            index = base + (k * 4 + axis) * most + slot
            made.append(
                pltpu.make_async_remote_copy(
                    src_ref=held.at[axis],
                    dst_ref=got.at[self.got_first(axis) + slot],
                    send_sem=self.send_sems.at[index],
                    recv_sem=self.recv_sems.at[index],
                    device_id=to,
                    device_id_type=MESH,
                )
            )
        return made

    def got_first(self, axis):
        return sum(size - 1 for size in self.sizes[:axis])

    def small_send(self, k, axis, held, got):
        self.small.append((k, axis, held, got))
        for copy in self.small_copies(k, axis, held, got):
            copy.start()

    def small_add(self, k, axis, held, got):
        for copy in self.small_copies(k, axis, held, got):
            copy.wait_recv()
        size, me = self.sizes[axis], self.place[axis]
        total = None
        for n in range(size):
            value = held[axis]
            for slot in range(size - 1):
                value = jnp.where(lax.rem(me - slot - 1 + size, size) == n, got[self.got_first(axis) + slot], value)
            total = value if total is None else total + value
        held[axis - 1 if axis else 4] = total

    def small_next(self, k, axis, held, got):
        self.small_add(k, axis, held, got)
        if axis:
            self.small_send(k, axis - 1, held, got)

    def finish(self):
        for i in range(len(self.groups)):
            for stage in range(self.STAGES):
                for copy in self.copies(stage, i):
                    copy.wait_send()
        for small in self.small:
            for copy in self.small_copies(*small):
                copy.wait_send()


def recv_shapes(grid, xs, groups, height):
    zs, ys = grid
    na = sum(split_of(size, xs)[1] for _, size in groups) // xs
    nb = sum(split_of(size, xs)[2] for _, size in groups)
    na = max(na, 16)
    return {
        "core": (zs, ys, max(groups[3][0], height - groups[3][0]) // 2, 256),
        "a1": (xs - 1, zs, ys, na, 256),
        "b1": (ys - 1, zs, nb, 256),
        "a2": (ys - 1, zs, na, 256),
        "b2": (zs - 1, nb, 256),
        "a3": (zs - 1, na, 256),
        "b3": (xs - 1, nb, 256),
    }


SMALL = 88


def last_kernel(share, wide_share, final_ref, early_ref, late_ref, xgrad_in, *refs):
    xgrad_out, norms, wide_gain, glu, left, conv, depth, point, qkv, out, up, down, sem = refs
    move = pltpu.make_async_copy(xgrad_in, xgrad_out, sem)
    move.start()
    starts, _, _ = offsets(share, wide_share)
    for k in range(8):
        for o in range(9):
            depth[o : o + 1, 256 * k : 256 * k + 256] = early_ref[8 * o + k : 8 * o + k + 1, :]
        wide_gain[0:1, 256 * k : 256 * k + 256] = early_ref[72 + k : 73 + k, :]
    for i in range(4):
        ref, first = ((late_ref, 0), (late_ref, 2), (early_ref, 80), (early_ref, 82))[i]
        for k in range(2):
            norms[i : i + 1, 256 * k : 256 * k + 256] = ref[first + k : first + k + 1, :]
    for name, ref, tiles, size in (
        ("glu", glu, 4, share),
        ("left", left, 8, share),
        ("point", point, 1, wide_share),
        ("qkv", qkv, 6, share),
        ("out", out, 2, share),
        ("up", up, 8, share),
        ("down", down, 2, wide_share),
    ):
        for n in range(tiles):
            part = name + str(n // 2) if name + str(n // 2) in starts else name
            first = starts[part] + (n % 2 if part != name else n) * size
            ref[:, 256 * n : 256 * n + 256] = final_ref[first : first + size, :].astype(f32)
    for k in range(3):
        first = starts["conv"] + k * share
        conv[k] = final_ref[first : first + share, :].astype(f32)
    move.wait()


def local(
    grid,
    xs,
    cell_input,
    lengths,
    pair_ids,
    cotangent,
    norm_gains,
    wide_gain,
    w_glu,
    w_left,
    w_conv3,
    w_depth,
    w_point,
    w_qkv,
    w_out,
    w_up,
    w_down,
):
    zs, ys = grid
    dp = zs * ys
    share, wide_share = 512 // dp, 2048 // dp
    rows = cell_input.shape[0]
    sents = lengths.shape[0]
    starts, groups, height = offsets(share, wide_share)
    wg = wide_gain.reshape(1, FF)
    shape = jax.ShapeDtypeStruct
    params = pltpu.CompilerParams(vmem_limit_bytes=62 << 20)
    kept = kept_shapes(sents)
    anywhere = pl.BlockSpec(memory_space=pl.ANY)
    front = pl.pallas_call(
        functools.partial(front_kernel, sents),
        out_shape=[shape((rows, D), bf)] + list(kept.values()),
        in_specs=[smem()] + [vmem()] * 13,
        out_specs=[vmem()] + [anywhere] * len(kept),
        scratch_shapes=[pltpu.VMEM(v.shape, v.dtype) for v in kept.values()]
        + [
            pltpu.SemaphoreType.DMA((len(kept), sents)),
            pltpu.VMEM((16, FF), f32),
            pltpu.VMEM((SEQ, D), f32),
            pltpu.VMEM((PAD, D), f32),
            pltpu.VMEM((SEQ, FF), f32),
            pltpu.VMEM((SEQ, HALF), f32),
            pltpu.VMEM((SEQ, 3 * D), bf),
        ],
        compiler_params=params,
        name="front",
    )(lengths, cell_input, cotangent, norm_gains, wg, w_glu, w_left, w_conv3, w_depth, w_point, w_qkv, w_out, w_up, w_down)
    cell_output, arrays = front[0], front[1:]
    recv = recv_shapes(grid, xs, groups, height)
    most = zs + ys + xs - 2
    semaphores = Sums.semaphores(grid, xs, groups)
    input_grad, final, early, late = pl.pallas_call(
        functools.partial(back_kernel, sents, grid, xs, tuple(recv)),
        out_shape=[shape((rows, D), f32), shape((height, 256), bf), shape((SMALL, 256), f32), shape((8, 256), f32)],
        in_specs=[smem(), smem(), anywhere] + [vmem()] * 8 + [anywhere] * len(kept),
        out_specs=[anywhere] * 4,
        scratch_shapes=[pltpu.VMEM(v, bf) for v in recv.values()]
        + [
            pltpu.SemaphoreType.DMA((28,)),
            pltpu.SemaphoreType.DMA((semaphores,)),
            pltpu.SemaphoreType.DMA((semaphores,)),
            pltpu.VMEM((zs, ys, height, 256), bf),
            pltpu.VMEM((height, 256), bf),
            pltpu.VMEM((5, 8, 128), f32),
            pltpu.VMEM((most, 8, 128), f32),
            pltpu.VMEM((5, SMALL, 256), f32),
            pltpu.VMEM((most, SMALL, 256), f32),
            pltpu.VMEM((5, 8, 256), f32),
            pltpu.VMEM((most, 8, 256), f32),
            pltpu.VMEM((sents, 8, 128), f32),
            pltpu.VMEM((rows, FF), bf),
            pltpu.VMEM((rows, FF), bf),
            pltpu.VMEM((rows, 3 * D), bf),
            pltpu.VMEM((sents, HEADS, SEQ, SEQ), bf),
            pltpu.VMEM((rows, D), f32),
            pltpu.VMEM((rows, D), bf),
            pltpu.VMEM((rows, D), bf),
            pltpu.VMEM((rows, D), bf),
            pltpu.VMEM((D, rows), bf),
            pltpu.VMEM((D, rows), bf),
            pltpu.VMEM((3 * D, rows), bf),
            pltpu.VMEM((rows, HALF), bf),
            pltpu.VMEM((rows, 8), f32),
            pltpu.VMEM((sents * 8, D), f32),
            pltpu.VMEM((2, 16, PAD, 128), f32),
            pltpu.VMEM((16, FF), f32),
            pltpu.VMEM((3 * D, SEQ), bf),
            pltpu.VMEM((16, PAD, 128), f32),
            pltpu.VMEM((SEQ, FF), f32),
            pltpu.VMEM((9, 8, FF), f32),
            pltpu.VMEM((SEQ, 128), f32),
            pltpu.VMEM((SEQ, 128), f32),
            pltpu.VMEM((PAD, HALF), f32),
            pltpu.VMEM((32, D), f32),
        ],
        compiler_params=pltpu.CompilerParams(vmem_limit_bytes=63 << 20, collective_id=0, has_side_effects=True),
        name="back",
    )(lengths, pair_ids, cotangent, norm_gains, wg, w_glu, w_left, w_conv3, w_depth, w_point, w_qkv, *arrays)
    input_grad, norms, gain, glu, left, conv, depth, point, qkv, out, up, down = pl.pallas_call(
        functools.partial(last_kernel, share, wide_share),
        out_shape=[
            shape((rows, D), f32),
            shape((4, D), f32),
            shape((1, FF), f32),
            shape((share, 2 * D), f32),
            shape((share, FF), f32),
            shape((3, share, HALF), f32),
            shape((9, FF), f32),
            shape((wide_share, HALF), f32),
            shape((share, 3 * D), f32),
            shape((share, D), f32),
            shape((share, FF), f32),
            shape((wide_share, D), f32),
        ],
        in_specs=[vmem()] * 3 + [anywhere],
        out_specs=[anywhere] + [vmem()] * 11,
        scratch_shapes=[pltpu.SemaphoreType.DMA(())],
        compiler_params=params,
        name="last",
    )(final, early, late, input_grad)
    return cell_output, input_grad, norms, gain.reshape(FF), glu, left, conv, depth, point, qkv, out, up, down


def solution(mesh):
    dp, head = mesh.shape["dp"], mesh.shape["head"]
    ys = 2 ** ((dp.bit_length() - 1) // 2)
    grid = (dp // ys, ys)
    xs = head // 2
    row = P(("dp", "head"), None)
    in_specs = (row, P(("dp", "head")), P(("dp", "head")), row) + (P(),) * 11
    share = P("dp", None)
    out_specs = (row, row, P(), P(), share, share, P(None, "dp", None), P(), share, share, share, share, share)
    return jax.shard_map(
        functools.partial(local, grid, xs), mesh=mesh, in_specs=in_specs, out_specs=out_specs, check_vma=False
    )
```

```python
import functools

import jax
import jax.numpy as jnp
from jax import lax
from jax.experimental import pallas as pl
from jax.experimental.pallas import tpu as pltpu
from jax.sharding import PartitionSpec as P

HEADS = 8
DH = 64
SEQ = 256
PAIRS = 4
D = 512
FF = 2048
HALF = 256
PAD = SEQ + 16
EPS = 1e-05
MESH = pl.DeviceIdType.MESH
bf = jnp.bfloat16
f32 = jnp.float32
GELU_A = 0.7978845608028654
GELU_B = 0.7978845608028654 * 0.044715
CH = 32


def nn(a, b):
    return lax.dot_general(a, b, (((1,), (0,)), ((), ())), preferred_element_type=f32)


def nt(a, b):
    return lax.dot_general(a, b, (((1,), (1,)), ((), ())), preferred_element_type=f32)


def tn(a, b):
    return lax.dot_general(a, b, (((0,), (0,)), ((), ())), preferred_element_type=f32)


def gelu_both(v):
    square = v * v
    t = jnp.tanh(v * (GELU_A + GELU_B * square))
    half = 0.5 + 0.5 * t
    slope = half + (0.5 * v) * (1.0 - t * t) * (GELU_A + (3.0 * GELU_B) * square)
    return v * half, slope


def sigmoid(v):
    return 0.5 + 0.5 * jnp.tanh(0.5 * v)


def fold8(v):
    total = v[0:8]
    for i in range(1, v.shape[0] // 8):
        total = total + v[8 * i : 8 * i + 8]
    return total


def norm(v):
    centred = v - jnp.mean(v, axis=-1, keepdims=True)
    rstd = lax.rsqrt(jnp.mean(centred * centred, axis=-1, keepdims=True) + EPS)
    return centred, rstd


def norm_back(g, low, gain, inverse, rstd):
    gy = g * gain
    m1 = jnp.mean(gy, axis=-1, keepdims=True)
    m2 = jnp.mean(g * low, axis=-1, keepdims=True)
    return rstd * (gy - m1 - (low * inverse) * m2)


def at(s, first, size):
    return pl.ds(pl.multiple_of(s * SEQ + first, size), size)


def row_of(first, size):
    return first + lax.broadcasted_iota(jnp.int32, (size, 1), 0)


KEPT = (
    "a", "b", "e", "f", "rstd", "sig", "u", "dgl", "dgr", "m",
    "depth", "qkvt", "pt", "mixt", "up", "gup", "ga", "gmixt", "gain_f",
)


def kept_shapes(sents):
    rows = sents * SEQ
    shape = jax.ShapeDtypeStruct
    return {
        "a": shape((rows, D), bf),
        "b": shape((rows, D), bf),
        "e": shape((rows, D), bf),
        "f": shape((rows, D), bf),
        "rstd": shape((rows, 8), f32),
        "sig": shape((rows, D), bf),
        "u": shape((rows, D), bf),
        "dgl": shape((rows, FF), bf),
        "dgr": shape((rows, HALF), bf),
        "m": shape((sents, 16, PAD, 128), f32),
        "depth": shape((8, sents, SEQ, 256), bf),
        "qkvt": shape((3 * D, rows), bf),
        "pt": shape((sents, HEADS, SEQ, SEQ), bf),
        "mixt": shape((D, rows), bf),
        "up": shape((rows, FF), bf),
        "gup": shape((rows, FF), bf),
        "ga": shape((rows, D), f32),
        "gmixt": shape((D, rows), bf),
        "gain_f": shape((sents * 8, D), f32),
    }


def part_of(name, s):
    if name in ("m", "pt"):
        return (s,)
    if name == "depth":
        return (slice(None), s)
    if name in ("qkvt", "mixt", "gmixt"):
        return (slice(None), pl.ds(pl.multiple_of(s * SEQ, SEQ), SEQ))
    if name == "gain_f":
        return (pl.ds(pl.multiple_of(s * 8, 8), 8),)
    return (pl.ds(pl.multiple_of(s * SEQ, SEQ), SEQ),)


def front_kernel(
    sents,
    len_ref,
    x_ref,
    cot_ref,
    gains_ref,
    wg_ref,
    wglu,
    wleft,
    wconv,
    wdepth,
    wpoint,
    wqkv,
    wout,
    wup,
    wdown,
    out_ref,
    *refs,
):
    far, refs = dict(zip(KEPT, refs)), refs[len(KEPT) :]
    near, refs = dict(zip(KEPT, refs)), refs[len(KEPT) :]
    ship_sems, wp_ref, xf_ref, bs_ref, wide_ref, sep_ref, qkv_ref = refs
    (a_ref, b_ref, e_ref, f_ref, rstd_ref, sig_ref, u_ref, dgl_ref, dgr_ref, m_ref) = [near[n] for n in KEPT[:10]]
    (depth_ref, qkvt_ref, pt_ref, mixt_ref, up_ref, gup_ref, ga_ref, gmixt_ref, gain_f_ref) = [near[n] for n in KEPT[10:]]

    def shipment(name, s):
        k = KEPT.index(name)
        where = part_of(name, s)
        return pltpu.make_async_copy(near[name].at[where], far[name].at[where], ship_sems.at[k, s])

    def ship(s, *names):
        for name in names:
            shipment(name, s).start()

    wp_ref[0:9, :] = wdepth[...].astype(f32) * wg_ref[...].astype(f32)
    gain_f_ref[...] = jnp.zeros_like(gain_f_ref)
    zero8 = jnp.zeros((8, 128), f32)

    def sentence(s, carry):
        mark = Marks()
        length = len_ref[s]
        gains = gains_ref[...].astype(f32)
        rows = at(s, 0, SEQ)
        mark("fw_glu")
        for c in range(0, SEQ, CH):
            cen, rstd = norm(x_ref[at(s, c, CH), :].astype(f32))
            a_ref[at(s, c, CH), :] = (cen * rstd * gains[0:1]).astype(bf)
            rstd_ref[at(s, c, CH), 0:1] = rstd
        a_low = a_ref[rows, :]
        for n in range(2):
            cols = slice(256 * n, 256 * n + 256)
            gcols = slice(512 + 256 * n, 768 + 256 * n)
            value = nn(a_low, wglu[:, cols])
            gate = nn(a_low, wglu[:, gcols])
            for c in range(0, SEQ, CH):
                sig = sigmoid(gate[c : c + CH])
                mixed = value[c : c + CH] * sig
                xf_ref[c : c + CH, cols] = x_ref[at(s, c, CH), cols].astype(f32) + mixed
                sig_ref[at(s, c, CH), cols] = sig.astype(bf)
                u_ref[at(s, c, CH), cols] = (mixed * (1.0 - sig)).astype(bf)
        ship(s, "a", "sig", "u")
        mark("fw_norm_b")
        for c in range(0, SEQ, CH):
            cen, rstd = norm(xf_ref[c : c + CH, :])
            rstd = jnp.where(row_of(c, CH) < length, rstd, 0.0)
            b_low = cen * rstd * gains[1:2]
            b_ref[at(s, c, CH), :] = b_low.astype(bf)
            rstd_ref[at(s, c, CH), 1:2] = rstd
            bs_ref[8 + c : 8 + c + CH, :] = b_low
        mark("fw_left")
        b_low = b_ref[rows, :]
        bs_ref[0:8, :] = jnp.zeros((8, D), f32)
        bs_ref[8 + SEQ : 16 + SEQ, :] = jnp.zeros((8, D), f32)
        right = (
            nn(bs_ref[7 : 7 + SEQ, :].astype(bf), wconv[0])
            + nn(b_low, wconv[1])
            + nn(bs_ref[9 : 9 + SEQ, :].astype(bf), wconv[2])
        )
        for n in range(8):
            cols = slice(256 * n, 256 * n + 256)
            left = nn(b_low, wleft[:, cols])
            for c in range(0, SEQ, CH):
                hidden, slope = gelu_both(left[c : c + CH])
                dgl_ref[at(s, c, CH), cols] = slope.astype(bf)
                if n == 0:
                    extra, slope = gelu_both(right[c : c + CH])
                    dgr_ref[at(s, c, CH), :] = slope.astype(bf)
                    hidden = hidden + extra
                wide_ref[c : c + CH, cols] = hidden
        ship(s, "b", "dgl", "dgr")
        mark("fw_wide_norm")
        for j in range(16):
            m_ref[s, j, 0:8, :] = zero8
            m_ref[s, j, 8 + SEQ : PAD, :] = zero8
        for c in range(0, SEQ, 8):
            mean = jnp.mean(wide_ref[c : c + 8, :], axis=-1, keepdims=True)
            cen = wide_ref[c : c + 8, :] - mean
            rstd = lax.rsqrt(jnp.mean(cen * cen, axis=-1, keepdims=True) + EPS)
            rstd = jnp.where(row_of(c, 8) < length, rstd, 0.0)
            rstd_ref[at(s, c, 8), 2:3] = rstd
            for j in range(16):
                m_ref[s, j, 8 + c : 16 + c, :] = cen[:, 128 * j : 128 * j + 128] * rstd
        mark("fw_depth")
        for j in range(16):
            cols = slice(128 * j, 128 * j + 128)
            taps = [wp_ref[o : o + 1, cols] for o in range(9)]
            for c in range(0, SEQ, CH):
                total = m_ref[s, j, c + 4 : c + 4 + CH, :] * taps[0]
                for o in range(1, 9):
                    total = total + m_ref[s, j, c + 4 + o : c + 4 + o + CH, :] * taps[o]
                depth_ref[j // 2, s, c : c + CH, 128 * (j % 2) : 128 * (j % 2) + 128] = total.astype(bf)
        ship(s, "m", "depth")
        mark("fw_point")
        depth = jnp.concatenate([depth_ref[n, s] for n in range(8)], axis=1)
        sep_ref[...] = nn(depth, wpoint[...])
        mark("fw_qkv")
        for c in range(0, SEQ, CH):
            conv = xf_ref[c : c + CH, :]
            conv = jnp.concatenate([conv[:, :HALF] + sep_ref[c : c + CH, :], conv[:, HALF:]], axis=1)
            xf_ref[c : c + CH, :] = conv
            cen, rstd = norm(conv)
            e_ref[at(s, c, CH), :] = (cen * rstd * gains[2:3]).astype(bf)
            rstd_ref[at(s, c, CH), 3:4] = rstd
        e_low = e_ref[rows, :]
        for n in range(6):
            cols = slice(256 * n, 256 * n + 256)
            part = nn(e_low, wqkv[:, cols]).astype(bf)
            qkv_ref[:, cols] = part
            qkvt_ref[cols, at(s, 0, SEQ)] = part.T
        ship(s, "e", "qkvt")
        mark("fw_attend")
        bias = jnp.where(row_of(0, SEQ) < jnp.maximum(length, 1), 0.0, -1e30)
        for h in range(HEADS):
            base = 3 * DH * h
            key = qkv_ref[:, base + DH : base + 2 * DH] * jnp.asarray(DH**-0.5, bf)
            query_t = qkvt_ref[base : base + DH, at(s, 0, SEQ)]
            value_t = qkvt_ref[base + 2 * DH : base + 3 * DH, at(s, 0, SEQ)]
            for q in range(0, SEQ, 128):
                scores = nn(key, query_t[:, q : q + 128]) + bias
                scores = jnp.exp(scores - jnp.max(scores, axis=0, keepdims=True))
                scores = scores * (1.0 / jnp.sum(scores, axis=0, keepdims=True))
                pt_ref[s, h, :, q : q + 128] = scores.astype(bf)
            mixt_ref[DH * h : DH * h + DH, at(s, 0, SEQ)] = nn(value_t, pt_ref[s, h]).astype(bf)
        ship(s, "pt", "mixt")
        mark("fw_out")
        for n in range(2):
            cols = slice(256 * n, 256 * n + 256)
            xf_ref[:, cols] += tn(mixt_ref[:, at(s, 0, SEQ)], wout[:, cols])
        mark("fw_up")
        for c in range(0, SEQ, CH):
            cen, rstd = norm(xf_ref[c : c + CH, :])
            f_ref[at(s, c, CH), :] = (cen * rstd * gains[3:4]).astype(bf)
            rstd_ref[at(s, c, CH), 4:5] = rstd
        f_low = f_ref[rows, :]
        for n in range(8):
            cols = slice(256 * n, 256 * n + 256)
            up = nn(f_low, wup[:, cols])
            for c in range(0, SEQ, CH):
                low, slope = gelu_both(up[c : c + CH])
                up_ref[at(s, c, CH), cols] = low.astype(bf)
                gup_ref[at(s, c, CH), cols] = slope.astype(bf)
        mark("fw_down")
        for n in range(2):
            cols = slice(256 * n, 256 * n + 256)
            down = nn(up_ref[rows, :], wdown[:, cols])
            out_ref[rows, cols] = (xf_ref[:, cols] + down).astype(bf)
        ship(s, "f", "rstd", "up")
        mark("bw_down")
        for c in range(0, SEQ, CH):
            live = row_of(c, CH) < length
            ga_ref[at(s, c, CH), :] = jnp.where(live, cot_ref[at(s, c, CH), :].astype(f32), 0.0)
        g_low = ga_ref[rows, :].astype(bf)
        for n in range(8):
            cols = slice(256 * n, 256 * n + 256)
            back = nt(g_low, wdown[cols, :])
            gup_ref[rows, cols] = (back * gup_ref[rows, cols].astype(f32)).astype(bf)
        mark("bw_up")
        ship(s, "gup")
        for n in range(2):
            cols = slice(256 * n, 256 * n + 256)
            wide_ref[:, cols] = nt(gup_ref[rows, :], wup[cols, :])
        inverse = 1.0 / gains[3:4]
        for c in range(0, SEQ, CH):
            g_f = wide_ref[c : c + CH, 0:D]
            low = f_ref[at(s, c, CH), :].astype(f32)
            gain_f_ref[pl.ds(pl.multiple_of(s * 8, 8), 8), :] += fold8(g_f * low)
            back = norm_back(g_f, low, gains[3:4], inverse, rstd_ref[at(s, c, CH), 4:5])
            ga_ref[at(s, c, CH), :] += back
        gmixt_ref[:, at(s, 0, SEQ)] = nt(wout[...], ga_ref[rows, :].astype(bf)).astype(bf)
        ship(s, "ga", "gmixt", "gain_f")
        mark()
        return carry

    lax.fori_loop(0, sents, sentence, 0)

    def landed(s, carry):
        for name in KEPT:
            shipment(name, s).wait()
        return carry

    lax.fori_loop(0, sents, landed, 0)


class Marks:
    def __init__(self):
        self.open = None

    def __call__(self, name=None):
        if self.open is not None:
            self.open.__exit__(None, None, None)
        self.open = None
        if name is not None:
            self.open = jax.named_scope(name)
            self.open.__enter__()


def vmem():
    return pl.BlockSpec(memory_space=pltpu.VMEM)


def smem():
    return pl.BlockSpec(memory_space=pltpu.SMEM)


def offsets(share, wide_share):
    sizes = (
        ("up", 8 * share, True),
        ("down", 2 * wide_share, True),
        ("out", 2 * share, False),
        ("qkv", 6 * share, True),
        ("point", wide_share, True),
        ("left", 2 * share, True),
        ("left1", 2 * share, True),
        ("left2", 2 * share, True),
        ("left3", 2 * share, True),
        ("conv", 3 * share, True),
        ("glu", 2 * share, True),
        ("glu1", 2 * share, True),
    )
    first, starts, groups, begin = 0, {}, [], 0
    for name, size, ends in sizes:
        starts[name] = first
        first += size
        if ends:
            first = -(-first // 32) * 32
            groups.append((begin, first - begin))
            begin = first
    return starts, groups, first


def put(g_ref, grid, tile, first, share, wide, chunk=0):
    _, ys = grid
    for part in range(tile.shape[1] // 256):
        for k in range(512 // share):
            block = chunk * (512 // share) + k
            piece = tile[k * share : (k + 1) * share, 256 * part : 256 * part + 256]
            rows = pl.ds(pl.multiple_of(first + part * share, 16), share)
            g_ref[block // ys, block % ys, rows, :] = piece.astype(bf)


def back_kernel(
    sents,
    grid,
    xs,
    names,
    len_ref,
    pair_ref,
    cot_far,
    gains_ref,
    wg_ref,
    wglu,
    wleft,
    wconv,
    wdepth,
    wpoint,
    wqkv,
    *refs,
):
    far, refs = dict(zip(KEPT, refs)), refs[len(KEPT) :]
    xgrad_far, final_far, early_far, late_far = refs[:4]
    recv, refs = dict(zip(names, refs[4:])), refs[4 + len(names) :]
    (
        fetch_sems,
        send_sems,
        recv_sems,
        g_ref,
        final_ref,
        count_ref,
        count_got,
        early_ref,
        early_got,
        late_ref,
        late_got,
        fac_ref,
        first_wide,
        second_wide,
        gqkv_ref,
        squares,
        conv_ref,
        gl_ref,
        fs_ref,
        gas_ref,
        mixt_ref,
        gmixt_ref,
        qkvt_ref,
        dgr_ref,
        rstd_ref,
        gain_f_ref,
        m_ref,
        wp_ref,
        gqkvt_ref,
        gd_ref,
        wide_ref,
        taps_ref,
        s1_ref,
        s2_ref,
        right_ref,
        gain_ref,
    ) = refs
    e_ref = gas_ref
    gr_refs = (gl_ref.at[:, 0:HALF], gl_ref.at[:, HALF:D], fs_ref.at[:, 0:HALF])
    sep_ref = fs_ref.at[:, HALF:D]
    up_ref = gleft_ref = dgl_ref = first_wide
    gup_ref = second_wide
    a_ref, b_ref, sig_ref, u_ref = [second_wide.at[:, D * k : D * k + D] for k in range(4)]
    gg_ref = gqkv_ref
    pt_ref, depth_view = squares, squares.reshape(8, sents, SEQ, 256)
    where = dict(
        a=a_ref, b=b_ref, e=e_ref, f=fs_ref, rstd=rstd_ref, sig=sig_ref, u=u_ref, dgl=first_wide, dgr=dgr_ref,
        qkvt=qkvt_ref, mixt=mixt_ref, up=first_wide, gup=second_wide, ga=conv_ref, gmixt=gmixt_ref, gain_f=gain_f_ref,
        pt=squares, depth=depth_view, cot=gl_ref,
    )
    far["cot"] = cot_far
    order = (
        "gmixt", "qkvt", "pt", "f", "gup", "ga", "cot", "up", "gain_f", "mixt", "rstd", "dgr",
        "e", "b", "a", "sig", "u", "dgl", "depth",
    )

    def fetch(name):
        return pltpu.make_async_copy(far[name], where[name], fetch_sems.at[order.index(name)])

    def start(*names):
        for name in names:
            fetch(name).start()

    def wait(*names):
        for name in names:
            fetch(name).wait()

    def fetch_m(s):
        return pltpu.make_async_copy(far["m"].at[s], m_ref.at[s % 2], fetch_sems.at[len(order) + s % 2])

    start(*order[:12])
    fetch_m(0).start()
    if sents > 1:
        fetch_m(1).start()
    share, wide_share = 512 // (grid[0] * grid[1]), 2048 // (grid[0] * grid[1])
    starts, groups, _ = offsets(share, wide_share)
    sums = Sums(grid, xs, groups, g_ref, final_ref, recv, send_sems, recv_sems)
    with jax.named_scope("greet"):
        sums.greet()
    lane = lax.broadcasted_iota(jnp.int32, (8, 128), 1)
    counts = jnp.zeros((8, 128), f32)
    for s in range(sents):
        counts = counts + jnp.where(lane == pair_ref[s], len_ref[s].astype(f32), 0.0)
    count_ref[3] = counts
    sums.small_send(0, 3, count_ref, count_got)

    def count_next(axis):
        sums.small_next(0, axis, count_ref, count_got)
        if axis == 0:
            counts = count_ref[4]
            total = jnp.sum(counts, axis=1, keepdims=True)
            for s in range(sents):
                mine = jnp.sum(jnp.where(lane == pair_ref[s], counts, 0.0), axis=1, keepdims=True)
                fac_ref[s] = jnp.broadcast_to(total / (PAIRS * mine), (8, 128))

    def factor_of(s):
        return fac_ref[s, 0:1, 0:1]

    def between(s, events):
        for k, steps in enumerate(events):
            pl.when(s == min(k, sents - 1))(functools.partial(sums.do, steps))

    wp_ref[0:9, :] = wdepth[...].astype(f32) * wg_ref[...].astype(f32)
    gain_ref[...] = jnp.zeros_like(gain_ref)
    taps_ref[...] = jnp.zeros_like(taps_ref)

    with jax.named_scope("await_attend"):
        wait("gmixt", "qkvt", "pt")

    def attend(first, s, carry):
        rows = at(s, 0, SEQ)
        for h in range(HEADS):
            base = 3 * DH * h
            g_o = gmixt_ref[DH * h : DH * h + DH, rows]
            query_t = qkvt_ref[base : base + DH, rows]
            key_t = qkvt_ref[base + DH : base + 2 * DH, rows]
            value = qkvt_ref[base + 2 * DH : base + 3 * DH, rows].T
            probs = pt_ref[s, h]
            halves = []
            for q in range(0, SEQ, 128):
                part = probs[:, q : q + 128].astype(f32)
                back = nn(value, g_o[:, q : q + 128])
                both = part * back
                halves.append((both - part * jnp.sum(both, axis=0, keepdims=True)).astype(bf))
            g_scores = jnp.concatenate(halves, axis=1)
            gqkvt_ref[base : base + DH, :] = (nn(key_t, g_scores) * DH**-0.5).astype(bf)
            gqkvt_ref[base + DH : base + 2 * DH, :] = (nt(query_t, g_scores) * DH**-0.5).astype(bf)
            gqkvt_ref[base + 2 * DH : base + 3 * DH, :] = nt(g_o, probs).astype(bf)
            if first and h % 2:
                count_next(3 - h // 2)
        factor = factor_of(s).astype(bf)
        for n in range(6):
            cols = slice(256 * n, 256 * n + 256)
            gqkv_ref[rows, cols] = gqkvt_ref[cols, :].T * factor
        if not first:
            between(s - 1, after_attend)
        return carry

    with jax.named_scope("attend_first"):
        lax.fori_loop(0, 1, functools.partial(attend, True), 0)

    with jax.named_scope("await_feed"):
        wait("f", "gup", "ga", "cot", "up", "gain_f", "mixt", "rstd")

    def scale(s, carry):
        factor = factor_of(s)
        length = len_ref[s]
        for c in range(0, SEQ, CH):
            rows = at(s, c, CH)
            weight = jnp.where(row_of(c, CH) < length, factor, 0.0)
            gl_ref[rows, :] = (gl_ref[rows, :].astype(f32) * weight).astype(bf)
            fs_ref[rows, :] = (fs_ref[rows, :].astype(f32) * factor).astype(bf)
            conv_ref[rows, :] = conv_ref[rows, :] * factor
            gas_ref[rows, :] = conv_ref[rows, :].astype(bf)
        gain_ref[24:32, :] += gain_f_ref[pl.ds(pl.multiple_of(s * 8, 8), 8), :] * factor
        return carry

    with jax.named_scope("scale"):
        lax.fori_loop(0, sents, scale, 0)

    def wide_tile(i):
        return pl.ds(pl.multiple_of(i * 512, 512), 512)

    def grad_up(i, carry):
        put(g_ref, grid, tn(fs_ref[...], gup_ref[:, wide_tile(i)]), starts["up"] + i * 2 * share, share, False)
        return carry

    with jax.named_scope("grad_up"):
        lax.fori_loop(0, 4, grad_up, 0)
    start("b", "a", "sig", "u")
    sums.advance(0)

    def grad_down(i, carry):
        put(g_ref, grid, tn(up_ref[:, wide_tile(i)], gl_ref[...]), starts["down"], wide_share, True, i)
        return carry

    with jax.named_scope("grad_down"):
        lax.fori_loop(0, 4, grad_down, 0)
    start("dgl")
    sums.advance(1, 0)
    with jax.named_scope("grad_out"):
        put(g_ref, grid, nn(mixt_ref[...], gas_ref[...]), starts["out"], share, False)
    start("e")
    sums.advance(1)
    after_attend = (sums.claim(0), sums.claim(1))
    with jax.named_scope("attend_rest"):
        lax.fori_loop(1, sents, functools.partial(attend, False), 0)
    start("depth")
    wait("e")

    def grad_qkv(i, carry):
        put(g_ref, grid, tn(e_ref[...], gqkv_ref[:, wide_tile(i)]), starts["qkv"] + i * 2 * share, share, False)
        return carry

    with jax.named_scope("grad_qkv"):
        lax.fori_loop(0, 3, grad_qkv, 0)
    sums.advance(2, 0)

    def attention_input(s, carry):
        gains = gains_ref[...].astype(f32)
        inverse = 1.0 / gains[2:3]
        rows = at(s, 0, SEQ)
        for n in range(2):
            cols = slice(256 * n, 256 * n + 256)
            wide_ref[:, cols] = nt(gqkv_ref[rows, :], wqkv[cols, :])
        for c in range(0, SEQ, CH):
            part = at(s, c, CH)
            g_e = wide_ref[c : c + CH, 0:D]
            low = e_ref[part, :].astype(f32)
            gain_ref[16:24, :] += fold8(g_e * low)
            g_conv = conv_ref[part, :] + norm_back(g_e, low, gains[2:3], inverse, rstd_ref[part, 3:4])
            conv_ref[part, :] = g_conv
            sep_ref[part, :] = g_conv[:, :HALF].astype(bf)
        return carry

    with jax.named_scope("attention_input"):
        lax.fori_loop(0, sents, attention_input, 0)

    sums.advance(2, 1)
    wait("depth")

    def grad_point(i, carry):
        depth = [depth_view[2 * i + k].reshape(sents * SEQ, 256) for k in range(2)]
        put(g_ref, grid, tn(jnp.concatenate(depth, axis=1), sep_ref[...]), starts["point"], wide_share, True, i)
        return carry

    with jax.named_scope("grad_point"):
        lax.fori_loop(0, 4, grad_point, 0)
    sums.advance(3, 0)

    wait("b", "a", "sig", "u", "dgr", "dgl")
    after_wide = (sums.claim(3, 1, 2, 0), sums.claim(3, 2, 1), sums.claim(3, 2))

    zero8 = jnp.zeros((8, 128), f32)

    def wide(s, carry):
        rows = at(s, 0, SEQ)
        mark = Marks()
        mark("g_depth")
        slot = s % 2
        fetch_m(s).wait()
        for n in range(8):
            back = nt(sep_ref[rows, :], wpoint[256 * n : 256 * n + 256, :])
            for k in range(2):
                gd_ref[2 * n + k, 8 : 8 + SEQ, :] = back[:, 128 * k : 128 * k + 128]
        mark("taps")
        for j in range(16):
            gd_ref[j, 0:8, :] = zero8
            gd_ref[j, 8 + SEQ : PAD, :] = zero8
            cols = slice(128 * j, 128 * j + 128)
            taps = [wp_ref[o : o + 1, cols] for o in range(9)]
            for c in range(0, SEQ, CH):
                total = gd_ref[j, c + 12 : c + 12 + CH, :] * taps[0]
                for o in range(1, 9):
                    total = total + gd_ref[j, c + 12 - o : c + 12 - o + CH, :] * taps[o]
                wide_ref[c : c + CH, cols] = total
                mine = m_ref[slot, j, c + 8 : c + 8 + CH, :]
                if j == 0:
                    s1_ref[c : c + CH, :] = total
                    s2_ref[c : c + CH, :] = total * mine
                else:
                    s1_ref[c : c + CH, :] += total
                    s2_ref[c : c + CH, :] += total * mine
            for o in range(9):
                sums = taps_ref[o, :, cols]
                for c in range(0, SEQ, CH):
                    sums = sums + fold8(m_ref[slot, j, c + 4 + o : c + 4 + o + CH, :] * gd_ref[j, c + 8 : c + 8 + CH, :])
                taps_ref[o, :, cols] = sums
        mark("g_hidden")
        right_ref[0:8, :] = jnp.zeros((8, HALF), f32)
        right_ref[8 + SEQ : PAD, :] = jnp.zeros((8, HALF), f32)
        for c in range(0, SEQ, CH):
            part = at(s, c, CH)
            rstd = rstd_ref[part, 2:3]
            m1 = jnp.sum(s1_ref[c : c + CH, :], axis=-1, keepdims=True) * (rstd / FF)
            m2 = jnp.sum(s2_ref[c : c + CH, :], axis=-1, keepdims=True) * (rstd / FF)
            for j in range(16):
                cols = slice(128 * j, 128 * j + 128)
                g_h = wide_ref[c : c + CH, cols] * rstd - m1 - m_ref[slot, j, c + 8 : c + 8 + CH, :] * m2
                gleft_ref[part, cols] = (g_h * dgl_ref[part, cols].astype(f32)).astype(bf)
                if j < 2:
                    right_ref[8 + c : 8 + c + CH, cols] = g_h * dgr_ref[part, cols].astype(f32)
        mark()

        @pl.when(s + 2 < sents)
        def _():
            fetch_m(s + 2).start()

        for k in range(3):
            gr_refs[k][rows, :] = right_ref[9 - k : 9 - k + SEQ, :].astype(bf)
        between(s, after_wide)
        return carry

    with jax.named_scope("wide"):
        lax.fori_loop(0, sents, wide, 0)

    for i, waiting in enumerate(((2,), (4, 3), (5,), (6, 3))):
        with jax.named_scope("grad_left"):
            put(g_ref, grid, tn(b_ref[...], gleft_ref[:, 512 * i : 512 * i + 512]), starts[("left", "left1", "left2", "left3")[i]], share, False)
        sums.advance(4 + i, *waiting)
    for k in range(3):
        with jax.named_scope("grad_conv"):
            put(g_ref, grid, tn(b_ref[...], gr_refs[k][...]), starts["conv"] + k * share, share, False)
    sums.advance(8, 7)

    wide_gain = wg_ref[...].astype(f32)
    total = jnp.zeros((1, FF), f32)
    for o in range(9):
        lines = jnp.sum(taps_ref[o], axis=0, keepdims=True)
        total = total + lines * wdepth[o : o + 1, :].astype(f32)
        for k in range(8):
            early_ref[3, 8 * o + k : 8 * o + k + 1, :] = (lines * wide_gain)[:, 256 * k : 256 * k + 256]
    for k in range(8):
        early_ref[3, 72 + k : 73 + k, :] = total[:, 256 * k : 256 * k + 256]

    def gain_rows(ref, first, i):
        lines = jnp.sum(gain_ref[8 * i : 8 * i + 8, :], axis=0, keepdims=True) / gains_ref[i : i + 1, :].astype(f32)
        for k in range(2):
            ref[3, first + k : first + k + 1, :] = lines[:, 256 * k : 256 * k + 256]

    early_ref[3, 80:88, :] = jnp.zeros((8, 256), f32)
    gain_rows(early_ref, 80, 2)
    gain_rows(early_ref, 82, 3)
    sums.small_send(1, 3, early_ref, early_got)

    def inputs(s, carry):
        gains = gains_ref[...].astype(f32)
        rows = at(s, 0, SEQ)
        mark = Marks()
        mark("g_b")
        for n in range(2):
            cols = slice(256 * n, 256 * n + 256)
            g_b = nt(gleft_ref[rows, :], wleft[cols, :])
            for k in range(3):
                g_b = g_b + nt(gr_refs[k][rows, :], wconv[k, cols, :])
            wide_ref[:, cols] = g_b
        mark("norm_b")
        inverse = 1.0 / gains[1:2]
        for c in range(0, SEQ, CH):
            part = at(s, c, CH)
            g_b = wide_ref[c : c + CH, 0:D]
            low = b_ref[part, :].astype(f32)
            gain_ref[8:16, :] += fold8(g_b * low)
            g_glu = conv_ref[part, :] + norm_back(g_b, low, gains[1:2], inverse, rstd_ref[part, 1:2])
            conv_ref[part, :] = g_glu
            gg_ref[part, 0:D] = (g_glu * sig_ref[part, :].astype(f32)).astype(bf)
            gg_ref[part, D : 2 * D] = (g_glu * u_ref[part, :].astype(f32)).astype(bf)
        mark("g_a")
        for n in range(2):
            cols = slice(256 * n, 256 * n + 256)
            wide_ref[:, cols] = nt(gg_ref[rows, 0 : 2 * D], wglu[cols, :])
        mark("norm_a")
        inverse = 1.0 / gains[0:1]
        for c in range(0, SEQ, CH):
            part = at(s, c, CH)
            g_a = wide_ref[c : c + CH, 0:D]
            low = a_ref[part, :].astype(f32)
            gain_ref[0:8, :] += fold8(g_a * low)
            conv_ref[part, :] += norm_back(g_a, low, gains[0:1], inverse, rstd_ref[part, 0:1])
        mark()
        between(s, after_inputs)
        return carry

    after_inputs = (sums.claim(8, 4), sums.claim(5, 6), sums.claim(7, 4))
    with jax.named_scope("inputs"):
        lax.fori_loop(0, sents, inputs, 0)
    leave = pltpu.make_async_copy(conv_ref, xgrad_far, fetch_sems.at[len(order) + 2])
    leave.start()
    late_ref[3] = jnp.zeros((8, 256), f32)
    gain_rows(late_ref, 0, 0)
    gain_rows(late_ref, 2, 1)
    sums.small_send(2, 3, late_ref, late_got)
    sums.small_next(1, 3, early_ref, early_got)
    for i, waiting in enumerate(((8, 5), (9, 6))):
        with jax.named_scope("grad_glu"):
            put(g_ref, grid, tn(a_ref[...], gg_ref[:, 512 * i : 512 * i + 512]), starts[("glu", "glu1")[i]], share, False)
        sums.advance(9 + i, *waiting)
    rounds = 0
    while any(stage < sums.STAGES for stage in sums.stage):
        sums.advance(*range(len(groups)))
        if rounds < 3:
            sums.small_next(1, 2 - rounds, early_ref, early_got)
        if rounds < 4:
            sums.small_next(2, 3 - rounds, late_ref, late_got)
        rounds += 1
    ends = (final_ref, final_far), (early_ref.at[4], early_far), (late_ref.at[4], late_far)
    ends = [pltpu.make_async_copy(*pair, fetch_sems.at[len(order) + 3 + k]) for k, pair in enumerate(ends)]
    for copy in ends:
        copy.start()
    with jax.named_scope("finish"):
        sums.finish()
    leave.wait()
    for copy in ends:
        copy.wait()


def coordinates(ys):
    dp, head = lax.axis_index("dp"), lax.axis_index("head")
    return dp // ys, dp % ys, head // 2, head % 2


def device(ys, z, y, x, c):
    return (z * ys + y, x * 2 + c)


def rows16(first, size):
    return pl.ds(pl.multiple_of(first, 16), size)


def split_of(size, xs):
    half = size // 2
    first = (half // (32 * xs)) * 16 * xs
    return half, first, half - first


class Sums:
    STAGES = 6

    def __init__(self, grid, xs, groups, g_ref, final_ref, recv, send_sems, recv_sems):
        self.zs, self.ys = grid
        self.xs = xs
        self.sizes = (*grid, xs, 2)
        self.groups = groups
        self.g, self.final = g_ref, final_ref
        self.recv = recv
        self.send_sems, self.recv_sems = send_sems, recv_sems
        self.place = coordinates(self.ys)
        self.stage = [-1] * len(groups)
        self.small = []

    def peers(self, axis):
        size = self.sizes[axis]
        for step in range(1, size):
            to = list(self.place)
            to[axis] = lax.rem(to[axis] + step, size)
            yield step - 1, to[axis], device(self.ys, *to)

    def greet(self):
        barrier = pltpu.get_barrier_semaphore()
        total = 0
        for axis in range(4):
            for _, _, to in self.peers(axis):
                pl.semaphore_signal(barrier, inc=1, device_id=to, device_id_type=MESH)
                total += 1
        pl.semaphore_wait(barrier, total)

    def core_first(self, i):
        return (self.groups[i][0] - (self.groups[3][0] if i > 2 else 0)) // 2

    def a_first(self, i):
        return sum(split_of(size, self.xs)[1] // self.xs for _, size in self.groups[:i])

    def b_first(self, i):
        return sum(split_of(size, self.xs)[2] for _, size in self.groups[:i])

    def rows(self, i):
        first, size = self.groups[i]
        half, na, nb = split_of(size, self.xs)
        mine = first + self.place[3] * half
        return first, half, mine, na, na // self.xs, mine + na, nb

    def plan(self, stage, i):
        z, y, x, c = self.place
        first, half, mine, na, part, b_row, nb = self.rows(i)
        g, recv, final = self.g, self.recv, self.final
        a_in, b_in = pl.ds(self.a_first(i), part), pl.ds(self.b_first(i), nb)
        a_rows, b_rows = rows16(mine + x * part, part), rows16(b_row, nb)
        axis_a, axis_b = ((None, 3), (2, 1), (1, 0), (0, 2), (2, 3), (3, None))[stage]
        copies_a, copies_b = [], []
        for slot, other, to in self.peers(axis_b) if axis_b is not None else ():
            if stage == 0:
                source = g.at[:, :, rows16(first + other * half, half), :]
                target = recv["core"].at[:, :, pl.ds(self.core_first(i), half), :]
            elif stage == 1:
                source, target = g.at[:, other, b_rows, :], recv["b1"].at[slot, :, b_in, :]
            elif stage == 2:
                source, target = g.at[other, y, b_rows, :], recv["b2"].at[slot, b_in, :]
            elif stage == 3:
                source, target = g.at[z, y, b_rows, :], recv["b3"].at[slot, b_in, :]
            else:
                source, target = final.at[b_rows, :], final.at[b_rows, :]
            copies_b.append((source, target, to))
        for slot, other, to in self.peers(axis_a) if axis_a is not None and na else ():
            if stage == 1:
                source, target = g.at[:, :, rows16(mine + other * part, part), :], recv["a1"].at[slot, :, :, a_in, :]
            elif stage == 2:
                source, target = g.at[:, other, a_rows, :], recv["a2"].at[slot, :, a_in, :]
            elif stage == 3:
                source, target = g.at[other, y, a_rows, :], recv["a3"].at[slot, a_in, :]
            else:
                rows = a_rows if stage == 4 else rows16(mine, na)
                source, target = final.at[rows, :], final.at[rows, :]
            copies_a.append((source, target, to))
        return copies_b, copies_a

    def copies(self, stage, i):
        counts = self.counts(self.sizes)
        first = i * sum(map(sum, counts)) + sum(map(sum, counts[:stage]))
        copies_b, copies_a = self.plan(stage, i)
        made = []
        for copies, extra in ((copies_b, 0), (copies_a, counts[stage][0])):
            for n, (source, target, to) in enumerate(copies):
                index = first + extra + n
                made.append(
                    pltpu.make_async_remote_copy(
                        src_ref=source,
                        dst_ref=target,
                        send_sem=self.send_sems.at[index],
                        recv_sem=self.recv_sems.at[index],
                        device_id=to,
                        device_id_type=MESH,
                    )
                )
        return made

    @staticmethod
    def counts(sizes):
        z, y, x, _ = (size - 1 for size in sizes)
        return ((1, 0), (y, x), (z, y), (x, z), (1, x), (0, 1))

    @staticmethod
    def semaphores(grid, xs, groups):
        sizes = (*grid, xs, 2)
        return len(groups) * sum(map(sum, Sums.counts(sizes))) + 12 * (max(sizes) - 1)

    def claim(self, *groups):
        steps = []
        for i in groups:
            if self.stage[i] < self.STAGES:
                steps.append((i, self.stage[i]))
                self.stage[i] += 1
        return steps

    def do(self, steps):
        for i, stage in steps:
            if stage >= 0:
                with jax.named_scope(f"await_{i}_{stage}"):
                    for copy in self.copies(stage, i):
                        copy.wait_recv()
                with jax.named_scope(f"add_{i}_{stage}"):
                    self.add(stage, i)
            if stage + 1 < self.STAGES:
                for copy in self.copies(stage + 1, i):
                    copy.start()

    def advance(self, *groups):
        self.do(self.claim(*groups))

    def over(self, i):
        return self.stage[i] == self.STAGES

    def add(self, stage, i):
        z, y, x, c = self.place
        first, half, mine, na, part, b_row, nb = self.rows(i)
        g, recv = self.g, self.recv
        a_in, b_in = pl.ds(self.a_first(i), part), pl.ds(self.b_first(i), nb)
        a_rows, b_rows = rows16(mine + x * part, part), rows16(b_row, nb)

        def total(mine, got):
            value = mine.astype(f32)
            for other in got:
                value = value + other.astype(f32)
            return value.astype(bf)

        if stage == 0:

            def core(block, carry):
                zb, yb = block // self.ys, block % self.ys
                g[zb, yb, rows16(mine, half), :] += recv["core"][zb, yb, pl.ds(self.core_first(i), half), :]
                return carry

            lax.fori_loop(0, self.zs * self.ys, core, 0)
        elif stage == 1:

            def one(zb, carry):
                got = [recv["b1"][slot, zb, b_in, :] for slot in range(self.ys - 1)]
                g[zb, y, b_rows, :] = total(g[zb, y, b_rows, :], got)
                for yb in range(self.ys) if na else ():
                    got = [recv["a1"][slot, zb, yb, a_in, :] for slot in range(self.xs - 1)]
                    g[zb, yb, a_rows, :] = total(g[zb, yb, a_rows, :], got)
                return carry

            lax.fori_loop(0, self.zs, one, 0)
        elif stage == 2:
            g[z, y, b_rows, :] = total(g[z, y, b_rows, :], [recv["b2"][slot, b_in, :] for slot in range(self.zs - 1)])
            if na:

                def two(zb, carry):
                    got = [recv["a2"][slot, zb, a_in, :] for slot in range(self.ys - 1)]
                    g[zb, y, a_rows, :] = total(g[zb, y, a_rows, :], got)
                    return carry

                lax.fori_loop(0, self.zs, two, 0)
        elif stage == 3:
            got = [recv["b3"][slot, b_in, :] for slot in range(self.xs - 1)]
            self.final[b_rows, :] = total(g[z, y, b_rows, :], got)
            if na:
                got = [recv["a3"][slot, a_in, :] for slot in range(self.zs - 1)]
                self.final[a_rows, :] = total(g[z, y, a_rows, :], got)

    def small_copies(self, k, axis, held, got):
        most = max(self.sizes) - 1
        base = len(self.groups) * sum(map(sum, self.counts(self.sizes)))
        made = []
        for slot, other, to in self.peers(axis):
            index = base + (k * 4 + axis) * most + slot
            made.append(
                pltpu.make_async_remote_copy(
                    src_ref=held.at[axis],
                    dst_ref=got.at[self.got_first(axis) + slot],
                    send_sem=self.send_sems.at[index],
                    recv_sem=self.recv_sems.at[index],
                    device_id=to,
                    device_id_type=MESH,
                )
            )
        return made

    def got_first(self, axis):
        return sum(size - 1 for size in self.sizes[:axis])

    def small_send(self, k, axis, held, got):
        self.small.append((k, axis, held, got))
        for copy in self.small_copies(k, axis, held, got):
            copy.start()

    def small_add(self, k, axis, held, got):
        for copy in self.small_copies(k, axis, held, got):
            copy.wait_recv()
        size, me = self.sizes[axis], self.place[axis]
        total = None
        for n in range(size):
            value = held[axis]
            for slot in range(size - 1):
                value = jnp.where(lax.rem(me - slot - 1 + size, size) == n, got[self.got_first(axis) + slot], value)
            total = value if total is None else total + value
        held[axis - 1 if axis else 4] = total

    def small_next(self, k, axis, held, got):
        self.small_add(k, axis, held, got)
        if axis:
            self.small_send(k, axis - 1, held, got)

    def finish(self):
        for i in range(len(self.groups)):
            for stage in range(self.STAGES):
                for copy in self.copies(stage, i):
                    copy.wait_send()
        for small in self.small:
            for copy in self.small_copies(*small):
                copy.wait_send()


def recv_shapes(grid, xs, groups, height):
    zs, ys = grid
    na = sum(split_of(size, xs)[1] for _, size in groups) // xs
    nb = sum(split_of(size, xs)[2] for _, size in groups)
    na = max(na, 16)
    return {
        "core": (zs, ys, max(groups[3][0], height - groups[3][0]) // 2, 256),
        "a1": (xs - 1, zs, ys, na, 256),
        "b1": (ys - 1, zs, nb, 256),
        "a2": (ys - 1, zs, na, 256),
        "b2": (zs - 1, nb, 256),
        "a3": (zs - 1, na, 256),
        "b3": (xs - 1, nb, 256),
    }


SMALL = 88


def last_kernel(share, wide_share, final_ref, early_ref, late_ref, xgrad_in, *refs):
    xgrad_out, norms, wide_gain, glu, left, conv, depth, point, qkv, out, up, down = refs
    xgrad_out[...] = xgrad_in[...]
    starts, _, _ = offsets(share, wide_share)
    for k in range(8):
        for o in range(9):
            depth[o : o + 1, 256 * k : 256 * k + 256] = early_ref[8 * o + k : 8 * o + k + 1, :]
        wide_gain[0:1, 256 * k : 256 * k + 256] = early_ref[72 + k : 73 + k, :]
    for i in range(4):
        ref, first = ((late_ref, 0), (late_ref, 2), (early_ref, 80), (early_ref, 82))[i]
        for k in range(2):
            norms[i : i + 1, 256 * k : 256 * k + 256] = ref[first + k : first + k + 1, :]
    for name, ref, tiles, size in (
        ("glu", glu, 4, share),
        ("left", left, 8, share),
        ("point", point, 1, wide_share),
        ("qkv", qkv, 6, share),
        ("out", out, 2, share),
        ("up", up, 8, share),
        ("down", down, 2, wide_share),
    ):
        for n in range(tiles):
            part = name + str(n // 2) if name + str(n // 2) in starts else name
            first = starts[part] + (n % 2 if part != name else n) * size
            ref[:, 256 * n : 256 * n + 256] = final_ref[first : first + size, :].astype(f32)
    for k in range(3):
        first = starts["conv"] + k * share
        conv[k] = final_ref[first : first + share, :].astype(f32)


def local(
    grid,
    xs,
    cell_input,
    lengths,
    pair_ids,
    cotangent,
    norm_gains,
    wide_gain,
    w_glu,
    w_left,
    w_conv3,
    w_depth,
    w_point,
    w_qkv,
    w_out,
    w_up,
    w_down,
):
    zs, ys = grid
    dp = zs * ys
    share, wide_share = 512 // dp, 2048 // dp
    rows = cell_input.shape[0]
    sents = lengths.shape[0]
    starts, groups, height = offsets(share, wide_share)
    wg = wide_gain.reshape(1, FF)
    shape = jax.ShapeDtypeStruct
    params = pltpu.CompilerParams(vmem_limit_bytes=62 << 20)
    kept = kept_shapes(sents)
    anywhere = pl.BlockSpec(memory_space=pl.ANY)
    front = pl.pallas_call(
        functools.partial(front_kernel, sents),
        out_shape=[shape((rows, D), bf)] + list(kept.values()),
        in_specs=[smem()] + [vmem()] * 13,
        out_specs=[vmem()] + [anywhere] * len(kept),
        scratch_shapes=[pltpu.VMEM(v.shape, v.dtype) for v in kept.values()]
        + [
            pltpu.SemaphoreType.DMA((len(kept), sents)),
            pltpu.VMEM((16, FF), f32),
            pltpu.VMEM((SEQ, D), f32),
            pltpu.VMEM((PAD, D), f32),
            pltpu.VMEM((SEQ, FF), f32),
            pltpu.VMEM((SEQ, HALF), f32),
            pltpu.VMEM((SEQ, 3 * D), bf),
        ],
        compiler_params=params,
        name="front",
    )(lengths, cell_input, cotangent, norm_gains, wg, w_glu, w_left, w_conv3, w_depth, w_point, w_qkv, w_out, w_up, w_down)
    cell_output, arrays = front[0], front[1:]
    recv = recv_shapes(grid, xs, groups, height)
    most = zs + ys + xs - 2
    semaphores = Sums.semaphores(grid, xs, groups)
    input_grad, final, early, late = pl.pallas_call(
        functools.partial(back_kernel, sents, grid, xs, tuple(recv)),
        out_shape=[shape((rows, D), f32), shape((height, 256), bf), shape((SMALL, 256), f32), shape((8, 256), f32)],
        in_specs=[smem(), smem(), anywhere] + [vmem()] * 8 + [anywhere] * len(kept),
        out_specs=[anywhere] * 4,
        scratch_shapes=[pltpu.VMEM(v, bf) for v in recv.values()]
        + [
            pltpu.SemaphoreType.DMA((28,)),
            pltpu.SemaphoreType.DMA((semaphores,)),
            pltpu.SemaphoreType.DMA((semaphores,)),
            pltpu.VMEM((zs, ys, height, 256), bf),
            pltpu.VMEM((height, 256), bf),
            pltpu.VMEM((5, 8, 128), f32),
            pltpu.VMEM((most, 8, 128), f32),
            pltpu.VMEM((5, SMALL, 256), f32),
            pltpu.VMEM((most, SMALL, 256), f32),
            pltpu.VMEM((5, 8, 256), f32),
            pltpu.VMEM((most, 8, 256), f32),
            pltpu.VMEM((sents, 8, 128), f32),
            pltpu.VMEM((rows, FF), bf),
            pltpu.VMEM((rows, FF), bf),
            pltpu.VMEM((rows, 3 * D), bf),
            pltpu.VMEM((sents, HEADS, SEQ, SEQ), bf),
            pltpu.VMEM((rows, D), f32),
            pltpu.VMEM((rows, D), bf),
            pltpu.VMEM((rows, D), bf),
            pltpu.VMEM((rows, D), bf),
            pltpu.VMEM((D, rows), bf),
            pltpu.VMEM((D, rows), bf),
            pltpu.VMEM((3 * D, rows), bf),
            pltpu.VMEM((rows, HALF), bf),
            pltpu.VMEM((rows, 8), f32),
            pltpu.VMEM((sents * 8, D), f32),
            pltpu.VMEM((2, 16, PAD, 128), f32),
            pltpu.VMEM((16, FF), f32),
            pltpu.VMEM((3 * D, SEQ), bf),
            pltpu.VMEM((16, PAD, 128), f32),
            pltpu.VMEM((SEQ, FF), f32),
            pltpu.VMEM((9, 8, FF), f32),
            pltpu.VMEM((SEQ, 128), f32),
            pltpu.VMEM((SEQ, 128), f32),
            pltpu.VMEM((PAD, HALF), f32),
            pltpu.VMEM((32, D), f32),
        ],
        compiler_params=pltpu.CompilerParams(vmem_limit_bytes=63 << 20, collective_id=0, has_side_effects=True),
        name="back",
    )(lengths, pair_ids, cotangent, norm_gains, wg, w_glu, w_left, w_conv3, w_depth, w_point, w_qkv, *arrays)
    input_grad, norms, gain, glu, left, conv, depth, point, qkv, out, up, down = pl.pallas_call(
        functools.partial(last_kernel, share, wide_share),
        out_shape=[
            shape((rows, D), f32),
            shape((4, D), f32),
            shape((1, FF), f32),
            shape((share, 2 * D), f32),
            shape((share, FF), f32),
            shape((3, share, HALF), f32),
            shape((9, FF), f32),
            shape((wide_share, HALF), f32),
            shape((share, 3 * D), f32),
            shape((share, D), f32),
            shape((share, FF), f32),
            shape((wide_share, D), f32),
        ],
        in_specs=[vmem()] * 4,
        out_specs=[vmem()] * 12,
        compiler_params=params,
        name="last",
    )(final, early, late, input_grad)
    return cell_output, input_grad, norms, gain.reshape(FF), glu, left, conv, depth, point, qkv, out, up, down


def solution(mesh):
    dp, head = mesh.shape["dp"], mesh.shape["head"]
    ys = 2 ** ((dp.bit_length() - 1) // 2)
    grid = (dp // ys, ys)
    xs = head // 2
    row = P(("dp", "head"), None)
    in_specs = (row, P(("dp", "head")), P(("dp", "head")), row) + (P(),) * 11
    share = P("dp", None)
    out_specs = (row, row, P(), P(), share, share, P(None, "dp", None), P(), share, share, share, share, share)
    return jax.shard_map(
        functools.partial(local, grid, xs), mesh=mesh, in_specs=in_specs, out_specs=out_specs, check_vma=False
    )
```

```python
import functools

import jax
import jax.numpy as jnp
from jax import lax
from jax.experimental import pallas as pl
from jax.experimental.pallas import tpu as pltpu
from jax.sharding import PartitionSpec as P

HEADS = 8
DH = 64
SEQ = 256
PAIRS = 4
D = 512
FF = 2048
HALF = 256
PAD = SEQ + 16
EPS = 1e-05
MESH = pl.DeviceIdType.MESH
bf = jnp.bfloat16
f32 = jnp.float32
GELU_A = 0.7978845608028654
GELU_B = 0.7978845608028654 * 0.044715
CH = 32


def nn(a, b):
    return lax.dot_general(a, b, (((1,), (0,)), ((), ())), preferred_element_type=f32)


def nt(a, b):
    return lax.dot_general(a, b, (((1,), (1,)), ((), ())), preferred_element_type=f32)


def tn(a, b):
    return lax.dot_general(a, b, (((0,), (0,)), ((), ())), preferred_element_type=f32)


def gelu_both(v):
    square = v * v
    t = jnp.tanh(v * (GELU_A + GELU_B * square))
    half = 0.5 + 0.5 * t
    slope = half + (0.5 * v) * (1.0 - t * t) * (GELU_A + (3.0 * GELU_B) * square)
    return v * half, slope


def sigmoid(v):
    return 0.5 + 0.5 * jnp.tanh(0.5 * v)


def fold8(v):
    total = v[0:8]
    for i in range(1, v.shape[0] // 8):
        total = total + v[8 * i : 8 * i + 8]
    return total


def norm(v):
    centred = v - jnp.mean(v, axis=-1, keepdims=True)
    rstd = lax.rsqrt(jnp.mean(centred * centred, axis=-1, keepdims=True) + EPS)
    return centred, rstd


def norm_back(g, low, gain, inverse, rstd):
    gy = g * gain
    m1 = jnp.mean(gy, axis=-1, keepdims=True)
    m2 = jnp.mean(g * low, axis=-1, keepdims=True)
    return rstd * (gy - m1 - (low * inverse) * m2)


def at(s, first, size):
    return pl.ds(pl.multiple_of(s * SEQ + first, size), size)


def one_row(ref):
    return jnp.concatenate([ref[j : j + 1, :] for j in range(ref.shape[0])], axis=1).astype(f32)


def row_of(first, size):
    return first + lax.broadcasted_iota(jnp.int32, (size, 1), 0)


KEPT = (
    "a", "b", "e", "f", "rstd", "sig", "u", "dgl", "dgr", "m",
    "depth", "qkvt", "pt", "mixt", "up", "gup", "ga", "gmixt", "gain_f", "gl",
)


def kept_shapes(sents):
    rows = sents * SEQ
    shape = jax.ShapeDtypeStruct
    return {
        "a": shape((rows, D), bf),
        "b": shape((rows, D), bf),
        "e": shape((rows, D), bf),
        "f": shape((rows, D), bf),
        "rstd": shape((rows, 8), f32),
        "sig": shape((rows, D), bf),
        "u": shape((rows, D), bf),
        "dgl": shape((rows, FF), bf),
        "dgr": shape((rows, HALF), bf),
        "m": shape((sents, 16, PAD, 128), f32),
        "depth": shape((8, sents, SEQ, 256), bf),
        "qkvt": shape((3 * D, rows), bf),
        "pt": shape((sents, HEADS, SEQ, SEQ), bf),
        "mixt": shape((D, rows), bf),
        "up": shape((rows, FF), bf),
        "gup": shape((rows, FF), bf),
        "ga": shape((rows, D), f32),
        "gmixt": shape((D, rows), bf),
        "gain_f": shape((sents * 8, D), f32),
        "gl": shape((rows, D), bf),
    }


def part_of(name, s):
    if name in ("m", "pt"):
        return (s,)
    if name == "depth":
        return (slice(None), s)
    if name in ("qkvt", "mixt", "gmixt"):
        return (slice(None), pl.ds(pl.multiple_of(s * SEQ, SEQ), SEQ))
    if name == "gain_f":
        return (pl.ds(pl.multiple_of(s * 8, 8), 8),)
    return (pl.ds(pl.multiple_of(s * SEQ, SEQ), SEQ),)


WEIGHTS = ((D, 2 * D), (D, FF), (3, D, HALF), (FF, HALF), (D, 3 * D), (D, D), (D, FF), (FF, D))


def front_kernel(
    sents,
    grid,
    xs,
    len_ref,
    pair_ref,
    x_ref,
    cot_ref,
    gains_ref,
    wg_ref,
    wglu,
    wleft,
    wconv,
    wdepth,
    wpoint,
    wqkv,
    wout,
    wup,
    wdown,
    out_far,
    *refs,
):
    far, refs = dict(zip(KEPT, refs)), refs[len(KEPT) :]
    held, refs = refs[: len(WEIGHTS) + 1], refs[len(WEIGHTS) + 1 :]
    weights = (wglu, wleft, wconv, wpoint, wqkv, wout, wup, wdown, cot_ref)
    load_sems, out_ref, refs = refs[0], refs[1], refs[2:]
    load = [pltpu.make_async_copy(w, h, load_sems.at[k]) for k, (w, h) in enumerate(zip(weights, held))]
    for copy in load[:3]:
        copy.start()
    wglu, wleft, wconv, wpoint, wqkv, wout, wup, wdown, cot_ref = held
    near, refs = dict(zip(KEPT, refs)), refs[len(KEPT) :]
    ship_sems, wp_ref, xf_ref, bs_ref, wide_ref, sep_ref, qkv_ref = refs[:7]
    send_sems, recv_sems, count_ref, count_got, fac_ref = refs[7:]
    sums = Sums(grid, xs, (), None, None, None, send_sems, recv_sems)
    sums.greet(False)
    lane = lax.broadcasted_iota(jnp.int32, (8, 128), 1)
    counts = jnp.zeros((8, 128), f32)
    for s in range(sents):
        counts = counts + jnp.where(lane == pair_ref[s], len_ref[s].astype(f32), 0.0)
    count_ref[3] = counts
    sums.small_send(0, 3, count_ref, count_got)

    def count_next(axis):
        sums.small_add(0, axis, count_ref, count_got)
        if axis:
            for copy in sums.small_copies(0, axis - 1, count_ref, count_got):
                copy.start()
        else:
            counts = count_ref[4]
            total = jnp.sum(counts, axis=1, keepdims=True)
            for k in range(sents):
                mine = jnp.sum(jnp.where(lane == pair_ref[k], counts, 0.0), axis=1, keepdims=True)
                fac_ref[k] = jnp.broadcast_to(total / (PAIRS * mine), (8, 128))

    (a_ref, b_ref, e_ref, f_ref, rstd_ref, sig_ref, u_ref, dgl_ref, dgr_ref, m_ref) = [near[n] for n in KEPT[:10]]
    (depth_ref, qkvt_ref, pt_ref, mixt_ref, up_ref, gup_ref, ga_ref, gmixt_ref, gain_f_ref, gl_ref) = [near[n] for n in KEPT[10:]]

    def shipment(name, s):
        k = KEPT.index(name)
        where = part_of(name, s)
        return pltpu.make_async_copy(near[name].at[where], far[name].at[where], ship_sems.at[k, s])

    def leave(s):
        return pltpu.make_async_copy(out_ref.at[at(s, 0, SEQ), :], out_far.at[at(s, 0, SEQ), :], ship_sems.at[len(KEPT), s])

    def ship(s, *names):
        for name in names:
            shipment(name, s).start()

    wp_ref[0:9, :] = wdepth[...].astype(f32) * one_row(wg_ref)
    gain_f_ref[...] = jnp.zeros_like(gain_f_ref)
    zero8 = jnp.zeros((8, 128), f32)

    def sentence(s, carry):
        mark = Marks()
        length = len_ref[s]

        def loaded(*which, then=(), axis=None):
            @pl.when(s == 0)
            def _():
                for k in which:
                    load[k].wait()
                for k in then:
                    load[k].start()
                if axis is not None:
                    count_next(axis)

        gains = gains_ref[...].astype(f32)
        rows = at(s, 0, SEQ)
        mark("fw_glu")
        for c in range(0, SEQ, CH):
            cen, rstd = norm(x_ref[at(s, c, CH), :].astype(f32))
            a_ref[at(s, c, CH), :] = (cen * rstd * gains[0:1]).astype(bf)
            rstd_ref[at(s, c, CH), 0:1] = rstd
        a_low = a_ref[rows, :]
        loaded(0, then=(3, 4))
        for n in range(2):
            cols = slice(256 * n, 256 * n + 256)
            gcols = slice(512 + 256 * n, 768 + 256 * n)
            value = nn(a_low, wglu[:, cols])
            gate = nn(a_low, wglu[:, gcols])
            for c in range(0, SEQ, CH):
                sig = sigmoid(gate[c : c + CH])
                mixed = value[c : c + CH] * sig
                xf_ref[c : c + CH, cols] = x_ref[at(s, c, CH), cols].astype(f32) + mixed
                sig_ref[at(s, c, CH), cols] = sig.astype(bf)
                u_ref[at(s, c, CH), cols] = (mixed * (1.0 - sig)).astype(bf)
        ship(s, "a", "sig", "u")
        mark("fw_norm_b")
        for c in range(0, SEQ, CH):
            cen, rstd = norm(xf_ref[c : c + CH, :])
            rstd = jnp.where(row_of(c, CH) < length, rstd, 0.0)
            b_low = cen * rstd * gains[1:2]
            b_ref[at(s, c, CH), :] = b_low.astype(bf)
            rstd_ref[at(s, c, CH), 1:2] = rstd
            bs_ref[8 + c : 8 + c + CH, :] = b_low
        mark("fw_left")
        b_low = b_ref[rows, :]
        bs_ref[0:8, :] = jnp.zeros((8, D), f32)
        bs_ref[8 + SEQ : 16 + SEQ, :] = jnp.zeros((8, D), f32)
        loaded(1, 2, then=(5, 6, 7, 8), axis=3)
        right = (
            nn(bs_ref[7 : 7 + SEQ, :].astype(bf), wconv[0])
            + nn(b_low, wconv[1])
            + nn(bs_ref[9 : 9 + SEQ, :].astype(bf), wconv[2])
        )
        for n in range(8):
            cols = slice(256 * n, 256 * n + 256)
            left = nn(b_low, wleft[:, cols])
            for c in range(0, SEQ, CH):
                hidden, slope = gelu_both(left[c : c + CH])
                dgl_ref[at(s, c, CH), cols] = slope.astype(bf)
                if n == 0:
                    extra, slope = gelu_both(right[c : c + CH])
                    dgr_ref[at(s, c, CH), :] = slope.astype(bf)
                    hidden = hidden + extra
                wide_ref[c : c + CH, cols] = hidden
        ship(s, "b", "dgl", "dgr")
        mark("fw_wide_norm")
        for j in range(16):
            m_ref[s, j, 0:8, :] = zero8
            m_ref[s, j, 8 + SEQ : PAD, :] = zero8
        for c in range(0, SEQ, 8):
            mean = jnp.mean(wide_ref[c : c + 8, :], axis=-1, keepdims=True)
            cen = wide_ref[c : c + 8, :] - mean
            rstd = lax.rsqrt(jnp.mean(cen * cen, axis=-1, keepdims=True) + EPS)
            rstd = jnp.where(row_of(c, 8) < length, rstd, 0.0)
            rstd_ref[at(s, c, 8), 2:3] = rstd
            for j in range(16):
                m_ref[s, j, 8 + c : 16 + c, :] = cen[:, 128 * j : 128 * j + 128] * rstd
        mark("fw_depth")
        for j in range(16):
            cols = slice(128 * j, 128 * j + 128)
            taps = [wp_ref[o : o + 1, cols] for o in range(9)]
            for c in range(0, SEQ, CH):
                total = m_ref[s, j, c + 4 : c + 4 + CH, :] * taps[0]
                for o in range(1, 9):
                    total = total + m_ref[s, j, c + 4 + o : c + 4 + o + CH, :] * taps[o]
                depth_ref[j // 2, s, c : c + CH, 128 * (j % 2) : 128 * (j % 2) + 128] = total.astype(bf)
        ship(s, "m", "depth")
        mark("fw_point")
        loaded(3, axis=2)
        depth = jnp.concatenate([depth_ref[n, s] for n in range(8)], axis=1)
        sep_ref[...] = nn(depth, wpoint[...])
        mark("fw_qkv")
        for c in range(0, SEQ, CH):
            conv = xf_ref[c : c + CH, :]
            conv = jnp.concatenate([conv[:, :HALF] + sep_ref[c : c + CH, :], conv[:, HALF:]], axis=1)
            xf_ref[c : c + CH, :] = conv
            cen, rstd = norm(conv)
            e_ref[at(s, c, CH), :] = (cen * rstd * gains[2:3]).astype(bf)
            rstd_ref[at(s, c, CH), 3:4] = rstd
        e_low = e_ref[rows, :]
        loaded(4)
        for n in range(6):
            cols = slice(256 * n, 256 * n + 256)
            part = nn(e_low, wqkv[:, cols]).astype(bf)
            qkv_ref[:, cols] = part
            qkvt_ref[cols, at(s, 0, SEQ)] = part.T
        ship(s, "e", "qkvt")
        mark("fw_attend")
        bias = jnp.where(row_of(0, SEQ) < jnp.maximum(length, 1), 0.0, -1e30)
        for h in range(HEADS):
            base = 3 * DH * h
            key = qkv_ref[:, base + DH : base + 2 * DH] * jnp.asarray(DH**-0.5, bf)
            query_t = qkvt_ref[base : base + DH, at(s, 0, SEQ)]
            value_t = qkvt_ref[base + 2 * DH : base + 3 * DH, at(s, 0, SEQ)]
            for q in range(0, SEQ, 128):
                scores = nn(key, query_t[:, q : q + 128]) + bias
                scores = jnp.exp(scores - jnp.max(scores, axis=0, keepdims=True))
                scores = scores * (1.0 / jnp.sum(scores, axis=0, keepdims=True))
                pt_ref[s, h, :, q : q + 128] = scores.astype(bf)
            mixt_ref[DH * h : DH * h + DH, at(s, 0, SEQ)] = nn(value_t, pt_ref[s, h]).astype(bf)
        ship(s, "pt", "mixt")
        mark("fw_out")
        loaded(5, axis=1)
        for n in range(2):
            cols = slice(256 * n, 256 * n + 256)
            xf_ref[:, cols] += tn(mixt_ref[:, at(s, 0, SEQ)], wout[:, cols])
        mark("fw_up")
        for c in range(0, SEQ, CH):
            cen, rstd = norm(xf_ref[c : c + CH, :])
            f_ref[at(s, c, CH), :] = (cen * rstd * gains[3:4]).astype(bf)
            rstd_ref[at(s, c, CH), 4:5] = rstd
        f_low = f_ref[rows, :]
        loaded(6)
        for n in range(8):
            cols = slice(256 * n, 256 * n + 256)
            up = nn(f_low, wup[:, cols])
            for c in range(0, SEQ, CH):
                low, slope = gelu_both(up[c : c + CH])
                up_ref[at(s, c, CH), cols] = low.astype(bf)
                gup_ref[at(s, c, CH), cols] = slope.astype(bf)
        mark("fw_down")
        loaded(7, 8, axis=0)
        for n in range(2):
            cols = slice(256 * n, 256 * n + 256)
            down = nn(up_ref[rows, :], wdown[:, cols])
            out_ref[rows, cols] = (xf_ref[:, cols] + down).astype(bf)
        ship(s, "f", "rstd", "up")
        leave(s).start()
        mark("bw_down")
        for c in range(0, SEQ, CH):
            weight = jnp.where(row_of(c, CH) < length, fac_ref[s, 0:1, 0:1], 0.0)
            g_out = cot_ref[at(s, c, CH), :].astype(f32) * weight
            ga_ref[at(s, c, CH), :] = g_out
            gl_ref[at(s, c, CH), :] = g_out.astype(bf)
        g_low = gl_ref[rows, :]
        for n in range(8):
            cols = slice(256 * n, 256 * n + 256)
            back = nt(g_low, wdown[cols, :])
            gup_ref[rows, cols] = (back * gup_ref[rows, cols].astype(f32)).astype(bf)
        mark("bw_up")
        ship(s, "gup", "gl")
        for n in range(2):
            cols = slice(256 * n, 256 * n + 256)
            wide_ref[:, cols] = nt(gup_ref[rows, :], wup[cols, :])
        inverse = 1.0 / gains[3:4]
        for c in range(0, SEQ, CH):
            g_f = wide_ref[c : c + CH, 0:D]
            low = f_ref[at(s, c, CH), :].astype(f32)
            gain_f_ref[pl.ds(pl.multiple_of(s * 8, 8), 8), :] += fold8(g_f * low)
            back = norm_back(g_f, low, gains[3:4], inverse, rstd_ref[at(s, c, CH), 4:5])
            ga_ref[at(s, c, CH), :] += back
        gmixt_ref[:, at(s, 0, SEQ)] = nt(wout[...], ga_ref[rows, :].astype(bf)).astype(bf)
        ship(s, "ga", "gmixt", "gain_f")
        mark()
        return carry

    lax.fori_loop(0, sents, sentence, 0)

    def landed(s, carry):
        for name in KEPT:
            shipment(name, s).wait()
        leave(s).wait()
        return carry

    lax.fori_loop(0, sents, landed, 0)
    for axis in range(4):
        for copy in sums.small_copies(0, axis, count_ref, count_got):
            copy.wait_send()


class Marks:
    def __init__(self):
        self.open = None

    def __call__(self, name=None):
        if self.open is not None:
            self.open.__exit__(None, None, None)
        self.open = None
        if name is not None:
            self.open = jax.named_scope(name)
            self.open.__enter__()


def vmem():
    return pl.BlockSpec(memory_space=pltpu.VMEM)


def smem():
    return pl.BlockSpec(memory_space=pltpu.SMEM)


def offsets(share, wide_share):
    sizes = (
        ("up", 8 * share, True),
        ("down", 2 * wide_share, True),
        ("out", 2 * share, False),
        ("qkv", 6 * share, True),
        ("point", wide_share, True),
        ("left", 4 * share, True),
        ("left2", 4 * share, True),
        ("conv", 3 * share, True),
        ("glu", 2 * share, True),
        ("glu1", 2 * share, True),
    )
    first, starts, groups, begin = 0, {}, [], 0
    for name, size, ends in sizes:
        starts[name] = first
        first += size
        if ends:
            first = -(-first // 32) * 32
            groups.append((begin, first - begin))
            begin = first
    return starts, groups, first


def put(g_ref, grid, tile, first, share, wide, chunk=0):
    _, ys = grid
    for part in range(tile.shape[1] // 256):
        for k in range(512 // share):
            block = chunk * (512 // share) + k
            piece = tile[k * share : (k + 1) * share, 256 * part : 256 * part + 256]
            rows = pl.ds(pl.multiple_of(first + part * share, 16), share)
            g_ref[block // ys, block % ys, rows, :] = piece.astype(bf)


SCHEDULE = {
    "grad_up3": (0,),
    "grad_down3": (1,),
    "grad_out": (0,),
    "attend1a": (1,),
    "grad_qkv0": (0,),
    "grad_qkv2": (2,),
    "grad_point2": (1, 2,),
    "grad_point3": (3,),
    "wide0b": (0, 3,),
    "wide1b": (1,),
    "wide2a": (0, 2,),
    "wide2c": (3, 1, 0,),
    "grad_left1": (4,),
    "grad_left3": (5, 1,),
    "grad_conv": (6, 2, 4,),
    "inputs0": (5, 3, 6,),
    "inputs1": (-1,),
    "inputs2": (2,),
    "grad_glu0": (7, 4,),
    "grad_glu1": (8,),
    "inputs_end1": (7, 5, 3,),
    "inputs_end2": (8, 6,),
    "end": (4, -1, -2, 2, 5, 7, 3, 6, 8, -2, -1, 4, 5, -2, 4, 7, 6, 5, 8, 6, -1, -2, 7, 8, 7, 8,),
}


def back_kernel(
    sents,
    grid,
    xs,
    names,
    gains_ref,
    wg_ref,
    wglu_far,
    wleft_far,
    wconv_far,
    wdepth,
    wpoint_far,
    wqkv_far,
    *refs,
):
    far, refs = dict(zip(KEPT, refs)), refs[len(KEPT) :]
    xgrad_far, final_far, early_far, late_far = refs[:4]
    recv, refs = dict(zip(names, refs[4:])), refs[4 + len(names) :]
    (wglu, wleft, wconv, wpoint, wqkv), refs = refs[:5], refs[5:]
    (
        fetch_sems,
        send_sems,
        recv_sems,
        g_ref,
        final_ref,
        early_ref,
        early_got,
        late_ref,
        late_got,
        first_wide,
        second_wide,
        gqkv_ref,
        squares,
        conv_ref,
        gl_ref,
        fs_ref,
        gas_ref,
        mixt_ref,
        gmixt_ref,
        qkvt_ref,
        dgr_ref,
        rstd_ref,
        gain_f_ref,
        m_ref,
        wp_ref,
        gqkvt_ref,
        gd_ref,
        wide_ref,
        taps_ref,
        s1_ref,
        s2_ref,
        right_ref,
        gain_ref,
    ) = refs
    e_ref = gas_ref
    gr_refs = (gl_ref.at[:, 0:HALF], gl_ref.at[:, HALF:D], fs_ref.at[:, 0:HALF])
    sep_ref = fs_ref.at[:, HALF:D]
    up_ref = gleft_ref = dgl_ref = first_wide
    gup_ref = second_wide
    a_ref, b_ref, sig_ref, u_ref = [second_wide.at[:, D * k : D * k + D] for k in range(4)]
    gg_ref = gqkv_ref
    pt_ref, depth_view = squares, squares.reshape(8, sents, SEQ, 256)
    where = dict(
        a=a_ref, b=b_ref, e=e_ref, f=fs_ref, rstd=rstd_ref, sig=sig_ref, u=u_ref, dgl=first_wide, dgr=dgr_ref,
        qkvt=qkvt_ref, mixt=mixt_ref, up=first_wide, gup=second_wide, ga=conv_ref, gmixt=gmixt_ref, gain_f=gain_f_ref,
        pt=squares, depth=depth_view, gl=gl_ref, wglu=wglu, wleft=wleft, wconv=wconv, wpoint=wpoint, wqkv=wqkv,
    )
    far.update(wglu=wglu_far, wleft=wleft_far, wconv=wconv_far, wpoint=wpoint_far, wqkv=wqkv_far)
    order = (
        "gmixt", "qkvt", "pt", "f", "gup", "ga", "gl", "up", "gain_f", "rstd", "mixt", "wqkv", "wpoint", "dgr",
        "wleft", "wconv", "wglu", "e", "b", "a", "sig", "u", "dgl", "depth",
    )

    def fetch(name):
        return pltpu.make_async_copy(far[name], where[name], fetch_sems.at[order.index(name)])

    def start(*names):
        for name in names:
            fetch(name).start()

    def wait(*names):
        for name in names:
            fetch(name).wait()

    def fetch_m(s):
        return pltpu.make_async_copy(far["m"].at[s], m_ref.at[s % 2], fetch_sems.at[len(order) + s % 2])

    start("gup", "f", "up", "gl", "ga", "mixt", "rstd", "gain_f")
    share, wide_share = 512 // (grid[0] * grid[1]), 2048 // (grid[0] * grid[1])
    starts, groups, _ = offsets(share, wide_share)
    sums = Sums(grid, xs, groups, g_ref, final_ref, recv, send_sems, recv_sems)
    with jax.named_scope("greet"):
        sums.greet()
    smalls = {-1: (1, early_ref, early_got), -2: (2, late_ref, late_got)}
    small_axis = {-1: 3, -2: 3}

    def claim(name):
        steps = []
        for i in SCHEDULE.get(name, ()):
            if i >= 0:
                steps += sums.claim(i)
            elif small_axis[i] >= 0:
                steps.append((i, small_axis[i]))
                small_axis[i] -= 1
        return steps

    def do(steps):
        for i, stage in steps:
            if i >= 0:
                sums.do([(i, stage)])
            else:
                k, held, got = smalls[i]
                sums.small_next(k, stage, held, got)

    def point(name):
        do(claim(name))

    def loop(name, first, last, body, parts=""):
        claims = {(k, part): claim(f"{name}{k}{part}") for k in range(first, last) for part in parts or ("",)}

        def within(k, part):
            for n in range(first, last):
                if claims[n, part]:
                    pl.when(k == n)(functools.partial(do, claims[n, part]))

        def round(k, carry):
            body(k, within)
            if not parts:
                within(k, "")
            return carry

        with jax.named_scope(name):
            lax.fori_loop(first, last, round, 0)

    wp_ref[0:9, :] = wdepth[...].astype(f32) * one_row(wg_ref)
    gain_ref[...] = jnp.zeros_like(gain_ref)
    taps_ref[...] = jnp.zeros_like(taps_ref)

    def wide_tile(i):
        return pl.ds(pl.multiple_of(i * 512, 512), 512)

    wait("f", "gup")

    def grad_up(i, within):
        tile = tn(fs_ref[...], gup_ref[:, wide_tile(i)])
        put(g_ref, grid, tile, starts["up"] + i * 2 * share, share, False)

    loop("grad_up", 0, 4, grad_up)
    wait("up", "gl")
    start("gmixt", "qkvt", "pt", "b", "a", "sig", "u")

    def grad_down(i, within):
        put(g_ref, grid, tn(up_ref[:, wide_tile(i)], gl_ref[...]), starts["down"], wide_share, True, i)

    loop("grad_down", 0, 4, grad_down)
    wait("ga", "mixt", "rstd", "gain_f")
    start("dgl", "wqkv")
    for c in range(0, sents * SEQ, CH):
        gas_ref[c : c + CH, :] = conv_ref[c : c + CH, :].astype(bf)
    with jax.named_scope("grad_out"):
        put(g_ref, grid, nn(mixt_ref[...], gas_ref[...]), starts["out"], share, False)
    start("e", "wpoint", "dgr")
    point("grad_out")

    for s in range(sents):
        gain_ref[24:32, :] += gain_f_ref[8 * s : 8 * s + 8, :]
    wait("gmixt", "qkvt", "pt")

    def attend(s, within):
        rows = at(s, 0, SEQ)
        for h in range(HEADS):
            base = 3 * DH * h
            g_o = gmixt_ref[DH * h : DH * h + DH, rows]
            query_t = qkvt_ref[base : base + DH, rows]
            key_t = qkvt_ref[base + DH : base + 2 * DH, rows]
            value = qkvt_ref[base + 2 * DH : base + 3 * DH, rows].T
            probs = pt_ref[s, h]
            halves = []
            for q in range(0, SEQ, 128):
                part = probs[:, q : q + 128].astype(f32)
                back = nn(value, g_o[:, q : q + 128])
                both = part * back
                halves.append((both - part * jnp.sum(both, axis=0, keepdims=True)).astype(bf))
            g_scores = jnp.concatenate(halves, axis=1)
            gqkvt_ref[base : base + DH, :] = (nn(key_t, g_scores) * DH**-0.5).astype(bf)
            gqkvt_ref[base + DH : base + 2 * DH, :] = (nt(query_t, g_scores) * DH**-0.5).astype(bf)
            gqkvt_ref[base + 2 * DH : base + 3 * DH, :] = nt(g_o, probs).astype(bf)
            if h % 4 == 3:
                within(s, "ab"[h // 4])
        for n in range(6):
            cols = slice(256 * n, 256 * n + 256)
            gqkv_ref[rows, cols] = gqkvt_ref[cols, :].T

    loop("attend", 0, sents, attend, "ab")
    start("depth")
    fetch_m(0).start()
    if sents > 1:
        fetch_m(1).start()
    wait("e")

    def grad_qkv(i, within):
        put(g_ref, grid, tn(e_ref[...], gqkv_ref[:, wide_tile(i)]), starts["qkv"] + i * 2 * share, share, False)

    loop("grad_qkv", 0, 3, grad_qkv)

    def attention_input(s, within):
        gains = gains_ref[...].astype(f32)
        inverse = 1.0 / gains[2:3]
        rows = at(s, 0, SEQ)
        for n in range(2):
            cols = slice(256 * n, 256 * n + 256)
            wide_ref[:, cols] = nt(gqkv_ref[rows, :], wqkv[cols, :])
        for c in range(0, SEQ, CH):
            part = at(s, c, CH)
            g_e = wide_ref[c : c + CH, 0:D]
            low = e_ref[part, :].astype(f32)
            gain_ref[16:24, :] += fold8(g_e * low)
            g_conv = conv_ref[part, :] + norm_back(g_e, low, gains[2:3], inverse, rstd_ref[part, 3:4])
            conv_ref[part, :] = g_conv
            sep_ref[part, :] = g_conv[:, :HALF].astype(bf)

    wait("wqkv")
    loop("attention_input", 0, sents, attention_input)
    wait("depth")

    def grad_point(i, within):
        depth = [depth_view[2 * i + k].reshape(sents * SEQ, 256) for k in range(2)]
        put(g_ref, grid, tn(jnp.concatenate(depth, axis=1), sep_ref[...]), starts["point"], wide_share, True, i)

    loop("grad_point", 0, 4, grad_point)
    start("wleft", "wconv", "wglu")
    wait("b", "a", "sig", "u", "dgr", "dgl", "wpoint")

    zero8 = jnp.zeros((8, 128), f32)

    def wide(s, within):
        rows = at(s, 0, SEQ)
        mark = Marks()
        mark("g_depth")
        slot = s % 2
        fetch_m(s).wait()
        for n in range(8):
            back = nt(sep_ref[rows, :], wpoint[256 * n : 256 * n + 256, :])
            for k in range(2):
                gd_ref[2 * n + k, 8 : 8 + SEQ, :] = back[:, 128 * k : 128 * k + 128]
        mark()
        within(s, "a")
        mark("taps")
        for j in range(16):
            gd_ref[j, 0:8, :] = zero8
            gd_ref[j, 8 + SEQ : PAD, :] = zero8
            cols = slice(128 * j, 128 * j + 128)
            taps = [wp_ref[o : o + 1, cols] for o in range(9)]
            lines = [taps_ref[o, :, cols] for o in range(9)]
            for c in range(0, SEQ, CH):
                total = gd_ref[j, c + 12 : c + 12 + CH, :] * taps[0]
                for o in range(1, 9):
                    total = total + gd_ref[j, c + 12 - o : c + 12 - o + CH, :] * taps[o]
                wide_ref[c : c + CH, cols] = total
                mine = m_ref[slot, j, c + 8 : c + 8 + CH, :]
                if j == 0:
                    s1_ref[c : c + CH, :] = total
                    s2_ref[c : c + CH, :] = total * mine
                else:
                    s1_ref[c : c + CH, :] += total
                    s2_ref[c : c + CH, :] += total * mine
                back = gd_ref[j, c + 8 : c + 8 + CH, :]
                for o in range(9):
                    lines[o] = lines[o] + fold8(m_ref[slot, j, c + 4 + o : c + 4 + o + CH, :] * back)
            for o in range(9):
                taps_ref[o, :, cols] = lines[o]
        mark()
        within(s, "b")
        mark("g_hidden")
        right_ref[0:8, :] = jnp.zeros((8, HALF), f32)
        right_ref[8 + SEQ : PAD, :] = jnp.zeros((8, HALF), f32)
        for c in range(0, SEQ, CH):
            part = at(s, c, CH)
            rstd = rstd_ref[part, 2:3]
            m1 = jnp.sum(s1_ref[c : c + CH, :], axis=-1, keepdims=True) * (rstd / FF)
            m2 = jnp.sum(s2_ref[c : c + CH, :], axis=-1, keepdims=True) * (rstd / FF)
            for j in range(16):
                cols = slice(128 * j, 128 * j + 128)
                g_h = wide_ref[c : c + CH, cols] * rstd - m1 - m_ref[slot, j, c + 8 : c + 8 + CH, :] * m2
                gleft_ref[part, cols] = (g_h * dgl_ref[part, cols].astype(f32)).astype(bf)
                if j < 2:
                    right_ref[8 + c : 8 + c + CH, cols] = g_h * dgr_ref[part, cols].astype(f32)
        mark()

        @pl.when(s + 2 < sents)
        def _():
            fetch_m(s + 2).start()

        for k in range(3):
            gr_refs[k][rows, :] = right_ref[9 - k : 9 - k + SEQ, :].astype(bf)
        within(s, "c")

    loop("wide", 0, sents, wide, "abc")
    for i in range(4):
        with jax.named_scope("grad_left"):
            put(g_ref, grid, tn(b_ref[...], gleft_ref[:, 512 * i : 512 * i + 512]), starts[("left", "left2")[i // 2]] + i % 2 * 2 * share, share, False)
        point(f"grad_left{i}")
    for k in range(3):
        with jax.named_scope("grad_conv"):
            put(g_ref, grid, tn(b_ref[...], gr_refs[k][...]), starts["conv"] + k * share, share, False)
    point("grad_conv")

    wide_gain = one_row(wg_ref)
    total = jnp.zeros((1, FF), f32)
    for o in range(9):
        lines = jnp.sum(taps_ref[o], axis=0, keepdims=True)
        total = total + lines * wdepth[o : o + 1, :].astype(f32)
        early_ref[3, o : o + 1, :] = lines * wide_gain
    early_ref[3, 9:10, :] = total
    early_ref[3, 10:16, :] = jnp.zeros((6, FF), f32)

    def gain_row(i):
        return jnp.sum(gain_ref[8 * i : 8 * i + 8, :], axis=0, keepdims=True) / gains_ref[i : i + 1, :].astype(f32)

    early_ref[3, 10:11, 0:D] = gain_row(2)
    early_ref[3, 11:12, 0:D] = gain_row(3)
    sums.small_send(1, 3, early_ref, early_got)
    point("taps")

    def inputs(s, within):
        gains = gains_ref[...].astype(f32)
        rows = at(s, 0, SEQ)
        mark = Marks()
        mark("g_b")
        for n in range(2):
            cols = slice(256 * n, 256 * n + 256)
            g_b = nt(gleft_ref[rows, :], wleft[cols, :])
            for k in range(3):
                g_b = g_b + nt(gr_refs[k][rows, :], wconv[k, cols, :])
            wide_ref[:, cols] = g_b
        mark("norm_b")
        inverse = 1.0 / gains[1:2]
        for c in range(0, SEQ, CH):
            part = at(s, c, CH)
            g_b = wide_ref[c : c + CH, 0:D]
            low = b_ref[part, :].astype(f32)
            gain_ref[8:16, :] += fold8(g_b * low)
            g_glu = conv_ref[part, :] + norm_back(g_b, low, gains[1:2], inverse, rstd_ref[part, 1:2])
            conv_ref[part, :] = g_glu
            gg_ref[part, 0:D] = (g_glu * sig_ref[part, :].astype(f32)).astype(bf)
            gg_ref[part, D : 2 * D] = (g_glu * u_ref[part, :].astype(f32)).astype(bf)
        mark()

    def inputs_end(s, within):
        gains = gains_ref[...].astype(f32)
        rows = at(s, 0, SEQ)
        mark = Marks()
        mark("g_a")
        for n in range(2):
            cols = slice(256 * n, 256 * n + 256)
            wide_ref[:, cols] = nt(gg_ref[rows, 0 : 2 * D], wglu[cols, :])
        mark("norm_a")
        inverse = 1.0 / gains[0:1]
        for c in range(0, SEQ, CH):
            part = at(s, c, CH)
            g_a = wide_ref[c : c + CH, 0:D]
            low = a_ref[part, :].astype(f32)
            gain_ref[0:8, :] += fold8(g_a * low)
            conv_ref[part, :] += norm_back(g_a, low, gains[0:1], inverse, rstd_ref[part, 0:1])
        mark()

    wait("wleft", "wconv", "wglu")
    loop("inputs", 0, sents, inputs)
    for i in range(2):
        with jax.named_scope("grad_glu"):
            put(g_ref, grid, tn(a_ref[...], gg_ref[:, 512 * i : 512 * i + 512]), starts[("glu", "glu1")[i]], share, False)
        point(f"grad_glu{i}")
    loop("inputs_end", 0, sents, inputs_end)
    leave = pltpu.make_async_copy(conv_ref, xgrad_far, fetch_sems.at[len(order) + 2])
    leave.start()
    late_ref[3] = jnp.zeros((8, D), f32)
    late_ref[3, 0:1, :] = gain_row(0)
    late_ref[3, 1:2, :] = gain_row(1)
    sums.small_send(2, 3, late_ref, late_got)
    point("end")
    for _ in range(sums.STAGES + 1):
        sums.advance(*range(len(groups)))
    for i, (k, held, got) in smalls.items():
        while small_axis[i] >= 0:
            sums.small_next(k, small_axis[i], held, got)
            small_axis[i] -= 1
    ends = (final_ref, final_far), (early_ref.at[4], early_far), (late_ref.at[4], late_far)
    ends = [pltpu.make_async_copy(*pair, fetch_sems.at[len(order) + 3 + k]) for k, pair in enumerate(ends)]
    for copy in ends:
        copy.start()
    with jax.named_scope("finish"):
        sums.finish()
    leave.wait()
    for copy in ends:
        copy.wait()


def coordinates(ys):
    dp, head = lax.axis_index("dp"), lax.axis_index("head")
    return dp // ys, dp % ys, head // 2, head % 2


def device(ys, z, y, x, c):
    return (z * ys + y, x * 2 + c)


def rows16(first, size):
    return pl.ds(pl.multiple_of(first, 16), size)


def split_of(size, xs):
    half = size // 2
    first = (half // (32 * xs)) * 16 * xs
    return half, first, half - first


class Sums:
    STAGES = 5

    def __init__(self, grid, xs, groups, g_ref, final_ref, recv, send_sems, recv_sems):
        self.zs, self.ys = grid
        self.xs = xs
        self.sizes = (*grid, xs, 2)
        self.groups = groups
        self.g, self.final = g_ref, final_ref
        self.recv = recv
        self.send_sems, self.recv_sems = send_sems, recv_sems
        self.place = coordinates(self.ys)
        self.stage = [-1] * len(groups)
        self.small = []

    def peers(self, axis):
        size = self.sizes[axis]
        for step in range(1, size):
            to = list(self.place)
            to[axis] = lax.rem(to[axis] + step, size)
            yield step - 1, to[axis], device(self.ys, *to)

    def heads(self):
        z, y, x, c = self.place
        for dx in range(self.xs):
            for dc in range(2):
                if dx or dc:
                    yield device(self.ys, z, y, lax.rem(x + dx, self.xs), lax.rem(c + dc, 2))

    def greet(self, heads=True):
        barrier = pltpu.get_barrier_semaphore()
        others = [to for axis in range(2 if heads else 4) for _, _, to in self.peers(axis)]
        others += self.heads() if heads else []
        for to in others:
            pl.semaphore_signal(barrier, inc=1, device_id=to, device_id_type=MESH)
        total = len(others)
        pl.semaphore_wait(barrier, total)

    def core_first(self, i):
        return (self.groups[i][0] - (self.groups[3][0] if i > 2 else 0)) // 2

    def a_first(self, i):
        return sum(split_of(size, self.xs)[1] // self.xs for _, size in self.groups[:i])

    def b_first(self, i):
        return sum(split_of(size, self.xs)[2] for _, size in self.groups[:i])

    def rows(self, i):
        first, size = self.groups[i]
        half, na, nb = split_of(size, self.xs)
        mine = first + self.place[3] * half
        return first, half, mine, na, na // self.xs, mine + na, nb

    def plan(self, stage, i):
        z, y, x, c = self.place
        first, half, mine, na, part, b_row, nb = self.rows(i)
        g, recv, final = self.g, self.recv, self.final
        a_in, b_in = pl.ds(self.a_first(i), part), pl.ds(self.b_first(i), nb)
        a_rows, b_rows = rows16(mine + x * part, part), rows16(b_row, nb)
        axis_a, axis_b = ((None, 3), (2, 1), (1, 0), (0, 2), (None, 3))[stage]
        copies_a, copies_b = [], []
        for slot, other, to in self.peers(axis_b) if axis_b is not None else ():
            if stage == 0:
                source = g.at[:, :, rows16(first + other * half, half), :]
                target = recv["core"].at[:, :, pl.ds(self.core_first(i), half), :]
            elif stage == 1:
                source, target = g.at[:, other, b_rows, :], recv["b1"].at[slot, :, b_in, :]
            elif stage == 2:
                source, target = g.at[other, y, b_rows, :], recv["b2"].at[slot, b_in, :]
            elif stage == 3:
                source, target = g.at[z, y, b_rows, :], recv["b3"].at[slot, b_in, :]
            else:
                source, target = final.at[b_rows, :], final.at[b_rows, :]
            copies_b.append((source, target, to))
        for slot, other, to in self.peers(axis_a) if axis_a is not None and na else ():
            if stage == 1:
                source, target = g.at[:, :, rows16(mine + other * part, part), :], recv["a1"].at[slot, :, :, a_in, :]
            elif stage == 2:
                source, target = g.at[:, other, a_rows, :], recv["a2"].at[slot, :, a_in, :]
            else:
                source, target = g.at[other, y, a_rows, :], recv["a3"].at[slot, a_in, :]
            copies_a.append((source, target, to))
        if stage == 4 and na:
            copies_a = [(final.at[a_rows, :], final.at[a_rows, :], to) for to in self.heads()]
        return copies_b, copies_a

    def copies(self, stage, i):
        counts = self.counts(self.sizes)
        first = i * sum(map(sum, counts)) + sum(map(sum, counts[:stage]))
        copies_b, copies_a = self.plan(stage, i)
        made = []
        for copies, extra in ((copies_b, 0), (copies_a, counts[stage][0])):
            for n, (source, target, to) in enumerate(copies):
                index = first + extra + n
                made.append(
                    pltpu.make_async_remote_copy(
                        src_ref=source,
                        dst_ref=target,
                        send_sem=self.send_sems.at[index],
                        recv_sem=self.recv_sems.at[index],
                        device_id=to,
                        device_id_type=MESH,
                    )
                )
        return made

    @staticmethod
    def counts(sizes):
        z, y, x, _ = (size - 1 for size in sizes)
        return ((1, 0), (y, x), (z, y), (x, z), (1, 2 * x + 1))

    @staticmethod
    def semaphores(grid, xs, groups):
        sizes = (*grid, xs, 2)
        return len(groups) * sum(map(sum, Sums.counts(sizes))) + 12 * (max(sizes) - 1)

    def claim(self, *groups):
        steps = []
        for i in groups:
            if self.stage[i] < self.STAGES:
                steps.append((i, self.stage[i]))
                self.stage[i] += 1
        return steps

    def do(self, steps):
        for i, stage in steps:
            if stage >= 0:
                with jax.named_scope(f"await_{i}_{stage}"):
                    for copy in self.copies(stage, i):
                        copy.wait_recv()
                with jax.named_scope(f"add_{i}_{stage}"):
                    self.add(stage, i)
            if stage + 1 < self.STAGES:
                for copy in self.copies(stage + 1, i):
                    copy.start()

    def advance(self, *groups):
        self.do(self.claim(*groups))

    def over(self, i):
        return self.stage[i] == self.STAGES

    def add(self, stage, i):
        z, y, x, c = self.place
        first, half, mine, na, part, b_row, nb = self.rows(i)
        g, recv = self.g, self.recv
        a_in, b_in = pl.ds(self.a_first(i), part), pl.ds(self.b_first(i), nb)
        a_rows, b_rows = rows16(mine + x * part, part), rows16(b_row, nb)

        def total(mine, got):
            value = mine.astype(f32)
            for other in got:
                value = value + other.astype(f32)
            return value.astype(bf)

        if stage == 0:

            def core(block, carry):
                zb, yb = block // self.ys, block % self.ys
                g[zb, yb, rows16(mine, half), :] += recv["core"][zb, yb, pl.ds(self.core_first(i), half), :]
                return carry

            lax.fori_loop(0, self.zs * self.ys, core, 0)
        elif stage == 1:

            def one(zb, carry):
                got = [recv["b1"][slot, zb, b_in, :] for slot in range(self.ys - 1)]
                g[zb, y, b_rows, :] = total(g[zb, y, b_rows, :], got)
                for yb in range(self.ys) if na else ():
                    got = [recv["a1"][slot, zb, yb, a_in, :] for slot in range(self.xs - 1)]
                    g[zb, yb, a_rows, :] = total(g[zb, yb, a_rows, :], got)
                return carry

            lax.fori_loop(0, self.zs, one, 0)
        elif stage == 2:
            g[z, y, b_rows, :] = total(g[z, y, b_rows, :], [recv["b2"][slot, b_in, :] for slot in range(self.zs - 1)])
            if na:

                def two(zb, carry):
                    got = [recv["a2"][slot, zb, a_in, :] for slot in range(self.ys - 1)]
                    g[zb, y, a_rows, :] = total(g[zb, y, a_rows, :], got)
                    return carry

                lax.fori_loop(0, self.zs, two, 0)
        elif stage == 3:
            got = [recv["b3"][slot, b_in, :] for slot in range(self.xs - 1)]
            self.final[b_rows, :] = total(g[z, y, b_rows, :], got)
            if na:
                got = [recv["a3"][slot, a_in, :] for slot in range(self.zs - 1)]
                self.final[a_rows, :] = total(g[z, y, a_rows, :], got)

    def small_copies(self, k, axis, held, got):
        most = max(self.sizes) - 1
        base = len(self.groups) * sum(map(sum, self.counts(self.sizes)))
        made = []
        for slot, other, to in self.peers(axis):
            index = base + (k * 4 + axis) * most + slot
            made.append(
                pltpu.make_async_remote_copy(
                    src_ref=held.at[axis],
                    dst_ref=got.at[self.got_first(axis) + slot],
                    send_sem=self.send_sems.at[index],
                    recv_sem=self.recv_sems.at[index],
                    device_id=to,
                    device_id_type=MESH,
                )
            )
        return made

    def got_first(self, axis):
        return sum(size - 1 for size in self.sizes[:axis])

    def small_send(self, k, axis, held, got):
        self.small.append((k, axis, held, got))
        for copy in self.small_copies(k, axis, held, got):
            copy.start()

    def small_add(self, k, axis, held, got):
        for copy in self.small_copies(k, axis, held, got):
            copy.wait_recv()
        size, me = self.sizes[axis], self.place[axis]
        total = None
        for n in range(size):
            value = held[axis]
            for slot in range(size - 1):
                value = jnp.where(lax.rem(me - slot - 1 + size, size) == n, got[self.got_first(axis) + slot], value)
            total = value if total is None else total + value
        held[axis - 1 if axis else 4] = total

    def small_next(self, k, axis, held, got):
        self.small_add(k, axis, held, got)
        if axis:
            self.small_send(k, axis - 1, held, got)

    def finish(self):
        for i in range(len(self.groups)):
            for stage in range(self.STAGES):
                for copy in self.copies(stage, i):
                    copy.wait_send()
        for small in self.small:
            for copy in self.small_copies(*small):
                copy.wait_send()


def recv_shapes(grid, xs, groups, height):
    zs, ys = grid
    na = sum(split_of(size, xs)[1] for _, size in groups) // xs
    nb = sum(split_of(size, xs)[2] for _, size in groups)
    na = max(na, 16)
    return {
        "core": (zs, ys, max(groups[3][0], height - groups[3][0]) // 2, 256),
        "a1": (xs - 1, zs, ys, na, 256),
        "b1": (ys - 1, zs, nb, 256),
        "a2": (ys - 1, zs, na, 256),
        "b2": (zs - 1, nb, 256),
        "a3": (zs - 1, na, 256),
        "b3": (xs - 1, nb, 256),
    }


SMALL = 16


def last_kernel(share, wide_share, final_ref, early_ref, late_ref, xgrad_in, cell_in, *refs):
    xgrad_out, cell_out, norms, wide_gain, glu, left, conv, depth, point, qkv, out, up, down = refs
    xgrad_out[...] = xgrad_in[...]
    cell_out[...] = cell_in[...]
    starts, _, _ = offsets(share, wide_share)
    depth[...] = early_ref[0:9, :]
    wide_gain[...] = early_ref[9:10, :]
    norms[0:2, :] = late_ref[0:2, :]
    norms[2:4, :] = early_ref[10:12, 0:D]
    for name, ref, tiles, size in (
        ("glu", glu, 4, share),
        ("left", left, 8, share),
        ("point", point, 1, wide_share),
        ("qkv", qkv, 6, share),
        ("out", out, 2, share),
        ("up", up, 8, share),
        ("down", down, 2, wide_share),
    ):
        for n in range(tiles):
            part, k = name, n
            if name in ("left", "glu") and n >= tiles // 2:
                part, k = ("left2" if name == "left" else "glu1"), n - tiles // 2
            first = starts[part] + k * size
            ref[:, 256 * n : 256 * n + 256] = final_ref[first : first + size, :].astype(f32)
    for k in range(3):
        first = starts["conv"] + k * share
        conv[k] = final_ref[first : first + share, :].astype(f32)


def local(
    grid,
    xs,
    cell_input,
    lengths,
    pair_ids,
    cotangent,
    norm_gains,
    wide_gain,
    w_glu,
    w_left,
    w_conv3,
    w_depth,
    w_point,
    w_qkv,
    w_out,
    w_up,
    w_down,
):
    zs, ys = grid
    dp = zs * ys
    share, wide_share = 512 // dp, 2048 // dp
    rows = cell_input.shape[0]
    sents = lengths.shape[0]
    starts, groups, height = offsets(share, wide_share)
    wg = wide_gain.reshape(FF // 128, 128)
    shape = jax.ShapeDtypeStruct
    params = pltpu.CompilerParams(vmem_limit_bytes=62 << 20)
    kept = kept_shapes(sents)
    anywhere = pl.BlockSpec(memory_space=pl.ANY)
    most = zs + ys + xs - 2
    counting = Sums.semaphores(grid, xs, ())
    front = pl.pallas_call(
        functools.partial(front_kernel, sents, grid, xs),
        out_shape=[shape((rows, D), bf)] + list(kept.values()),
        in_specs=[smem(), smem(), vmem(), anywhere] + [vmem()] * 2 + [anywhere] * 3 + [vmem()] + [anywhere] * 5,
        out_specs=[anywhere] * (1 + len(kept)),
        scratch_shapes=[pltpu.VMEM(v, bf) for v in (*WEIGHTS, (rows, D))]
        + [pltpu.SemaphoreType.DMA((9,)), pltpu.VMEM((rows, D), bf)]
        + [pltpu.VMEM(v.shape, v.dtype) for v in kept.values()]
        + [
            pltpu.SemaphoreType.DMA((len(kept) + 1, sents)),
            pltpu.VMEM((16, FF), f32),
            pltpu.VMEM((SEQ, D), f32),
            pltpu.VMEM((PAD, D), f32),
            pltpu.VMEM((SEQ, FF), f32),
            pltpu.VMEM((SEQ, HALF), f32),
            pltpu.VMEM((SEQ, 3 * D), bf),
            pltpu.SemaphoreType.DMA((counting,)),
            pltpu.SemaphoreType.DMA((counting,)),
            pltpu.VMEM((5, 8, 128), f32),
            pltpu.VMEM((most, 8, 128), f32),
            pltpu.VMEM((sents, 8, 128), f32),
        ],
        compiler_params=pltpu.CompilerParams(vmem_limit_bytes=62 << 20, collective_id=1, has_side_effects=True),
        name="front",
    )(lengths, pair_ids, cell_input, cotangent, norm_gains, wg, w_glu, w_left, w_conv3, w_depth, w_point, w_qkv, w_out, w_up, w_down)
    cell, arrays = front[0], front[1:]
    recv = recv_shapes(grid, xs, groups, height)
    semaphores = Sums.semaphores(grid, xs, groups)
    input_grad, final, early, late = pl.pallas_call(
        functools.partial(back_kernel, sents, grid, xs, tuple(recv)),
        out_shape=[shape((rows, D), f32), shape((height, 256), bf), shape((SMALL, FF), f32), shape((8, D), f32)],
        in_specs=[vmem()] * 2 + [anywhere] * 3 + [vmem()] + [anywhere] * (2 + len(kept)),
        out_specs=[anywhere] * 4,
        scratch_shapes=[pltpu.VMEM(v, bf) for v in (*recv.values(), *WEIGHTS[:5])]
        + [
            pltpu.SemaphoreType.DMA((32,)),
            pltpu.SemaphoreType.DMA((semaphores,)),
            pltpu.SemaphoreType.DMA((semaphores,)),
            pltpu.VMEM((zs, ys, height, 256), bf),
            pltpu.VMEM((height, 256), bf),
            pltpu.VMEM((5, SMALL, FF), f32),
            pltpu.VMEM((most, SMALL, FF), f32),
            pltpu.VMEM((5, 8, D), f32),
            pltpu.VMEM((most, 8, D), f32),
            pltpu.VMEM((rows, FF), bf),
            pltpu.VMEM((rows, FF), bf),
            pltpu.VMEM((rows, 3 * D), bf),
            pltpu.VMEM((sents, HEADS, SEQ, SEQ), bf),
            pltpu.VMEM((rows, D), f32),
            pltpu.VMEM((rows, D), bf),
            pltpu.VMEM((rows, D), bf),
            pltpu.VMEM((rows, D), bf),
            pltpu.VMEM((D, rows), bf),
            pltpu.VMEM((D, rows), bf),
            pltpu.VMEM((3 * D, rows), bf),
            pltpu.VMEM((rows, HALF), bf),
            pltpu.VMEM((rows, 8), f32),
            pltpu.VMEM((sents * 8, D), f32),
            pltpu.VMEM((2, 16, PAD, 128), f32),
            pltpu.VMEM((16, FF), f32),
            pltpu.VMEM((3 * D, SEQ), bf),
            pltpu.VMEM((16, PAD, 128), f32),
            pltpu.VMEM((SEQ, FF), f32),
            pltpu.VMEM((9, 8, FF), f32),
            pltpu.VMEM((SEQ, 128), f32),
            pltpu.VMEM((SEQ, 128), f32),
            pltpu.VMEM((PAD, HALF), f32),
            pltpu.VMEM((32, D), f32),
        ],
        compiler_params=pltpu.CompilerParams(vmem_limit_bytes=63 << 20, collective_id=0, has_side_effects=True),
        name="back",
    )(norm_gains, wg, w_glu, w_left, w_conv3, w_depth, w_point, w_qkv, *arrays)
    input_grad, cell_output, norms, gain, glu, left, conv, depth, point, qkv, out, up, down = pl.pallas_call(
        functools.partial(last_kernel, share, wide_share),
        out_shape=[
            shape((rows, D), f32),
            shape((rows, D), bf),
            shape((4, D), f32),
            shape((1, FF), f32),
            shape((share, 2 * D), f32),
            shape((share, FF), f32),
            shape((3, share, HALF), f32),
            shape((9, FF), f32),
            shape((wide_share, HALF), f32),
            shape((share, 3 * D), f32),
            shape((share, D), f32),
            shape((share, FF), f32),
            shape((wide_share, D), f32),
        ],
        in_specs=[vmem()] * 5,
        out_specs=[vmem()] * 13,
        compiler_params=params,
        name="last",
    )(final, early, late, input_grad, cell)
    return cell_output, input_grad, norms, gain.reshape(FF), glu, left, conv, depth, point, qkv, out, up, down


def solution(mesh):
    dp, head = mesh.shape["dp"], mesh.shape["head"]
    ys = 2 ** ((dp.bit_length() - 1) // 2)
    grid = (dp // ys, ys)
    xs = head // 2
    row = P(("dp", "head"), None)
    in_specs = (row, P(("dp", "head")), P(("dp", "head")), row) + (P(),) * 11
    share = P("dp", None)
    out_specs = (row, row, P(), P(), share, share, P(None, "dp", None), P(), share, share, share, share, share)
    return jax.shard_map(
        functools.partial(local, grid, xs), mesh=mesh, in_specs=in_specs, out_specs=out_specs, check_vma=False
    )
```

```python
import functools

import jax
import jax.numpy as jnp
from jax import lax
from jax.experimental import pallas as pl
from jax.experimental.pallas import tpu as pltpu
from jax.sharding import PartitionSpec as P

HEADS = 8
DH = 64
SEQ = 256
PAIRS = 4
D = 512
FF = 2048
HALF = 256
PAD = SEQ + 16
EPS = 1e-05
MESH = pl.DeviceIdType.MESH
bf = jnp.bfloat16
f32 = jnp.float32
GELU_A = 0.7978845608028654
GELU_B = 0.7978845608028654 * 0.044715
CH = 32


def nn(a, b):
    return lax.dot_general(a, b, (((1,), (0,)), ((), ())), preferred_element_type=f32)


def nt(a, b):
    return lax.dot_general(a, b, (((1,), (1,)), ((), ())), preferred_element_type=f32)


def tn(a, b):
    return lax.dot_general(a, b, (((0,), (0,)), ((), ())), preferred_element_type=f32)


def gelu_both(v):
    square = v * v
    t = jnp.tanh(v * (GELU_A + GELU_B * square))
    half = 0.5 + 0.5 * t
    slope = half + (0.5 * v) * (1.0 - t * t) * (GELU_A + (3.0 * GELU_B) * square)
    return v * half, slope


def sigmoid(v):
    return 0.5 + 0.5 * jnp.tanh(0.5 * v)


def fold8(v):
    total = v[0:8]
    for i in range(1, v.shape[0] // 8):
        total = total + v[8 * i : 8 * i + 8]
    return total


def norm(v):
    centred = v - jnp.mean(v, axis=-1, keepdims=True)
    rstd = lax.rsqrt(jnp.mean(centred * centred, axis=-1, keepdims=True) + EPS)
    return centred, rstd


def norm_back(g, low, gain, inverse, rstd):
    gy = g * gain
    m1 = jnp.mean(gy, axis=-1, keepdims=True)
    m2 = jnp.mean(g * low, axis=-1, keepdims=True)
    return rstd * (gy - m1 - (low * inverse) * m2)


def at(s, first, size):
    return pl.ds(pl.multiple_of(s * SEQ + first, size), size)


def one_row(ref):
    return jnp.concatenate([ref[j : j + 1, :] for j in range(ref.shape[0])], axis=1).astype(f32)


def row_of(first, size):
    return first + lax.broadcasted_iota(jnp.int32, (size, 1), 0)


KEPT = (
    "a", "b", "e", "f", "rstd", "sig", "u", "dgl", "dgr", "m",
    "depth", "qkvt", "pt", "mixt", "up", "gup", "ga", "gmixt", "gain_f", "gl",
)


def kept_shapes(sents):
    rows = sents * SEQ
    shape = jax.ShapeDtypeStruct
    return {
        "a": shape((rows, D), bf),
        "b": shape((rows, D), bf),
        "e": shape((rows, D), bf),
        "f": shape((rows, D), bf),
        "rstd": shape((rows, 8), f32),
        "sig": shape((rows, D), bf),
        "u": shape((rows, D), bf),
        "dgl": shape((rows, FF), bf),
        "dgr": shape((rows, HALF), bf),
        "m": shape((sents, 16, PAD, 128), f32),
        "depth": shape((8, sents, SEQ, 256), bf),
        "qkvt": shape((3 * D, rows), bf),
        "pt": shape((sents, HEADS, SEQ, SEQ), bf),
        "mixt": shape((D, rows), bf),
        "up": shape((rows, FF), bf),
        "gup": shape((rows, FF), bf),
        "ga": shape((rows, D), f32),
        "gmixt": shape((D, rows), bf),
        "gain_f": shape((sents * 8, D), f32),
        "gl": shape((rows, D), bf),
    }


def part_of(name, s):
    if name in ("m", "pt"):
        return (s,)
    if name == "depth":
        return (slice(None), s)
    if name in ("qkvt", "mixt", "gmixt"):
        return (slice(None), pl.ds(pl.multiple_of(s * SEQ, SEQ), SEQ))
    if name == "gain_f":
        return (pl.ds(pl.multiple_of(s * 8, 8), 8),)
    return (pl.ds(pl.multiple_of(s * SEQ, SEQ), SEQ),)


WEIGHTS = ((D, 2 * D), (D, FF), (3, D, HALF), (FF, HALF), (D, 3 * D), (D, D), (D, FF), (FF, D))


def front_kernel(
    sents,
    grid,
    xs,
    len_ref,
    pair_ref,
    x_ref,
    cot_ref,
    gains_ref,
    wg_ref,
    wglu,
    wleft,
    wconv,
    wdepth,
    wpoint,
    wqkv,
    wout,
    wup,
    wdown,
    out_far,
    *refs,
):
    far, refs = dict(zip(KEPT, refs)), refs[len(KEPT) :]
    held, refs = refs[: len(WEIGHTS) + 1], refs[len(WEIGHTS) + 1 :]
    weights = (wglu, wleft, wconv, wpoint, wqkv, wout, wup, wdown, cot_ref)
    load_sems, out_ref, refs = refs[0], refs[1], refs[2:]
    load = [pltpu.make_async_copy(w, h, load_sems.at[k]) for k, (w, h) in enumerate(zip(weights, held))]
    for copy in load[:3]:
        copy.start()
    wglu, wleft, wconv, wpoint, wqkv, wout, wup, wdown, cot_ref = held
    near, refs = dict(zip(KEPT, refs)), refs[len(KEPT) :]
    ship_sems, wp_ref, xf_ref, bs_ref, wide_ref, sep_ref, qkv_ref = refs[:7]
    send_sems, recv_sems, count_ref, count_got, fac_ref = refs[7:]
    sums = Sums(grid, xs, (), None, None, None, send_sems, recv_sems)
    sums.greet(False)
    lane = lax.broadcasted_iota(jnp.int32, (8, 128), 1)
    counts = jnp.zeros((8, 128), f32)
    for s in range(sents):
        counts = counts + jnp.where(lane == pair_ref[s], len_ref[s].astype(f32), 0.0)
    count_ref[3] = counts
    sums.small_send(0, 3, count_ref, count_got)

    def count_next(axis):
        sums.small_add(0, axis, count_ref, count_got)
        if axis:
            for copy in sums.small_copies(0, axis - 1, count_ref, count_got):
                copy.start()
        else:
            counts = count_ref[4]
            total = jnp.sum(counts, axis=1, keepdims=True)
            for k in range(sents):
                mine = jnp.sum(jnp.where(lane == pair_ref[k], counts, 0.0), axis=1, keepdims=True)
                fac_ref[k] = jnp.broadcast_to(total / (PAIRS * mine), (8, 128))

    (a_ref, b_ref, e_ref, f_ref, rstd_ref, sig_ref, u_ref, dgl_ref, dgr_ref, m_ref) = [near[n] for n in KEPT[:10]]
    (depth_ref, qkvt_ref, pt_ref, mixt_ref, up_ref, gup_ref, ga_ref, gmixt_ref, gain_f_ref, gl_ref) = [near[n] for n in KEPT[10:]]

    def shipment(name, s):
        k = KEPT.index(name)
        where = part_of(name, s)
        return pltpu.make_async_copy(near[name].at[where], far[name].at[where], ship_sems.at[k, s])

    def leave(s):
        return pltpu.make_async_copy(out_ref.at[at(s, 0, SEQ), :], out_far.at[at(s, 0, SEQ), :], ship_sems.at[len(KEPT), s])

    def ship(s, *names):
        for name in names:
            shipment(name, s).start()

    wp_ref[0:9, :] = wdepth[...].astype(f32) * one_row(wg_ref)
    gain_f_ref[...] = jnp.zeros_like(gain_f_ref)
    zero8 = jnp.zeros((8, 128), f32)

    def sentence(s, carry):
        length = len_ref[s]

        def loaded(*which, then=(), axis=None):
            @pl.when(s == 0)
            def _():
                for k in which:
                    load[k].wait()
                for k in then:
                    load[k].start()
                if axis is not None:
                    count_next(axis)

        gains = gains_ref[...].astype(f32)
        rows = at(s, 0, SEQ)
        for c in range(0, SEQ, CH):
            cen, rstd = norm(x_ref[at(s, c, CH), :].astype(f32))
            a_ref[at(s, c, CH), :] = (cen * rstd * gains[0:1]).astype(bf)
            rstd_ref[at(s, c, CH), 0:1] = rstd
        a_low = a_ref[rows, :]
        loaded(0, then=(3, 4))
        for n in range(2):
            cols = slice(256 * n, 256 * n + 256)
            gcols = slice(512 + 256 * n, 768 + 256 * n)
            value = nn(a_low, wglu[:, cols])
            gate = nn(a_low, wglu[:, gcols])
            for c in range(0, SEQ, CH):
                sig = sigmoid(gate[c : c + CH])
                mixed = value[c : c + CH] * sig
                xf_ref[c : c + CH, cols] = x_ref[at(s, c, CH), cols].astype(f32) + mixed
                sig_ref[at(s, c, CH), cols] = sig.astype(bf)
                u_ref[at(s, c, CH), cols] = (mixed * (1.0 - sig)).astype(bf)
        ship(s, "a", "sig", "u")
        for c in range(0, SEQ, CH):
            cen, rstd = norm(xf_ref[c : c + CH, :])
            rstd = jnp.where(row_of(c, CH) < length, rstd, 0.0)
            b_low = cen * rstd * gains[1:2]
            b_ref[at(s, c, CH), :] = b_low.astype(bf)
            rstd_ref[at(s, c, CH), 1:2] = rstd
            bs_ref[8 + c : 8 + c + CH, :] = b_low
        b_low = b_ref[rows, :]
        bs_ref[0:8, :] = jnp.zeros((8, D), f32)
        bs_ref[8 + SEQ : 16 + SEQ, :] = jnp.zeros((8, D), f32)
        loaded(1, 2, then=(5, 6, 7, 8), axis=3)
        right = (
            nn(bs_ref[7 : 7 + SEQ, :].astype(bf), wconv[0])
            + nn(b_low, wconv[1])
            + nn(bs_ref[9 : 9 + SEQ, :].astype(bf), wconv[2])
        )
        for n in range(8):
            cols = slice(256 * n, 256 * n + 256)
            left = nn(b_low, wleft[:, cols])
            for c in range(0, SEQ, CH):
                hidden, slope = gelu_both(left[c : c + CH])
                dgl_ref[at(s, c, CH), cols] = slope.astype(bf)
                if n == 0:
                    extra, slope = gelu_both(right[c : c + CH])
                    dgr_ref[at(s, c, CH), :] = slope.astype(bf)
                    hidden = hidden + extra
                wide_ref[c : c + CH, cols] = hidden
        ship(s, "b", "dgl", "dgr")
        for j in range(16):
            m_ref[s, j, 0:8, :] = zero8
            m_ref[s, j, 8 + SEQ : PAD, :] = zero8
        for c in range(0, SEQ, 8):
            mean = jnp.mean(wide_ref[c : c + 8, :], axis=-1, keepdims=True)
            cen = wide_ref[c : c + 8, :] - mean
            rstd = lax.rsqrt(jnp.mean(cen * cen, axis=-1, keepdims=True) + EPS)
            rstd = jnp.where(row_of(c, 8) < length, rstd, 0.0)
            rstd_ref[at(s, c, 8), 2:3] = rstd
            for j in range(16):
                m_ref[s, j, 8 + c : 16 + c, :] = cen[:, 128 * j : 128 * j + 128] * rstd
        for j in range(16):
            cols = slice(128 * j, 128 * j + 128)
            taps = [wp_ref[o : o + 1, cols] for o in range(9)]
            for c in range(0, SEQ, CH):
                total = m_ref[s, j, c + 4 : c + 4 + CH, :] * taps[0]
                for o in range(1, 9):
                    total = total + m_ref[s, j, c + 4 + o : c + 4 + o + CH, :] * taps[o]
                depth_ref[j // 2, s, c : c + CH, 128 * (j % 2) : 128 * (j % 2) + 128] = total.astype(bf)
        ship(s, "m", "depth")
        loaded(3, axis=2)
        depth = jnp.concatenate([depth_ref[n, s] for n in range(8)], axis=1)
        sep_ref[...] = nn(depth, wpoint[...])
        for c in range(0, SEQ, CH):
            conv = xf_ref[c : c + CH, :]
            conv = jnp.concatenate([conv[:, :HALF] + sep_ref[c : c + CH, :], conv[:, HALF:]], axis=1)
            xf_ref[c : c + CH, :] = conv
            cen, rstd = norm(conv)
            e_ref[at(s, c, CH), :] = (cen * rstd * gains[2:3]).astype(bf)
            rstd_ref[at(s, c, CH), 3:4] = rstd
        e_low = e_ref[rows, :]
        loaded(4)
        for n in range(6):
            cols = slice(256 * n, 256 * n + 256)
            part = nn(e_low, wqkv[:, cols]).astype(bf)
            qkv_ref[:, cols] = part
            qkvt_ref[cols, at(s, 0, SEQ)] = part.T
        ship(s, "e", "qkvt")
        bias = jnp.where(row_of(0, SEQ) < jnp.maximum(length, 1), 0.0, -1e30)
        for h in range(HEADS):
            base = 3 * DH * h
            key = qkv_ref[:, base + DH : base + 2 * DH] * jnp.asarray(DH**-0.5, bf)
            query_t = qkvt_ref[base : base + DH, at(s, 0, SEQ)]
            value_t = qkvt_ref[base + 2 * DH : base + 3 * DH, at(s, 0, SEQ)]
            for q in range(0, SEQ, 128):
                scores = nn(key, query_t[:, q : q + 128]) + bias
                scores = jnp.exp(scores - jnp.max(scores, axis=0, keepdims=True))
                scores = scores * (1.0 / jnp.sum(scores, axis=0, keepdims=True))
                pt_ref[s, h, :, q : q + 128] = scores.astype(bf)
            mixt_ref[DH * h : DH * h + DH, at(s, 0, SEQ)] = nn(value_t, pt_ref[s, h]).astype(bf)
        ship(s, "pt", "mixt")
        loaded(5, axis=1)
        for n in range(2):
            cols = slice(256 * n, 256 * n + 256)
            xf_ref[:, cols] += tn(mixt_ref[:, at(s, 0, SEQ)], wout[:, cols])
        for c in range(0, SEQ, CH):
            cen, rstd = norm(xf_ref[c : c + CH, :])
            f_ref[at(s, c, CH), :] = (cen * rstd * gains[3:4]).astype(bf)
            rstd_ref[at(s, c, CH), 4:5] = rstd
        f_low = f_ref[rows, :]
        loaded(6)
        for n in range(8):
            cols = slice(256 * n, 256 * n + 256)
            up = nn(f_low, wup[:, cols])
            for c in range(0, SEQ, CH):
                low, slope = gelu_both(up[c : c + CH])
                up_ref[at(s, c, CH), cols] = low.astype(bf)
                gup_ref[at(s, c, CH), cols] = slope.astype(bf)
        loaded(7, 8, axis=0)
        for n in range(2):
            cols = slice(256 * n, 256 * n + 256)
            down = nn(up_ref[rows, :], wdown[:, cols])
            out_ref[rows, cols] = (xf_ref[:, cols] + down).astype(bf)
        ship(s, "f", "rstd", "up")
        leave(s).start()
        for c in range(0, SEQ, CH):
            weight = jnp.where(row_of(c, CH) < length, fac_ref[s, 0:1, 0:1], 0.0)
            g_out = cot_ref[at(s, c, CH), :].astype(f32) * weight
            ga_ref[at(s, c, CH), :] = g_out
            gl_ref[at(s, c, CH), :] = g_out.astype(bf)
        g_low = gl_ref[rows, :]
        for n in range(8):
            cols = slice(256 * n, 256 * n + 256)
            back = nt(g_low, wdown[cols, :])
            gup_ref[rows, cols] = (back * gup_ref[rows, cols].astype(f32)).astype(bf)
        ship(s, "gup", "gl")
        for n in range(2):
            cols = slice(256 * n, 256 * n + 256)
            wide_ref[:, cols] = nt(gup_ref[rows, :], wup[cols, :])
        inverse = 1.0 / gains[3:4]
        for c in range(0, SEQ, CH):
            g_f = wide_ref[c : c + CH, 0:D]
            low = f_ref[at(s, c, CH), :].astype(f32)
            gain_f_ref[pl.ds(pl.multiple_of(s * 8, 8), 8), :] += fold8(g_f * low)
            back = norm_back(g_f, low, gains[3:4], inverse, rstd_ref[at(s, c, CH), 4:5])
            ga_ref[at(s, c, CH), :] += back
        gmixt_ref[:, at(s, 0, SEQ)] = nt(wout[...], ga_ref[rows, :].astype(bf)).astype(bf)
        ship(s, "ga", "gmixt", "gain_f")
        return carry

    lax.fori_loop(0, sents, sentence, 0)

    def landed(s, carry):
        for name in KEPT:
            shipment(name, s).wait()
        leave(s).wait()
        return carry

    lax.fori_loop(0, sents, landed, 0)
    for axis in range(4):
        for copy in sums.small_copies(0, axis, count_ref, count_got):
            copy.wait_send()


def vmem():
    return pl.BlockSpec(memory_space=pltpu.VMEM)


def smem():
    return pl.BlockSpec(memory_space=pltpu.SMEM)


def offsets(share, wide_share):
    sizes = (
        ("up", 8 * share, True),
        ("down", 2 * wide_share, True),
        ("out", 2 * share, False),
        ("qkv", 6 * share, True),
        ("point", wide_share, True),
        ("left", 4 * share, True),
        ("left2", 4 * share, True),
        ("conv", 3 * share, True),
        ("glu", 2 * share, True),
        ("glu1", 2 * share, True),
    )
    first, starts, groups, begin = 0, {}, [], 0
    for name, size, ends in sizes:
        starts[name] = first
        first += size
        if ends:
            first = -(-first // 32) * 32
            groups.append((begin, first - begin))
            begin = first
    return starts, groups, first


def put(g_ref, grid, tile, first, share, wide, chunk=0):
    _, ys = grid
    for part in range(tile.shape[1] // 256):
        for k in range(512 // share):
            block = chunk * (512 // share) + k
            piece = tile[k * share : (k + 1) * share, 256 * part : 256 * part + 256]
            rows = pl.ds(pl.multiple_of(first + part * share, 16), share)
            g_ref[block // ys, block % ys, rows, :] = piece.astype(bf)


SCHEDULE = {
    "u3": (0,),
    "d3": (1,),
    "o": (0,),
    "a1a": (1,),
    "q0": (0,),
    "q2": (2,),
    "p1": (1,),
    "p2": (2,),
    "p3": (3,),
    "w0b": (0, 3,),
    "w1b": (1,),
    "w1c": (0,),
    "w2a": (2,),
    "w2b": (3, 1,),
    "w2c": (0,),
    "l1": (4, 1,),
    "l3": (5, 2,),
    "c": (6, 4,),
    "t": (5, 3,),
    "i0": (6, -1,),
    "i1": (2,),
    "i2": (4,),
    "g0": (7,),
    "g1": (8, 5,),
    "e0": (3, 7,),
    "e1": (8, -1, 6,),
    "e2": (4, 2, 3,),
    "z": (5, -2, 7, 8, -1, -2, 4, 6, 5, -2, 4, 7, 5, 8, -1, 6, -2, -1, 7, 6, 8, 7, 8,),
}


def back_kernel(
    sents,
    grid,
    xs,
    names,
    gains_ref,
    wg_ref,
    wglu_far,
    wleft_far,
    wconv_far,
    wdepth,
    wpoint_far,
    wqkv_far,
    *refs,
):
    far, refs = dict(zip(KEPT, refs)), refs[len(KEPT) :]
    xgrad_far, final_far, early_far, late_far = refs[:4]
    recv, refs = dict(zip(names, refs[4:])), refs[4 + len(names) :]
    (wglu, wleft, wconv, wpoint, wqkv), refs = refs[:5], refs[5:]
    (
        fetch_sems,
        send_sems,
        recv_sems,
        g_ref,
        final_ref,
        early_ref,
        early_got,
        late_ref,
        late_got,
        first_wide,
        second_wide,
        gqkv_ref,
        squares,
        conv_ref,
        gl_ref,
        fs_ref,
        gas_ref,
        mixt_ref,
        gmixt_ref,
        qkvt_ref,
        dgr_ref,
        rstd_ref,
        gain_f_ref,
        m_ref,
        wp_ref,
        gqkvt_ref,
        gd_ref,
        wide_ref,
        taps_ref,
        s1_ref,
        s2_ref,
        right_ref,
        gain_ref,
    ) = refs
    e_ref = gas_ref
    gr_refs = (gl_ref.at[:, 0:HALF], gl_ref.at[:, HALF:D], fs_ref.at[:, 0:HALF])
    sep_ref = fs_ref.at[:, HALF:D]
    up_ref = gleft_ref = dgl_ref = first_wide
    gup_ref = second_wide
    a_ref, b_ref, sig_ref, u_ref = [second_wide.at[:, D * k : D * k + D] for k in range(4)]
    gg_ref = gqkv_ref
    pt_ref, depth_view = squares, squares.reshape(8, sents, SEQ, 256)
    where = dict(
        a=a_ref, b=b_ref, e=e_ref, f=fs_ref, rstd=rstd_ref, sig=sig_ref, u=u_ref, dgl=first_wide, dgr=dgr_ref,
        qkvt=qkvt_ref, mixt=mixt_ref, up=first_wide, gup=second_wide, ga=conv_ref, gmixt=gmixt_ref, gain_f=gain_f_ref,
        pt=squares, depth=depth_view, gl=gl_ref, wglu=wglu, wleft=wleft, wconv=wconv, wpoint=wpoint, wqkv=wqkv,
    )
    far.update(wglu=wglu_far, wleft=wleft_far, wconv=wconv_far, wpoint=wpoint_far, wqkv=wqkv_far)
    order = (
        "gmixt", "qkvt", "pt", "f", "gup", "ga", "gl", "up", "gain_f", "rstd", "mixt", "wqkv", "wpoint", "dgr",
        "wleft", "wconv", "wglu", "e", "b", "a", "sig", "u", "dgl", "depth",
    )

    def fetch(name):
        return pltpu.make_async_copy(far[name], where[name], fetch_sems.at[order.index(name)])

    def start(*names):
        for name in names:
            fetch(name).start()

    def wait(*names):
        for name in names:
            fetch(name).wait()

    def fetch_m(s):
        return pltpu.make_async_copy(far["m"].at[s], m_ref.at[s % 2], fetch_sems.at[len(order) + s % 2])

    start("gup", "f", "up", "gl", "ga", "mixt", "rstd", "gain_f")
    share, wide_share = 512 // (grid[0] * grid[1]), 2048 // (grid[0] * grid[1])
    starts, groups, _ = offsets(share, wide_share)
    sums = Sums(grid, xs, groups, g_ref, final_ref, recv, send_sems, recv_sems)
    sums.greet()
    small_step = {-1: 4, -2: 3}

    def claim(name):
        steps = []
        for i in SCHEDULE.get(name, ()):
            if i >= 0:
                steps += sums.claim(i)
            elif small_step[i] >= 0:
                steps.append((i, small_step[i]))
                small_step[i] -= 1
        return steps

    def do(steps):
        for i, stage in steps:
            if i >= 0:
                sums.do([(i, stage)])
            elif i == -1:
                sums.early_next(stage, early_ref, early_got)
            else:
                sums.small_next(2, stage, late_ref, late_got)

    def point(name):
        do(claim(name))

    def loop(name, first, last, body, parts=""):
        claims = {(k, part): claim(f"{name}{k}{part}") for k in range(first, last) for part in parts or ("",)}

        def within(k, part):
            for n in range(first, last):
                if claims[n, part]:
                    pl.when(k == n)(functools.partial(do, claims[n, part]))

        def round(k, carry):
            body(k, within)
            if not parts:
                within(k, "")
            return carry

        lax.fori_loop(first, last, round, 0)

    wp_ref[0:9, :] = wdepth[...].astype(f32) * one_row(wg_ref)
    gain_ref[...] = jnp.zeros_like(gain_ref)
    taps_ref[...] = jnp.zeros_like(taps_ref)

    def wide_tile(i):
        return pl.ds(pl.multiple_of(i * 512, 512), 512)

    wait("f", "gup")

    def grad_up(i, within):
        tile = tn(fs_ref[...], gup_ref[:, wide_tile(i)])
        put(g_ref, grid, tile, starts["up"] + i * 2 * share, share, False)

    loop("u", 0, 4, grad_up)
    wait("up", "gl")
    start("gmixt", "qkvt", "pt", "b", "a", "sig", "u")

    def grad_down(i, within):
        put(g_ref, grid, tn(up_ref[:, wide_tile(i)], gl_ref[...]), starts["down"], wide_share, True, i)

    loop("d", 0, 4, grad_down)
    wait("ga", "mixt", "rstd", "gain_f")
    start("dgl", "wqkv")
    for c in range(0, sents * SEQ, CH):
        gas_ref[c : c + CH, :] = conv_ref[c : c + CH, :].astype(bf)
    put(g_ref, grid, nn(mixt_ref[...], gas_ref[...]), starts["out"], share, False)
    start("e", "wpoint", "dgr")
    point("o")

    for s in range(sents):
        gain_ref[24:32, :] += gain_f_ref[8 * s : 8 * s + 8, :]
    wait("gmixt", "qkvt", "pt")

    def attend(s, within):
        rows = at(s, 0, SEQ)
        for h in range(HEADS):
            base = 3 * DH * h
            g_o = gmixt_ref[DH * h : DH * h + DH, rows]
            query_t = qkvt_ref[base : base + DH, rows]
            key_t = qkvt_ref[base + DH : base + 2 * DH, rows]
            value = qkvt_ref[base + 2 * DH : base + 3 * DH, rows].T
            probs = pt_ref[s, h]
            halves = []
            for q in range(0, SEQ, 128):
                part = probs[:, q : q + 128].astype(f32)
                back = nn(value, g_o[:, q : q + 128])
                both = part * back
                halves.append((both - part * jnp.sum(both, axis=0, keepdims=True)).astype(bf))
            g_scores = jnp.concatenate(halves, axis=1)
            gqkvt_ref[base : base + DH, :] = (nn(key_t, g_scores) * DH**-0.5).astype(bf)
            gqkvt_ref[base + DH : base + 2 * DH, :] = (nt(query_t, g_scores) * DH**-0.5).astype(bf)
            gqkvt_ref[base + 2 * DH : base + 3 * DH, :] = nt(g_o, probs).astype(bf)
            if h % 4 == 3:
                within(s, "ab"[h // 4])
        for n in range(6):
            cols = slice(256 * n, 256 * n + 256)
            gqkv_ref[rows, cols] = gqkvt_ref[cols, :].T

    loop("a", 0, sents, attend, "ab")
    start("depth")
    fetch_m(0).start()
    if sents > 1:
        fetch_m(1).start()
    wait("e")

    def grad_qkv(i, within):
        put(g_ref, grid, tn(e_ref[...], gqkv_ref[:, wide_tile(i)]), starts["qkv"] + i * 2 * share, share, False)

    loop("q", 0, 3, grad_qkv)

    def attention_input(s, within):
        gains = gains_ref[...].astype(f32)
        inverse = 1.0 / gains[2:3]
        rows = at(s, 0, SEQ)
        for n in range(2):
            cols = slice(256 * n, 256 * n + 256)
            wide_ref[:, cols] = nt(gqkv_ref[rows, :], wqkv[cols, :])
        for c in range(0, SEQ, CH):
            part = at(s, c, CH)
            g_e = wide_ref[c : c + CH, 0:D]
            low = e_ref[part, :].astype(f32)
            gain_ref[16:24, :] += fold8(g_e * low)
            g_conv = conv_ref[part, :] + norm_back(g_e, low, gains[2:3], inverse, rstd_ref[part, 3:4])
            conv_ref[part, :] = g_conv
            sep_ref[part, :] = g_conv[:, :HALF].astype(bf)

    wait("wqkv")
    loop("n", 0, sents, attention_input)
    wait("depth")

    def grad_point(i, within):
        depth = [depth_view[2 * i + k].reshape(sents * SEQ, 256) for k in range(2)]
        put(g_ref, grid, tn(jnp.concatenate(depth, axis=1), sep_ref[...]), starts["point"], wide_share, True, i)

    loop("p", 0, 4, grad_point)
    start("wleft", "wconv", "wglu")
    wait("b", "a", "sig", "u", "dgr", "dgl", "wpoint")

    zero8 = jnp.zeros((8, 128), f32)

    def wide(s, within):
        rows = at(s, 0, SEQ)
        slot = s % 2
        fetch_m(s).wait()
        for n in range(8):
            back = nt(sep_ref[rows, :], wpoint[256 * n : 256 * n + 256, :])
            for k in range(2):
                gd_ref[2 * n + k, 8 : 8 + SEQ, :] = back[:, 128 * k : 128 * k + 128]
        within(s, "a")
        for j in range(16):
            gd_ref[j, 0:8, :] = zero8
            gd_ref[j, 8 + SEQ : PAD, :] = zero8
            cols = slice(128 * j, 128 * j + 128)
            taps = [wp_ref[o : o + 1, cols] for o in range(9)]
            lines = [taps_ref[o, :, cols] for o in range(9)]
            for c in range(0, SEQ, CH):
                total = gd_ref[j, c + 12 : c + 12 + CH, :] * taps[0]
                for o in range(1, 9):
                    total = total + gd_ref[j, c + 12 - o : c + 12 - o + CH, :] * taps[o]
                wide_ref[c : c + CH, cols] = total
                mine = m_ref[slot, j, c + 8 : c + 8 + CH, :]
                if j == 0:
                    s1_ref[c : c + CH, :] = total
                    s2_ref[c : c + CH, :] = total * mine
                else:
                    s1_ref[c : c + CH, :] += total
                    s2_ref[c : c + CH, :] += total * mine
                back = gd_ref[j, c + 8 : c + 8 + CH, :]
                for o in range(9):
                    lines[o] = lines[o] + fold8(m_ref[slot, j, c + 4 + o : c + 4 + o + CH, :] * back)
            for o in range(9):
                taps_ref[o, :, cols] = lines[o]
        within(s, "b")
        right_ref[0:8, :] = jnp.zeros((8, HALF), f32)
        right_ref[8 + SEQ : PAD, :] = jnp.zeros((8, HALF), f32)
        for c in range(0, SEQ, CH):
            part = at(s, c, CH)
            rstd = rstd_ref[part, 2:3]
            m1 = jnp.sum(s1_ref[c : c + CH, :], axis=-1, keepdims=True) * (rstd / FF)
            m2 = jnp.sum(s2_ref[c : c + CH, :], axis=-1, keepdims=True) * (rstd / FF)
            for j in range(16):
                cols = slice(128 * j, 128 * j + 128)
                g_h = wide_ref[c : c + CH, cols] * rstd - m1 - m_ref[slot, j, c + 8 : c + 8 + CH, :] * m2
                gleft_ref[part, cols] = (g_h * dgl_ref[part, cols].astype(f32)).astype(bf)
                if j < 2:
                    right_ref[8 + c : 8 + c + CH, cols] = g_h * dgr_ref[part, cols].astype(f32)

        @pl.when(s + 2 < sents)
        def _():
            fetch_m(s + 2).start()

        for k in range(3):
            gr_refs[k][rows, :] = right_ref[9 - k : 9 - k + SEQ, :].astype(bf)
        within(s, "c")

    loop("w", 0, sents, wide, "abc")
    for i in range(4):
        put(g_ref, grid, tn(b_ref[...], gleft_ref[:, 512 * i : 512 * i + 512]), starts[("left", "left2")[i // 2]] + i % 2 * 2 * share, share, False)
        point(f"l{i}")
    for k in range(3):
        put(g_ref, grid, tn(b_ref[...], gr_refs[k][...]), starts["conv"] + k * share, share, False)
    point("c")

    wide_gain = one_row(wg_ref)
    total = jnp.zeros((1, FF), f32)
    for o in range(9):
        lines = jnp.sum(taps_ref[o], axis=0, keepdims=True)
        total = total + lines * wdepth[o : o + 1, :].astype(f32)
        early_ref[0, o : o + 1, :] = lines * wide_gain
    early_ref[0, 9:10, :] = total
    early_ref[0, 10:16, :] = jnp.zeros((6, FF), f32)

    def gain_row(i):
        return jnp.sum(gain_ref[8 * i : 8 * i + 8, :], axis=0, keepdims=True) / gains_ref[i : i + 1, :].astype(f32)

    early_ref[0, 10:11, 0:D] = gain_row(2)
    early_ref[0, 11:12, 0:D] = gain_row(3)
    sums.early_next(5, early_ref, early_got)
    point("t")

    def inputs(s, within):
        gains = gains_ref[...].astype(f32)
        rows = at(s, 0, SEQ)
        for n in range(2):
            cols = slice(256 * n, 256 * n + 256)
            g_b = nt(gleft_ref[rows, :], wleft[cols, :])
            for k in range(3):
                g_b = g_b + nt(gr_refs[k][rows, :], wconv[k, cols, :])
            wide_ref[:, cols] = g_b
        inverse = 1.0 / gains[1:2]
        for c in range(0, SEQ, CH):
            part = at(s, c, CH)
            g_b = wide_ref[c : c + CH, 0:D]
            low = b_ref[part, :].astype(f32)
            gain_ref[8:16, :] += fold8(g_b * low)
            g_glu = conv_ref[part, :] + norm_back(g_b, low, gains[1:2], inverse, rstd_ref[part, 1:2])
            conv_ref[part, :] = g_glu
            gg_ref[part, 0:D] = (g_glu * sig_ref[part, :].astype(f32)).astype(bf)
            gg_ref[part, D : 2 * D] = (g_glu * u_ref[part, :].astype(f32)).astype(bf)

    def inputs_end(s, within):
        gains = gains_ref[...].astype(f32)
        rows = at(s, 0, SEQ)
        for n in range(2):
            cols = slice(256 * n, 256 * n + 256)
            wide_ref[:, cols] = nt(gg_ref[rows, 0 : 2 * D], wglu[cols, :])
        inverse = 1.0 / gains[0:1]
        for c in range(0, SEQ, CH):
            part = at(s, c, CH)
            g_a = wide_ref[c : c + CH, 0:D]
            low = a_ref[part, :].astype(f32)
            gain_ref[0:8, :] += fold8(g_a * low)
            conv_ref[part, :] += norm_back(g_a, low, gains[0:1], inverse, rstd_ref[part, 0:1])

    wait("wleft", "wconv", "wglu")
    loop("i", 0, sents, inputs)
    for i in range(2):
        put(g_ref, grid, tn(a_ref[...], gg_ref[:, 512 * i : 512 * i + 512]), starts[("glu", "glu1")[i]], share, False)
        point(f"g{i}")
    loop("e", 0, sents, inputs_end)
    leave = pltpu.make_async_copy(conv_ref, xgrad_far, fetch_sems.at[len(order) + 2])
    leave.start()
    late_ref[3] = jnp.zeros((8, D), f32)
    late_ref[3, 0:1, :] = gain_row(0)
    late_ref[3, 1:2, :] = gain_row(1)
    sums.small_send(2, 3, late_ref, late_got)
    point("z")
    for _ in range(sums.STAGES + 1):
        sums.advance(*range(len(groups)))
    for i in small_step:
        while small_step[i] >= 0:
            do([(i, small_step[i])])
            small_step[i] -= 1
    ends = (final_ref, final_far), (early_ref.at[2], early_far), (late_ref.at[4], late_far)
    ends = [pltpu.make_async_copy(*pair, fetch_sems.at[len(order) + 3 + k]) for k, pair in enumerate(ends)]
    for copy in ends:
        copy.start()
    sums.finish()
    sums.early_sent(early_ref, early_got)
    leave.wait()
    for copy in ends:
        copy.wait()


def coordinates(ys):
    dp, head = lax.axis_index("dp"), lax.axis_index("head")
    return dp // ys, dp % ys, head // 2, head % 2


def device(ys, z, y, x, c):
    return (z * ys + y, x * 2 + c)


def rows16(first, size):
    return pl.ds(pl.multiple_of(first, 16), size)


def split_of(size, xs):
    half = size // 2
    first = (half // (32 * xs)) * 16 * xs
    return half, first, half - first


class Sums:
    STAGES = 5

    def __init__(self, grid, xs, groups, g_ref, final_ref, recv, send_sems, recv_sems):
        self.zs, self.ys = grid
        self.xs = xs
        self.sizes = (*grid, xs, 2)
        self.groups = groups
        self.g, self.final = g_ref, final_ref
        self.recv = recv
        self.send_sems, self.recv_sems = send_sems, recv_sems
        self.place = coordinates(self.ys)
        self.stage = [-1] * len(groups)
        self.small = []

    def peers(self, axis):
        size = self.sizes[axis]
        for step in range(1, size):
            to = list(self.place)
            to[axis] = lax.rem(to[axis] + step, size)
            yield step - 1, to[axis], device(self.ys, *to)

    def heads(self):
        z, y, x, c = self.place
        for dx in range(self.xs):
            for dc in range(2):
                if dx or dc:
                    yield device(self.ys, z, y, lax.rem(x + dx, self.xs), lax.rem(c + dc, 2))

    def greet(self, heads=True):
        barrier = pltpu.get_barrier_semaphore()
        others = [to for axis in range(2 if heads else 4) for _, _, to in self.peers(axis)]
        others += self.heads() if heads else []
        for to in others:
            pl.semaphore_signal(barrier, inc=1, device_id=to, device_id_type=MESH)
        total = len(others)
        pl.semaphore_wait(barrier, total)

    def core_first(self, i):
        return (self.groups[i][0] - (self.groups[3][0] if i > 2 else 0)) // 2

    def a_first(self, i):
        return sum(split_of(size, self.xs)[1] // self.xs for _, size in self.groups[:i])

    def b_first(self, i):
        return sum(split_of(size, self.xs)[2] for _, size in self.groups[:i])

    def rows(self, i):
        first, size = self.groups[i]
        half, na, nb = split_of(size, self.xs)
        mine = first + self.place[3] * half
        return first, half, mine, na, na // self.xs, mine + na, nb

    def plan(self, stage, i):
        z, y, x, c = self.place
        first, half, mine, na, part, b_row, nb = self.rows(i)
        g, recv, final = self.g, self.recv, self.final
        a_in, b_in = pl.ds(self.a_first(i), part), pl.ds(self.b_first(i), nb)
        a_rows, b_rows = rows16(mine + x * part, part), rows16(b_row, nb)
        axis_a, axis_b = ((None, 3), (2, 1), (1, 0), (0, 2), (None, 3))[stage]
        copies_a, copies_b = [], []
        for slot, other, to in self.peers(axis_b) if axis_b is not None else ():
            if stage == 0:
                source = g.at[:, :, rows16(first + other * half, half), :]
                target = recv["core"].at[:, :, pl.ds(self.core_first(i), half), :]
            elif stage == 1:
                source, target = g.at[:, other, b_rows, :], recv["b1"].at[slot, :, b_in, :]
            elif stage == 2:
                source, target = g.at[other, y, b_rows, :], recv["b2"].at[slot, b_in, :]
            elif stage == 3:
                source, target = g.at[z, y, b_rows, :], recv["b3"].at[slot, b_in, :]
            else:
                source, target = final.at[b_rows, :], final.at[b_rows, :]
            copies_b.append((source, target, to))
        for slot, other, to in self.peers(axis_a) if axis_a is not None and na else ():
            if stage == 1:
                source, target = g.at[:, :, rows16(mine + other * part, part), :], recv["a1"].at[slot, :, :, a_in, :]
            elif stage == 2:
                source, target = g.at[:, other, a_rows, :], recv["a2"].at[slot, :, a_in, :]
            else:
                source, target = g.at[other, y, a_rows, :], recv["a3"].at[slot, a_in, :]
            copies_a.append((source, target, to))
        if stage == 4 and na:
            copies_a = [(final.at[a_rows, :], final.at[a_rows, :], to) for to in self.heads()]
        return copies_b, copies_a

    def copies(self, stage, i):
        counts = self.counts(self.sizes)
        first = i * sum(map(sum, counts)) + sum(map(sum, counts[:stage]))
        copies_b, copies_a = self.plan(stage, i)
        made = []
        for copies, extra in ((copies_b, 0), (copies_a, counts[stage][0])):
            for n, (source, target, to) in enumerate(copies):
                index = first + extra + n
                made.append(
                    pltpu.make_async_remote_copy(
                        src_ref=source,
                        dst_ref=target,
                        send_sem=self.send_sems.at[index],
                        recv_sem=self.recv_sems.at[index],
                        device_id=to,
                        device_id_type=MESH,
                    )
                )
        return made

    @staticmethod
    def counts(sizes):
        z, y, x, _ = (size - 1 for size in sizes)
        return ((1, 0), (y, x), (z, y), (x, z), (1, 2 * x + 1))

    @staticmethod
    def semaphores(grid, xs, groups):
        sizes = (*grid, xs, 2)
        return len(groups) * sum(map(sum, Sums.counts(sizes))) + 12 * (max(sizes) - 1) + sum(sizes) + 2 * xs

    def claim(self, *groups):
        steps = []
        for i in groups:
            if self.stage[i] < self.STAGES:
                steps.append((i, self.stage[i]))
                self.stage[i] += 1
        return steps

    def do(self, steps):
        for i, stage in steps:
            if stage >= 0:
                for copy in self.copies(stage, i):
                    copy.wait_recv()
                self.add(stage, i)
            if stage + 1 < self.STAGES:
                for copy in self.copies(stage + 1, i):
                    copy.start()

    def advance(self, *groups):
        self.do(self.claim(*groups))

    def over(self, i):
        return self.stage[i] == self.STAGES

    def add(self, stage, i):
        z, y, x, c = self.place
        first, half, mine, na, part, b_row, nb = self.rows(i)
        g, recv = self.g, self.recv
        a_in, b_in = pl.ds(self.a_first(i), part), pl.ds(self.b_first(i), nb)
        a_rows, b_rows = rows16(mine + x * part, part), rows16(b_row, nb)

        def total(mine, got):
            value = mine.astype(f32)
            for other in got:
                value = value + other.astype(f32)
            return value.astype(bf)

        if stage == 0:

            def core(block, carry):
                zb, yb = block // self.ys, block % self.ys
                g[zb, yb, rows16(mine, half), :] += recv["core"][zb, yb, pl.ds(self.core_first(i), half), :]
                return carry

            lax.fori_loop(0, self.zs * self.ys, core, 0)
        elif stage == 1:

            def one(zb, carry):
                got = [recv["b1"][slot, zb, b_in, :] for slot in range(self.ys - 1)]
                g[zb, y, b_rows, :] = total(g[zb, y, b_rows, :], got)
                for yb in range(self.ys) if na else ():
                    got = [recv["a1"][slot, zb, yb, a_in, :] for slot in range(self.xs - 1)]
                    g[zb, yb, a_rows, :] = total(g[zb, yb, a_rows, :], got)
                return carry

            lax.fori_loop(0, self.zs, one, 0)
        elif stage == 2:
            g[z, y, b_rows, :] = total(g[z, y, b_rows, :], [recv["b2"][slot, b_in, :] for slot in range(self.zs - 1)])
            if na:

                def two(zb, carry):
                    got = [recv["a2"][slot, zb, a_in, :] for slot in range(self.ys - 1)]
                    g[zb, y, a_rows, :] = total(g[zb, y, a_rows, :], got)
                    return carry

                lax.fori_loop(0, self.zs, two, 0)
        elif stage == 3:
            got = [recv["b3"][slot, b_in, :] for slot in range(self.xs - 1)]
            self.final[b_rows, :] = total(g[z, y, b_rows, :], got)
            if na:
                got = [recv["a3"][slot, a_in, :] for slot in range(self.zs - 1)]
                self.final[a_rows, :] = total(g[z, y, a_rows, :], got)

    def small_copies(self, k, axis, held, got):
        most = max(self.sizes) - 1
        base = len(self.groups) * sum(map(sum, self.counts(self.sizes)))
        made = []
        for slot, other, to in self.peers(axis):
            index = base + (k * 4 + axis) * most + slot
            made.append(
                pltpu.make_async_remote_copy(
                    src_ref=held.at[axis],
                    dst_ref=got.at[self.got_first(axis) + slot],
                    send_sem=self.send_sems.at[index],
                    recv_sem=self.recv_sems.at[index],
                    device_id=to,
                    device_id_type=MESH,
                )
            )
        return made

    def got_first(self, axis):
        return sum(size - 1 for size in self.sizes[:axis])

    def small_send(self, k, axis, held, got):
        self.small.append((k, axis, held, got))
        for copy in self.small_copies(k, axis, held, got):
            copy.start()

    def small_add(self, k, axis, held, got):
        for copy in self.small_copies(k, axis, held, got):
            copy.wait_recv()
        size, me = self.sizes[axis], self.place[axis]
        total = None
        for n in range(size):
            value = held[axis]
            for slot in range(size - 1):
                value = jnp.where(lax.rem(me - slot - 1 + size, size) == n, got[self.got_first(axis) + slot], value)
            total = value if total is None else total + value
        held[axis - 1 if axis else 4] = total

    def early_plan(self, step, held, got):
        z, y, x, c = self.place
        half = held.shape[2] // 2
        part = half // self.xs
        mine = pl.ds(pl.multiple_of(c * half + x * part, 128), part)
        if step == 4:
            return [
                (held.at[0, :, pl.ds(pl.multiple_of(other * half, 128), half)], got.at[0], to)
                for _, other, to in self.peers(3)
            ]
        if step == 3:
            return [
                (
                    held.at[0, :, pl.ds(pl.multiple_of(c * half + other * part, 128), part)],
                    got.at[1 + slot, :, pl.ds(0, part)],
                    to,
                )
                for slot, other, to in self.peers(2)
            ]
        if step == 0:
            return [(held.at[2, :, mine], held.at[2, :, mine], to) for to in self.heads()]
        first = self.xs + (0 if step == 2 else self.ys - 1)
        return [
            (held.at[2 - step, :, mine], got.at[first + slot, :, pl.ds(0, part)], to)
            for slot, _, to in self.peers(step - 1)
        ]

    def early_copies(self, step, held, got):
        counts = (2 * self.xs - 1, self.zs - 1, self.ys - 1, self.xs - 1, 1)
        base = len(self.groups) * sum(map(sum, self.counts(self.sizes))) + 12 * (max(self.sizes) - 1) + sum(counts[:step])
        return [
            pltpu.make_async_remote_copy(
                src_ref=source,
                dst_ref=target,
                send_sem=self.send_sems.at[base + n],
                recv_sem=self.recv_sems.at[base + n],
                device_id=to,
                device_id_type=MESH,
            )
            for n, (source, target, to) in enumerate(self.early_plan(step, held, got))
        ]

    def early_next(self, step, held, got):
        z, y, x, c = self.place
        half = held.shape[2] // 2
        part = half // self.xs
        mine = pl.ds(pl.multiple_of(c * half + x * part, 128), part)
        if step < 5:
            for copy in self.early_copies(step, held, got):
                copy.wait_recv()
        if step == 4:
            held[0, :, pl.ds(pl.multiple_of(c * half, 128), half)] += got[0]
        elif step == 3:
            for slot in range(self.xs - 1):
                held[0, :, mine] += got[1 + slot, :, 0:part]
        elif step in (1, 2):
            axis = step - 1
            size, me = self.sizes[axis], self.place[axis]
            first = self.xs + (0 if step == 2 else self.ys - 1)
            total = None
            for n in range(size):
                value = held[2 - step, :, mine]
                for slot in range(size - 1):
                    value = jnp.where(lax.rem(me - slot - 1 + size, size) == n, got[first + slot, :, 0:part], value)
                total = value if total is None else total + value
            held[3 - step, :, mine] = total
        if step:
            for copy in self.early_copies(step - 1, held, got):
                copy.start()

    def early_sent(self, held, got):
        for step in range(5):
            for copy in self.early_copies(step, held, got):
                copy.wait_send()

    def small_next(self, k, axis, held, got):
        self.small_add(k, axis, held, got)
        if axis:
            self.small_send(k, axis - 1, held, got)

    def finish(self):
        for i in range(len(self.groups)):
            for stage in range(self.STAGES):
                for copy in self.copies(stage, i):
                    copy.wait_send()
        for small in self.small:
            for copy in self.small_copies(*small):
                copy.wait_send()


def recv_shapes(grid, xs, groups, height):
    zs, ys = grid
    na = sum(split_of(size, xs)[1] for _, size in groups) // xs
    nb = sum(split_of(size, xs)[2] for _, size in groups)
    na = max(na, 16)
    return {
        "core": (zs, ys, max(groups[3][0], height - groups[3][0]) // 2, 256),
        "a1": (xs - 1, zs, ys, na, 256),
        "b1": (ys - 1, zs, nb, 256),
        "a2": (ys - 1, zs, na, 256),
        "b2": (zs - 1, nb, 256),
        "a3": (zs - 1, na, 256),
        "b3": (xs - 1, nb, 256),
    }


SMALL = 16


def last_kernel(share, wide_share, final_ref, early_ref, late_ref, xgrad_in, cell_in, *refs):
    xgrad_out, cell_out, norms, wide_gain, glu, left, conv, depth, point, qkv, out, up, down = refs
    xgrad_out[...] = xgrad_in[...]
    cell_out[...] = cell_in[...]
    starts, _, _ = offsets(share, wide_share)
    depth[...] = early_ref[0:9, :]
    wide_gain[...] = early_ref[9:10, :]
    norms[0:2, :] = late_ref[0:2, :]
    norms[2:4, :] = early_ref[10:12, 0:D]
    for name, ref, tiles, size in (
        ("glu", glu, 4, share),
        ("left", left, 8, share),
        ("point", point, 1, wide_share),
        ("qkv", qkv, 6, share),
        ("out", out, 2, share),
        ("up", up, 8, share),
        ("down", down, 2, wide_share),
    ):
        for n in range(tiles):
            part, k = name, n
            if name in ("left", "glu") and n >= tiles // 2:
                part, k = ("left2" if name == "left" else "glu1"), n - tiles // 2
            first = starts[part] + k * size
            ref[:, 256 * n : 256 * n + 256] = final_ref[first : first + size, :].astype(f32)
    for k in range(3):
        first = starts["conv"] + k * share
        conv[k] = final_ref[first : first + share, :].astype(f32)


def local(
    grid,
    xs,
    cell_input,
    lengths,
    pair_ids,
    cotangent,
    norm_gains,
    wide_gain,
    w_glu,
    w_left,
    w_conv3,
    w_depth,
    w_point,
    w_qkv,
    w_out,
    w_up,
    w_down,
):
    zs, ys = grid
    dp = zs * ys
    share, wide_share = 512 // dp, 2048 // dp
    rows = cell_input.shape[0]
    sents = lengths.shape[0]
    starts, groups, height = offsets(share, wide_share)
    wg = wide_gain.reshape(FF // 128, 128)
    shape = jax.ShapeDtypeStruct
    params = pltpu.CompilerParams(vmem_limit_bytes=62 << 20)
    kept = kept_shapes(sents)
    anywhere = pl.BlockSpec(memory_space=pl.ANY)
    most = zs + ys + xs - 2
    counting = Sums.semaphores(grid, xs, ())
    front = pl.pallas_call(
        functools.partial(front_kernel, sents, grid, xs),
        out_shape=[shape((rows, D), bf)] + list(kept.values()),
        in_specs=[smem(), smem(), vmem(), anywhere] + [vmem()] * 2 + [anywhere] * 3 + [vmem()] + [anywhere] * 5,
        out_specs=[anywhere] * (1 + len(kept)),
        scratch_shapes=[pltpu.VMEM(v, bf) for v in (*WEIGHTS, (rows, D))]
        + [pltpu.SemaphoreType.DMA((9,)), pltpu.VMEM((rows, D), bf)]
        + [pltpu.VMEM(v.shape, v.dtype) for v in kept.values()]
        + [
            pltpu.SemaphoreType.DMA((len(kept) + 1, sents)),
            pltpu.VMEM((16, FF), f32),
            pltpu.VMEM((SEQ, D), f32),
            pltpu.VMEM((PAD, D), f32),
            pltpu.VMEM((SEQ, FF), f32),
            pltpu.VMEM((SEQ, HALF), f32),
            pltpu.VMEM((SEQ, 3 * D), bf),
            pltpu.SemaphoreType.DMA((counting,)),
            pltpu.SemaphoreType.DMA((counting,)),
            pltpu.VMEM((5, 8, 128), f32),
            pltpu.VMEM((most, 8, 128), f32),
            pltpu.VMEM((sents, 8, 128), f32),
        ],
        compiler_params=pltpu.CompilerParams(vmem_limit_bytes=62 << 20, collective_id=1, has_side_effects=True),
        name="front",
    )(lengths, pair_ids, cell_input, cotangent, norm_gains, wg, w_glu, w_left, w_conv3, w_depth, w_point, w_qkv, w_out, w_up, w_down)
    cell, arrays = front[0], front[1:]
    recv = recv_shapes(grid, xs, groups, height)
    semaphores = Sums.semaphores(grid, xs, groups)
    input_grad, final, early, late = pl.pallas_call(
        functools.partial(back_kernel, sents, grid, xs, tuple(recv)),
        out_shape=[shape((rows, D), f32), shape((height, 256), bf), shape((SMALL, FF), f32), shape((8, D), f32)],
        in_specs=[vmem()] * 2 + [anywhere] * 3 + [vmem()] + [anywhere] * (2 + len(kept)),
        out_specs=[anywhere] * 4,
        scratch_shapes=[pltpu.VMEM(v, bf) for v in (*recv.values(), *WEIGHTS[:5])]
        + [
            pltpu.SemaphoreType.DMA((32,)),
            pltpu.SemaphoreType.DMA((semaphores,)),
            pltpu.SemaphoreType.DMA((semaphores,)),
            pltpu.VMEM((zs, ys, height, 256), bf),
            pltpu.VMEM((height, 256), bf),
            pltpu.VMEM((3, SMALL, FF), f32),
            pltpu.VMEM((most, SMALL, FF // 2), f32),
            pltpu.VMEM((5, 8, D), f32),
            pltpu.VMEM((most, 8, D), f32),
            pltpu.VMEM((rows, FF), bf),
            pltpu.VMEM((rows, FF), bf),
            pltpu.VMEM((rows, 3 * D), bf),
            pltpu.VMEM((sents, HEADS, SEQ, SEQ), bf),
            pltpu.VMEM((rows, D), f32),
            pltpu.VMEM((rows, D), bf),
            pltpu.VMEM((rows, D), bf),
            pltpu.VMEM((rows, D), bf),
            pltpu.VMEM((D, rows), bf),
            pltpu.VMEM((D, rows), bf),
            pltpu.VMEM((3 * D, rows), bf),
            pltpu.VMEM((rows, HALF), bf),
            pltpu.VMEM((rows, 8), f32),
            pltpu.VMEM((sents * 8, D), f32),
            pltpu.VMEM((2, 16, PAD, 128), f32),
            pltpu.VMEM((16, FF), f32),
            pltpu.VMEM((3 * D, SEQ), bf),
            pltpu.VMEM((16, PAD, 128), f32),
            pltpu.VMEM((SEQ, FF), f32),
            pltpu.VMEM((9, 8, FF), f32),
            pltpu.VMEM((SEQ, 128), f32),
            pltpu.VMEM((SEQ, 128), f32),
            pltpu.VMEM((PAD, HALF), f32),
            pltpu.VMEM((32, D), f32),
        ],
        compiler_params=pltpu.CompilerParams(vmem_limit_bytes=63 << 20, collective_id=0, has_side_effects=True),
        name="back",
    )(norm_gains, wg, w_glu, w_left, w_conv3, w_depth, w_point, w_qkv, *arrays)
    input_grad, cell_output, norms, gain, glu, left, conv, depth, point, qkv, out, up, down = pl.pallas_call(
        functools.partial(last_kernel, share, wide_share),
        out_shape=[
            shape((rows, D), f32),
            shape((rows, D), bf),
            shape((4, D), f32),
            shape((1, FF), f32),
            shape((share, 2 * D), f32),
            shape((share, FF), f32),
            shape((3, share, HALF), f32),
            shape((9, FF), f32),
            shape((wide_share, HALF), f32),
            shape((share, 3 * D), f32),
            shape((share, D), f32),
            shape((share, FF), f32),
            shape((wide_share, D), f32),
        ],
        in_specs=[vmem()] * 5,
        out_specs=[vmem()] * 13,
        compiler_params=params,
        name="last",
    )(final, early, late, input_grad, cell)
    return cell_output, input_grad, norms, gain.reshape(FF), glu, left, conv, depth, point, qkv, out, up, down


def solution(mesh):
    dp, head = mesh.shape["dp"], mesh.shape["head"]
    ys = 2 ** ((dp.bit_length() - 1) // 2)
    grid = (dp // ys, ys)
    xs = head // 2
    row = P(("dp", "head"), None)
    in_specs = (row, P(("dp", "head")), P(("dp", "head")), row) + (P(),) * 11
    share = P("dp", None)
    out_specs = (row, row, P(), P(), share, share, P(None, "dp", None), P(), share, share, share, share, share)
    return jax.shard_map(
        functools.partial(local, grid, xs), mesh=mesh, in_specs=in_specs, out_specs=out_specs, check_vma=False
    )
```

```python
import functools

import jax
import jax.numpy as jnp
from jax import lax
from jax.experimental import pallas as pl
from jax.experimental.pallas import tpu as pltpu
from jax.sharding import PartitionSpec as P

HEADS = 8
DH = 64
SEQ = 256
PAIRS = 4
D = 512
FF = 2048
HALF = 256
PAD = SEQ + 16
EPS = 1e-05
MESH = pl.DeviceIdType.MESH
bf = jnp.bfloat16
f32 = jnp.float32
GELU_A = 0.7978845608028654
GELU_B = 0.7978845608028654 * 0.044715
CH = 32


def nn(a, b):
    return lax.dot_general(a, b, (((1,), (0,)), ((), ())), preferred_element_type=f32)


def nt(a, b):
    return lax.dot_general(a, b, (((1,), (1,)), ((), ())), preferred_element_type=f32)


def tn(a, b):
    return lax.dot_general(a, b, (((0,), (0,)), ((), ())), preferred_element_type=f32)


def gelu_both(v):
    square = v * v
    t = jnp.tanh(v * (GELU_A + GELU_B * square))
    half = 0.5 + 0.5 * t
    slope = half + (0.5 * v) * (1.0 - t * t) * (GELU_A + (3.0 * GELU_B) * square)
    return v * half, slope


def sigmoid(v):
    return 0.5 + 0.5 * jnp.tanh(0.5 * v)


def fold8(v):
    total = v[0:8]
    for i in range(1, v.shape[0] // 8):
        total = total + v[8 * i : 8 * i + 8]
    return total


def norm(v):
    centred = v - jnp.mean(v, axis=-1, keepdims=True)
    rstd = lax.rsqrt(jnp.mean(centred * centred, axis=-1, keepdims=True) + EPS)
    return centred, rstd


def norm_back(g, low, gain, inverse, rstd):
    gy = g * gain
    m1 = jnp.mean(gy, axis=-1, keepdims=True)
    m2 = jnp.mean(g * low, axis=-1, keepdims=True)
    return rstd * (gy - m1 - (low * inverse) * m2)


def at(s, first, size):
    return pl.ds(pl.multiple_of(s * SEQ + first, size), size)


def one_row(ref):
    return jnp.concatenate([ref[j : j + 1, :] for j in range(ref.shape[0])], axis=1).astype(f32)


def row_of(first, size):
    return first + lax.broadcasted_iota(jnp.int32, (size, 1), 0)


KEPT = (
    "a", "b", "e", "f", "rstd", "sig", "u", "dgl", "dgr", "m",
    "depth", "qkvt", "pt", "mixt", "up", "gup", "ga", "gmixt", "gain_f", "gl",
)


def kept_shapes(sents):
    rows = sents * SEQ
    shape = jax.ShapeDtypeStruct
    return {
        "a": shape((rows, D), bf),
        "b": shape((rows, D), bf),
        "e": shape((rows, D), bf),
        "f": shape((rows, D), bf),
        "rstd": shape((rows, 8), f32),
        "sig": shape((rows, D), bf),
        "u": shape((rows, D), bf),
        "dgl": shape((rows, FF), bf),
        "dgr": shape((rows, HALF), bf),
        "m": shape((sents, 16, PAD, 128), f32),
        "depth": shape((8, sents, SEQ, 256), bf),
        "qkvt": shape((3 * D, rows), bf),
        "pt": shape((sents, HEADS, SEQ, SEQ), bf),
        "mixt": shape((D, rows), bf),
        "up": shape((rows, FF), bf),
        "gup": shape((rows, FF), bf),
        "ga": shape((rows, D), f32),
        "gmixt": shape((D, rows), bf),
        "gain_f": shape((sents * 8, D), f32),
        "gl": shape((rows, D), bf),
    }


def part_of(name, s):
    if name in ("m", "pt"):
        return (s,)
    if name == "depth":
        return (slice(None), s)
    if name in ("qkvt", "mixt", "gmixt"):
        return (slice(None), pl.ds(pl.multiple_of(s * SEQ, SEQ), SEQ))
    if name == "gain_f":
        return (pl.ds(pl.multiple_of(s * 8, 8), 8),)
    return (pl.ds(pl.multiple_of(s * SEQ, SEQ), SEQ),)


WEIGHTS = ((D, 2 * D), (D, FF), (3, D, HALF), (FF, HALF), (D, 3 * D), (D, D), (D, FF), (FF, D))


def front_kernel(
    sents,
    grid,
    xs,
    len_ref,
    pair_ref,
    x_ref,
    cot_ref,
    gains_ref,
    wg_ref,
    wglu,
    wleft,
    wconv,
    wdepth,
    wpoint,
    wqkv,
    wout,
    wup,
    wdown,
    out_far,
    *refs,
):
    far, refs = dict(zip(KEPT, refs)), refs[len(KEPT) :]
    held, refs = refs[: len(WEIGHTS) + 1], refs[len(WEIGHTS) + 1 :]
    weights = (wglu, wleft, wconv, wpoint, wqkv, wout, wup, wdown, cot_ref)
    load_sems, out_ref, refs = refs[0], refs[1], refs[2:]
    load = [pltpu.make_async_copy(w, h, load_sems.at[k]) for k, (w, h) in enumerate(zip(weights, held))]
    for copy in load[:3]:
        copy.start()
    wglu, wleft, wconv, wpoint, wqkv, wout, wup, wdown, cot_ref = held
    near, refs = dict(zip(KEPT, refs)), refs[len(KEPT) :]
    ship_sems, wp_ref, xf_ref, bs_ref, wide_ref, sep_ref, qkv_ref = refs[:7]
    send_sems, recv_sems, count_ref, count_got, fac_ref = refs[7:]
    sums = Sums(grid, xs, (), None, None, None, send_sems, recv_sems)
    others = sums.greet(False)
    lane = lax.broadcasted_iota(jnp.int32, (8, 128), 1)
    counts = jnp.zeros((8, 128), f32)
    for s in range(sents):
        counts = counts + jnp.where(lane == pair_ref[s], len_ref[s].astype(f32), 0.0)
    count_ref[3] = counts

    def count_next(axis):
        if axis < 4:
            sums.small_add(0, axis, count_ref, count_got)
        else:
            sums.greeted(others)
        if axis:
            for copy in sums.small_copies(0, axis - 1, count_ref, count_got):
                copy.start()
        else:
            counts = count_ref[4]
            total = jnp.sum(counts, axis=1, keepdims=True)
            for k in range(sents):
                mine = jnp.sum(jnp.where(lane == pair_ref[k], counts, 0.0), axis=1, keepdims=True)
                fac_ref[k] = jnp.broadcast_to(total / (PAIRS * mine), (8, 128))

    (a_ref, b_ref, e_ref, f_ref, rstd_ref, sig_ref, u_ref, dgl_ref, dgr_ref, m_ref) = [near[n] for n in KEPT[:10]]
    (depth_ref, qkvt_ref, pt_ref, mixt_ref, up_ref, gup_ref, ga_ref, gmixt_ref, gain_f_ref, gl_ref) = [near[n] for n in KEPT[10:]]

    def shipment(name, s):
        k = KEPT.index(name)
        where = part_of(name, s)
        return pltpu.make_async_copy(near[name].at[where], far[name].at[where], ship_sems.at[k, s])

    def leave(s):
        return pltpu.make_async_copy(out_ref.at[at(s, 0, SEQ), :], out_far.at[at(s, 0, SEQ), :], ship_sems.at[len(KEPT), s])

    def ship(s, *names):
        for name in names:
            shipment(name, s).start()

    wp_ref[0:9, :] = wdepth[...].astype(f32) * one_row(wg_ref)
    gain_f_ref[...] = jnp.zeros_like(gain_f_ref)
    zero8 = jnp.zeros((8, 128), f32)

    def sentence(s, carry):
        length = len_ref[s]

        def loaded(*which, then=(), axis=None):
            @pl.when(s == 0)
            def _():
                for k in which:
                    load[k].wait()
                for k in then:
                    load[k].start()
                if axis is not None:
                    count_next(axis)

        gains = gains_ref[...].astype(f32)
        rows = at(s, 0, SEQ)
        for c in range(0, SEQ, CH):
            cen, rstd = norm(x_ref[at(s, c, CH), :].astype(f32))
            a_ref[at(s, c, CH), :] = (cen * rstd * gains[0:1]).astype(bf)
            rstd_ref[at(s, c, CH), 0:1] = rstd
        a_low = a_ref[rows, :]
        loaded(0, then=(3, 4), axis=4)
        for n in range(2):
            cols = slice(256 * n, 256 * n + 256)
            gcols = slice(512 + 256 * n, 768 + 256 * n)
            value = nn(a_low, wglu[:, cols])
            gate = nn(a_low, wglu[:, gcols])
            for c in range(0, SEQ, CH):
                sig = sigmoid(gate[c : c + CH])
                mixed = value[c : c + CH] * sig
                xf_ref[c : c + CH, cols] = x_ref[at(s, c, CH), cols].astype(f32) + mixed
                sig_ref[at(s, c, CH), cols] = sig.astype(bf)
                u_ref[at(s, c, CH), cols] = (mixed * (1.0 - sig)).astype(bf)
        ship(s, "a", "sig", "u")
        for c in range(0, SEQ, CH):
            cen, rstd = norm(xf_ref[c : c + CH, :])
            rstd = jnp.where(row_of(c, CH) < length, rstd, 0.0)
            b_low = cen * rstd * gains[1:2]
            b_ref[at(s, c, CH), :] = b_low.astype(bf)
            rstd_ref[at(s, c, CH), 1:2] = rstd
            bs_ref[8 + c : 8 + c + CH, :] = b_low
        b_low = b_ref[rows, :]
        bs_ref[0:8, :] = jnp.zeros((8, D), f32)
        bs_ref[8 + SEQ : 16 + SEQ, :] = jnp.zeros((8, D), f32)
        loaded(1, 2, then=(5, 6, 7, 8), axis=3)
        right = (
            nn(bs_ref[7 : 7 + SEQ, :].astype(bf), wconv[0])
            + nn(b_low, wconv[1])
            + nn(bs_ref[9 : 9 + SEQ, :].astype(bf), wconv[2])
        )
        for n in range(8):
            cols = slice(256 * n, 256 * n + 256)
            left = nn(b_low, wleft[:, cols])
            for c in range(0, SEQ, CH):
                hidden, slope = gelu_both(left[c : c + CH])
                dgl_ref[at(s, c, CH), cols] = slope.astype(bf)
                if n == 0:
                    extra, slope = gelu_both(right[c : c + CH])
                    dgr_ref[at(s, c, CH), :] = slope.astype(bf)
                    hidden = hidden + extra
                wide_ref[c : c + CH, cols] = hidden
        ship(s, "b", "dgl", "dgr")
        for j in range(16):
            m_ref[s, j, 0:8, :] = zero8
            m_ref[s, j, 8 + SEQ : PAD, :] = zero8
        for c in range(0, SEQ, 8):
            mean = jnp.mean(wide_ref[c : c + 8, :], axis=-1, keepdims=True)
            cen = wide_ref[c : c + 8, :] - mean
            rstd = lax.rsqrt(jnp.mean(cen * cen, axis=-1, keepdims=True) + EPS)
            rstd = jnp.where(row_of(c, 8) < length, rstd, 0.0)
            rstd_ref[at(s, c, 8), 2:3] = rstd
            for j in range(16):
                m_ref[s, j, 8 + c : 16 + c, :] = cen[:, 128 * j : 128 * j + 128] * rstd
        for j in range(16):
            cols = slice(128 * j, 128 * j + 128)
            taps = [wp_ref[o : o + 1, cols] for o in range(9)]
            for c in range(0, SEQ, CH):
                total = m_ref[s, j, c + 4 : c + 4 + CH, :] * taps[0]
                for o in range(1, 9):
                    total = total + m_ref[s, j, c + 4 + o : c + 4 + o + CH, :] * taps[o]
                depth_ref[j // 2, s, c : c + CH, 128 * (j % 2) : 128 * (j % 2) + 128] = total.astype(bf)
        ship(s, "m", "depth")
        loaded(3, axis=2)
        depth = jnp.concatenate([depth_ref[n, s] for n in range(8)], axis=1)
        sep_ref[...] = nn(depth, wpoint[...])
        for c in range(0, SEQ, CH):
            conv = xf_ref[c : c + CH, :]
            conv = jnp.concatenate([conv[:, :HALF] + sep_ref[c : c + CH, :], conv[:, HALF:]], axis=1)
            xf_ref[c : c + CH, :] = conv
            cen, rstd = norm(conv)
            e_ref[at(s, c, CH), :] = (cen * rstd * gains[2:3]).astype(bf)
            rstd_ref[at(s, c, CH), 3:4] = rstd
        e_low = e_ref[rows, :]
        loaded(4)
        for n in range(6):
            cols = slice(256 * n, 256 * n + 256)
            part = nn(e_low, wqkv[:, cols]).astype(bf)
            qkv_ref[:, cols] = part
            qkvt_ref[cols, at(s, 0, SEQ)] = part.T
        ship(s, "e", "qkvt")
        bias = jnp.where(row_of(0, SEQ) < jnp.maximum(length, 1), 0.0, -1e30)
        for h in range(HEADS):
            base = 3 * DH * h
            key = qkv_ref[:, base + DH : base + 2 * DH] * jnp.asarray(DH**-0.5, bf)
            query_t = qkvt_ref[base : base + DH, at(s, 0, SEQ)]
            value_t = qkvt_ref[base + 2 * DH : base + 3 * DH, at(s, 0, SEQ)]
            for q in range(0, SEQ, 128):
                scores = nn(key, query_t[:, q : q + 128]) + bias
                scores = jnp.exp(scores - jnp.max(scores, axis=0, keepdims=True))
                scores = scores * (1.0 / jnp.sum(scores, axis=0, keepdims=True))
                pt_ref[s, h, :, q : q + 128] = scores.astype(bf)
            mixt_ref[DH * h : DH * h + DH, at(s, 0, SEQ)] = nn(value_t, pt_ref[s, h]).astype(bf)
        ship(s, "pt", "mixt")
        loaded(5, axis=1)
        for n in range(2):
            cols = slice(256 * n, 256 * n + 256)
            xf_ref[:, cols] += tn(mixt_ref[:, at(s, 0, SEQ)], wout[:, cols])
        for c in range(0, SEQ, CH):
            cen, rstd = norm(xf_ref[c : c + CH, :])
            f_ref[at(s, c, CH), :] = (cen * rstd * gains[3:4]).astype(bf)
            rstd_ref[at(s, c, CH), 4:5] = rstd
        f_low = f_ref[rows, :]
        loaded(6)
        for n in range(8):
            cols = slice(256 * n, 256 * n + 256)
            up = nn(f_low, wup[:, cols])
            for c in range(0, SEQ, CH):
                low, slope = gelu_both(up[c : c + CH])
                up_ref[at(s, c, CH), cols] = low.astype(bf)
                gup_ref[at(s, c, CH), cols] = slope.astype(bf)
        loaded(7, 8, axis=0)
        for n in range(2):
            cols = slice(256 * n, 256 * n + 256)
            down = nn(up_ref[rows, :], wdown[:, cols])
            out_ref[rows, cols] = (xf_ref[:, cols] + down).astype(bf)
        ship(s, "f", "rstd", "up")
        leave(s).start()
        for c in range(0, SEQ, CH):
            weight = jnp.where(row_of(c, CH) < length, fac_ref[s, 0:1, 0:1], 0.0)
            g_out = cot_ref[at(s, c, CH), :].astype(f32) * weight
            ga_ref[at(s, c, CH), :] = g_out
            gl_ref[at(s, c, CH), :] = g_out.astype(bf)
        g_low = gl_ref[rows, :]
        for n in range(8):
            cols = slice(256 * n, 256 * n + 256)
            back = nt(g_low, wdown[cols, :])
            gup_ref[rows, cols] = (back * gup_ref[rows, cols].astype(f32)).astype(bf)
        ship(s, "gup", "gl")
        for n in range(2):
            cols = slice(256 * n, 256 * n + 256)
            wide_ref[:, cols] = nt(gup_ref[rows, :], wup[cols, :])
        inverse = 1.0 / gains[3:4]
        for c in range(0, SEQ, CH):
            g_f = wide_ref[c : c + CH, 0:D]
            low = f_ref[at(s, c, CH), :].astype(f32)
            gain_f_ref[pl.ds(pl.multiple_of(s * 8, 8), 8), :] += fold8(g_f * low)
            back = norm_back(g_f, low, gains[3:4], inverse, rstd_ref[at(s, c, CH), 4:5])
            ga_ref[at(s, c, CH), :] += back
        gmixt_ref[:, at(s, 0, SEQ)] = nt(wout[...], ga_ref[rows, :].astype(bf)).astype(bf)
        ship(s, "ga", "gmixt", "gain_f")
        return carry

    lax.fori_loop(0, sents, sentence, 0)

    def landed(s, carry):
        for name in KEPT:
            shipment(name, s).wait()
        leave(s).wait()
        return carry

    lax.fori_loop(0, sents, landed, 0)
    for axis in range(4):
        for copy in sums.small_copies(0, axis, count_ref, count_got):
            copy.wait_send()


def vmem():
    return pl.BlockSpec(memory_space=pltpu.VMEM)


def smem():
    return pl.BlockSpec(memory_space=pltpu.SMEM)


def offsets(share, wide_share):
    sizes = (
        ("up", 8 * share, True),
        ("down", 2 * wide_share, True),
        ("out", 2 * share, False),
        ("qkv", 6 * share, True),
        ("point", wide_share, True),
        ("left", 4 * share, True),
        ("left2", 4 * share, True),
        ("conv", 3 * share, True),
        ("glu", 2 * share, True),
        ("glu1", 2 * share, True),
    )
    first, starts, groups, begin = 0, {}, [], 0
    for name, size, ends in sizes:
        starts[name] = first
        first += size
        if ends:
            first = -(-first // 32) * 32
            groups.append((begin, first - begin))
            begin = first
    return starts, groups, first


def put(g_ref, grid, tile, first, share, wide, chunk=0):
    _, ys = grid
    for part in range(tile.shape[1] // 256):
        for k in range(512 // share):
            block = chunk * (512 // share) + k
            piece = tile[k * share : (k + 1) * share, 256 * part : 256 * part + 256]
            rows = pl.ds(pl.multiple_of(first + part * share, 16), share)
            g_ref[block // ys, block % ys, rows, :] = piece.astype(bf)


SCHEDULE = {
    "u3": (0,),
    "d3": (1,),
    "o": (0,),
    "a1a": (1,),
    "q0": (0,),
    "q2": (2,),
    "p1": (1,),
    "p2": (2,),
    "p3": (3,),
    "w0b": (0,),
    "w0c": (3,),
    "w1c": (1,),
    "w2b": (0,),
    "w2c": (2,),
    "l1": (4, 3, 1,),
    "l2": (0,),
    "l3": (5,),
    "c": (6, 4, 1,),
    "i0": (5, 2,),
    "i1": (6,),
    "i2": (3, 4,),
    "g0": (7,),
    "g1": (8,),
    "r0": (5, 7,),
    "r1": (8, 2, 6,),
    "r2": (3, 4,),
    "e0": (5,),
    "e1": (7, -1, 2,),
    "e2": (3, 8, 6,),
    "z": (-1, 4, -2, 5, -1, 4, 7, -2, 5, 8, 6, -2, 6, -1, 7, 8, -1, -2, 7, 8,),
}


def back_kernel(
    sents,
    grid,
    xs,
    names,
    gains_ref,
    wg_ref,
    wglu_far,
    wleft_far,
    wconv_far,
    wdepth,
    wpoint_far,
    wqkv_far,
    *refs,
):
    far, refs = dict(zip(KEPT, refs)), refs[len(KEPT) :]
    xgrad_far, final_far, early_far, late_far = refs[:4]
    recv, refs = dict(zip(names, refs[4:])), refs[4 + len(names) :]
    (wglu, wleft, wconv, wpoint, wqkv), refs = refs[:5], refs[5:]
    (
        fetch_sems,
        send_sems,
        recv_sems,
        g_ref,
        final_ref,
        early_ref,
        early_got,
        late_ref,
        late_got,
        first_wide,
        second_wide,
        gqkv_ref,
        squares,
        conv_ref,
        gl_ref,
        fs_ref,
        gas_ref,
        mixt_ref,
        gmixt_ref,
        qkvt_ref,
        dgr_ref,
        rstd_ref,
        gain_f_ref,
        m_ref,
        wp_ref,
        gqkvt_ref,
        gd_ref,
        wide_ref,
        taps_ref,
        s1_ref,
        s2_ref,
        right_ref,
        gain_ref,
    ) = refs
    e_ref = gas_ref
    gr_refs = (gl_ref.at[:, 0:HALF], gl_ref.at[:, HALF:D], fs_ref.at[:, 0:HALF])
    sep_ref = fs_ref.at[:, HALF:D]
    up_ref = gleft_ref = dgl_ref = first_wide
    gup_ref = second_wide
    a_ref, b_ref, sig_ref, u_ref = [second_wide.at[:, D * k : D * k + D] for k in range(4)]
    gg_ref = gqkv_ref
    pt_ref, depth_view = squares, squares.reshape(8, sents, SEQ, 256)
    where = dict(
        a=a_ref, b=b_ref, e=e_ref, f=fs_ref, rstd=rstd_ref, sig=sig_ref, u=u_ref, dgl=first_wide, dgr=dgr_ref,
        qkvt=qkvt_ref, mixt=mixt_ref, up=first_wide, gup=second_wide, ga=conv_ref, gmixt=gmixt_ref, gain_f=gain_f_ref,
        pt=squares, depth=depth_view, gl=gl_ref, wglu=wglu, wleft=wleft, wconv=wconv, wpoint=wpoint, wqkv=wqkv,
    )
    far.update(wglu=wglu_far, wleft=wleft_far, wconv=wconv_far, wpoint=wpoint_far, wqkv=wqkv_far)
    order = (
        "gmixt", "qkvt", "pt", "f", "gup", "ga", "gl", "up", "gain_f", "rstd", "mixt", "wqkv", "wpoint", "dgr",
        "wleft", "wconv", "wglu", "e", "b", "a", "sig", "u", "dgl", "depth",
    )

    def wide_tile(i):
        return pl.ds(pl.multiple_of(i * 512, 512), 512)

    def fetch(name):
        return pltpu.make_async_copy(far[name], where[name], fetch_sems.at[order.index(name)])

    def start(*names):
        for name in names:
            fetch(name).start()

    def wait(*names):
        for name in names:
            fetch(name).wait()

    def fetch_tile(name, i):
        tile = wide_tile(i)
        sem = fetch_sems.at[len(order) + 6 + (4 if name == "up" else 0) + i]
        return pltpu.make_async_copy(far[name].at[:, tile], where[name].at[:, tile], sem)

    def fetch_m(s):
        return pltpu.make_async_copy(far["m"].at[s], m_ref.at[s % 2], fetch_sems.at[len(order) + s % 2])

    start("f")
    for i in range(4):
        fetch_tile("gup", i).start()
    share, wide_share = 512 // (grid[0] * grid[1]), 2048 // (grid[0] * grid[1])
    starts, groups, _ = offsets(share, wide_share)
    sums = Sums(grid, xs, groups, g_ref, final_ref, recv, send_sems, recv_sems)
    sums.greeted(sums.greet())
    small_step = {-1: 4, -2: 3}

    def claim(name):
        steps = []
        for i in SCHEDULE.get(name, ()):
            if i >= 0:
                steps += sums.claim(i)
            elif small_step[i] >= 0:
                steps.append((i, small_step[i]))
                small_step[i] -= 1
        return steps

    def do(steps):
        for i, stage in steps:
            if i >= 0:
                sums.do([(i, stage)])
            elif i == -1:
                sums.early_next(stage, early_ref, early_got)
            else:
                sums.small_next(2, stage, late_ref, late_got)

    def point(name):
        do(claim(name))

    def loop(name, first, last, body, parts=""):
        claims = {(k, part): claim(f"{name}{k}{part}") for k in range(first, last) for part in parts or ("",)}

        def within(k, part):
            for n in range(first, last):
                if claims[n, part]:
                    pl.when(k == n)(functools.partial(do, claims[n, part]))

        def round(k, carry):
            body(k, within)
            if not parts:
                within(k, "")
            return carry

        lax.fori_loop(first, last, round, 0)

    wp_ref[0:9, :] = wdepth[...].astype(f32) * one_row(wg_ref)
    gain_ref[...] = jnp.zeros_like(gain_ref)
    taps_ref[...] = jnp.zeros_like(taps_ref)

    wait("f")
    start("gl")
    for i in range(4):
        fetch_tile("up", i).start()
    start("mixt", "ga", "rstd", "gain_f")

    def grad_up(i, within):
        fetch_tile("gup", i).wait()
        tile = tn(fs_ref[...], gup_ref[:, wide_tile(i)])
        put(g_ref, grid, tile, starts["up"] + i * 2 * share, share, False)

    loop("u", 0, 4, grad_up)
    wait("gl")
    start("gmixt", "qkvt", "pt", "b", "a", "sig", "u")

    def grad_down(i, within):
        fetch_tile("up", i).wait()
        put(g_ref, grid, tn(up_ref[:, wide_tile(i)], gl_ref[...]), starts["down"], wide_share, True, i)

    loop("d", 0, 4, grad_down)
    wait("ga", "mixt", "rstd", "gain_f")
    start("dgl", "wqkv")
    for c in range(0, sents * SEQ, CH):
        gas_ref[c : c + CH, :] = conv_ref[c : c + CH, :].astype(bf)
    put(g_ref, grid, nn(mixt_ref[...], gas_ref[...]), starts["out"], share, False)
    start("e", "wpoint", "dgr")
    point("o")

    for s in range(sents):
        gain_ref[24:32, :] += gain_f_ref[8 * s : 8 * s + 8, :]
    wait("gmixt", "qkvt", "pt")

    def attend(s, within):
        rows = at(s, 0, SEQ)
        for h in range(HEADS):
            base = 3 * DH * h
            g_o = gmixt_ref[DH * h : DH * h + DH, rows]
            query_t = qkvt_ref[base : base + DH, rows]
            key_t = qkvt_ref[base + DH : base + 2 * DH, rows]
            value = qkvt_ref[base + 2 * DH : base + 3 * DH, rows].T
            probs = pt_ref[s, h]
            halves = []
            for q in range(0, SEQ, 128):
                part = probs[:, q : q + 128].astype(f32)
                back = nn(value, g_o[:, q : q + 128])
                both = part * back
                halves.append((both - part * jnp.sum(both, axis=0, keepdims=True)).astype(bf))
            g_scores = jnp.concatenate(halves, axis=1)
            gqkvt_ref[base : base + DH, :] = (nn(key_t, g_scores) * DH**-0.5).astype(bf)
            gqkvt_ref[base + DH : base + 2 * DH, :] = (nt(query_t, g_scores) * DH**-0.5).astype(bf)
            gqkvt_ref[base + 2 * DH : base + 3 * DH, :] = nt(g_o, probs).astype(bf)
            if h % 4 == 3:
                within(s, "ab"[h // 4])
        for n in range(6):
            cols = slice(256 * n, 256 * n + 256)
            gqkv_ref[rows, cols] = gqkvt_ref[cols, :].T

    loop("a", 0, sents, attend, "ab")
    start("depth")
    fetch_m(0).start()
    if sents > 1:
        fetch_m(1).start()
    wait("e")

    def grad_qkv(i, within):
        put(g_ref, grid, tn(e_ref[...], gqkv_ref[:, wide_tile(i)]), starts["qkv"] + i * 2 * share, share, False)

    loop("q", 0, 3, grad_qkv)

    def attention_input(s, within):
        gains = gains_ref[...].astype(f32)
        inverse = 1.0 / gains[2:3]
        rows = at(s, 0, SEQ)
        for n in range(2):
            cols = slice(256 * n, 256 * n + 256)
            wide_ref[:, cols] = nt(gqkv_ref[rows, :], wqkv[cols, :])
        for c in range(0, SEQ, CH):
            part = at(s, c, CH)
            g_e = wide_ref[c : c + CH, 0:D]
            low = e_ref[part, :].astype(f32)
            gain_ref[16:24, :] += fold8(g_e * low)
            g_conv = conv_ref[part, :] + norm_back(g_e, low, gains[2:3], inverse, rstd_ref[part, 3:4])
            conv_ref[part, :] = g_conv
            sep_ref[part, :] = g_conv[:, :HALF].astype(bf)

    wait("wqkv")
    loop("n", 0, sents, attention_input)
    wait("depth")

    def grad_point(i, within):
        depth = [depth_view[2 * i + k].reshape(sents * SEQ, 256) for k in range(2)]
        put(g_ref, grid, tn(jnp.concatenate(depth, axis=1), sep_ref[...]), starts["point"], wide_share, True, i)

    loop("p", 0, 4, grad_point)
    start("wleft", "wconv", "wglu")
    wait("b", "a", "sig", "u", "dgr", "dgl", "wpoint")

    zero8 = jnp.zeros((8, 128), f32)

    def g_depth(rows):
        for n in range(8):
            back = nt(sep_ref[rows, :], wpoint[256 * n : 256 * n + 256, :])
            for k in range(2):
                gd_ref[2 * n + k, 8 : 8 + SEQ, :] = back[:, 128 * k : 128 * k + 128]

    def wide(s, within):
        rows = at(s, 0, SEQ)
        slot = s % 2
        fetch_m(s).wait()
        g_depth(rows)
        within(s, "a")
        for j in range(16):
            gd_ref[j, 0:8, :] = zero8
            gd_ref[j, 8 + SEQ : PAD, :] = zero8
            cols = slice(128 * j, 128 * j + 128)
            taps = [wp_ref[o : o + 1, cols] for o in range(9)]
            for c in range(0, SEQ, CH):
                total = gd_ref[j, c + 12 : c + 12 + CH, :] * taps[0]
                for o in range(1, 9):
                    total = total + gd_ref[j, c + 12 - o : c + 12 - o + CH, :] * taps[o]
                wide_ref[c : c + CH, cols] = total
                mine = m_ref[slot, j, c + 8 : c + 8 + CH, :]
                if j == 0:
                    s1_ref[c : c + CH, :] = total
                    s2_ref[c : c + CH, :] = total * mine
                else:
                    s1_ref[c : c + CH, :] += total
                    s2_ref[c : c + CH, :] += total * mine
        within(s, "b")
        right_ref[0:8, :] = jnp.zeros((8, HALF), f32)
        right_ref[8 + SEQ : PAD, :] = jnp.zeros((8, HALF), f32)
        for c in range(0, SEQ, CH):
            part = at(s, c, CH)
            rstd = rstd_ref[part, 2:3]
            m1 = jnp.sum(s1_ref[c : c + CH, :], axis=-1, keepdims=True) * (rstd / FF)
            m2 = jnp.sum(s2_ref[c : c + CH, :], axis=-1, keepdims=True) * (rstd / FF)
            for j in range(16):
                cols = slice(128 * j, 128 * j + 128)
                g_h = wide_ref[c : c + CH, cols] * rstd - m1 - m_ref[slot, j, c + 8 : c + 8 + CH, :] * m2
                gleft_ref[part, cols] = (g_h * dgl_ref[part, cols].astype(f32)).astype(bf)
                if j < 2:
                    right_ref[8 + c : 8 + c + CH, cols] = g_h * dgr_ref[part, cols].astype(f32)

        @pl.when(s + 2 < sents)
        def _():
            fetch_m(s + 2).start()

        for k in range(3):
            gr_refs[k][rows, :] = right_ref[9 - k : 9 - k + SEQ, :].astype(bf)
        within(s, "c")

    loop("w", 0, sents, wide, "abc")
    for i in range(4):
        put(g_ref, grid, tn(b_ref[...], gleft_ref[:, 512 * i : 512 * i + 512]), starts[("left", "left2")[i // 2]] + i % 2 * 2 * share, share, False)
        point(f"l{i}")
    for k in range(3):
        put(g_ref, grid, tn(b_ref[...], gr_refs[k][...]), starts["conv"] + k * share, share, False)
    point("c")

    def inputs(s, within):
        gains = gains_ref[...].astype(f32)
        rows = at(s, 0, SEQ)
        for n in range(2):
            cols = slice(256 * n, 256 * n + 256)
            g_b = nt(gleft_ref[rows, :], wleft[cols, :])
            for k in range(3):
                g_b = g_b + nt(gr_refs[k][rows, :], wconv[k, cols, :])
            wide_ref[:, cols] = g_b
        inverse = 1.0 / gains[1:2]
        for c in range(0, SEQ, CH):
            part = at(s, c, CH)
            g_b = wide_ref[c : c + CH, 0:D]
            low = b_ref[part, :].astype(f32)
            gain_ref[8:16, :] += fold8(g_b * low)
            g_glu = conv_ref[part, :] + norm_back(g_b, low, gains[1:2], inverse, rstd_ref[part, 1:2])
            conv_ref[part, :] = g_glu
            gg_ref[part, 0:D] = (g_glu * sig_ref[part, :].astype(f32)).astype(bf)
            gg_ref[part, D : 2 * D] = (g_glu * u_ref[part, :].astype(f32)).astype(bf)

    def inputs_end(s, within):
        gains = gains_ref[...].astype(f32)
        rows = at(s, 0, SEQ)
        for n in range(2):
            cols = slice(256 * n, 256 * n + 256)
            wide_ref[:, cols] = nt(gg_ref[rows, 0 : 2 * D], wglu[cols, :])
        inverse = 1.0 / gains[0:1]
        for c in range(0, SEQ, CH):
            part = at(s, c, CH)
            g_a = wide_ref[c : c + CH, 0:D]
            low = a_ref[part, :].astype(f32)
            gain_ref[0:8, :] += fold8(g_a * low)
            conv_ref[part, :] += norm_back(g_a, low, gains[0:1], inverse, rstd_ref[part, 0:1])

    wait("wleft", "wconv", "wglu")
    loop("i", 0, sents, inputs)
    for i in range(2):
        put(g_ref, grid, tn(a_ref[...], gg_ref[:, 512 * i : 512 * i + 512]), starts[("glu", "glu1")[i]], share, False)
        point(f"g{i}")
    def tap_sums(i, within):
        s = sents - 1 - i

        @pl.when(i >= 2)
        def _():
            fetch_m(s).wait()

        @pl.when(i >= 1)
        def _():
            g_depth(at(s, 0, SEQ))

        for j in range(16):
            cols = slice(128 * j, 128 * j + 128)
            lines = [taps_ref[o, :, cols] for o in range(9)]
            for c in range(0, SEQ, CH):
                back = gd_ref[j, c + 8 : c + 8 + CH, :]
                for o in range(9):
                    lines[o] = lines[o] + fold8(m_ref[s % 2, j, c + 4 + o : c + 4 + o + CH, :] * back)
            for o in range(9):
                taps_ref[o, :, cols] = lines[o]

        @pl.when(s >= 2)
        def _():
            fetch_m(s - 2).start()

    loop("r", 0, sents, tap_sums)
    wide_gain = one_row(wg_ref)
    total = jnp.zeros((1, FF), f32)
    for o in range(9):
        lines = jnp.sum(taps_ref[o], axis=0, keepdims=True)
        total = total + lines * wdepth[o : o + 1, :].astype(f32)
        early_ref[0, o : o + 1, :] = lines * wide_gain
    early_ref[0, 9:10, :] = total
    early_ref[0, 10:16, :] = jnp.zeros((6, FF), f32)

    def gain_row(i):
        return jnp.sum(gain_ref[8 * i : 8 * i + 8, :], axis=0, keepdims=True) / gains_ref[i : i + 1, :].astype(f32)

    early_ref[0, 10:11, 0:D] = gain_row(2)
    early_ref[0, 11:12, 0:D] = gain_row(3)
    sums.early_next(5, early_ref, early_got)
    point("t")

    loop("e", 0, sents, inputs_end)
    leave = pltpu.make_async_copy(conv_ref, xgrad_far, fetch_sems.at[len(order) + 2])
    leave.start()
    late_ref[3] = jnp.zeros((8, D), f32)
    late_ref[3, 0:1, :] = gain_row(0)
    late_ref[3, 1:2, :] = gain_row(1)
    sums.small_send(2, 3, late_ref, late_got)
    point("z")
    for _ in range(sums.STAGES + 1):
        sums.advance(*range(len(groups)))
    for i in small_step:
        while small_step[i] >= 0:
            do([(i, small_step[i])])
            small_step[i] -= 1
    ends = (final_ref, final_far), (early_ref.at[2], early_far), (late_ref.at[4], late_far)
    ends = [pltpu.make_async_copy(*pair, fetch_sems.at[len(order) + 3 + k]) for k, pair in enumerate(ends)]
    for copy in ends:
        copy.start()
    sums.finish()
    sums.early_sent(early_ref, early_got)
    leave.wait()
    for copy in ends:
        copy.wait()


def coordinates(ys):
    dp, head = lax.axis_index("dp"), lax.axis_index("head")
    return dp // ys, dp % ys, head // 2, head % 2


def device(ys, z, y, x, c):
    return (z * ys + y, x * 2 + c)


def rows16(first, size):
    return pl.ds(pl.multiple_of(first, 16), size)


def split_of(size, xs):
    half = size // 2
    first = (half // (32 * xs)) * 16 * xs
    return half, first, half - first


class Sums:
    STAGES = 5

    def __init__(self, grid, xs, groups, g_ref, final_ref, recv, send_sems, recv_sems):
        self.zs, self.ys = grid
        self.xs = xs
        self.sizes = (*grid, xs, 2)
        self.groups = groups
        self.g, self.final = g_ref, final_ref
        self.recv = recv
        self.send_sems, self.recv_sems = send_sems, recv_sems
        self.place = coordinates(self.ys)
        self.stage = [-1] * len(groups)
        self.small = []

    def peers(self, axis):
        size = self.sizes[axis]
        for step in range(1, size):
            to = list(self.place)
            to[axis] = lax.rem(to[axis] + step, size)
            yield step - 1, to[axis], device(self.ys, *to)

    def heads(self):
        z, y, x, c = self.place
        for dx in range(self.xs):
            for dc in range(2):
                if dx or dc:
                    yield device(self.ys, z, y, lax.rem(x + dx, self.xs), lax.rem(c + dc, 2))

    def greet(self, heads=True):
        others = [to for axis in range(2 if heads else 4) for _, _, to in self.peers(axis)]
        others += self.heads() if heads else []
        for to in others:
            pl.semaphore_signal(pltpu.get_barrier_semaphore(), inc=1, device_id=to, device_id_type=MESH)
        return len(others)

    def greeted(self, total):
        pl.semaphore_wait(pltpu.get_barrier_semaphore(), total)

    def core_first(self, i):
        return (self.groups[i][0] - (self.groups[3][0] if i > 2 else 0)) // 2

    def a_first(self, i):
        return sum(split_of(size, self.xs)[1] // self.xs for _, size in self.groups[:i])

    def b_first(self, i):
        return sum(split_of(size, self.xs)[2] for _, size in self.groups[:i])

    def rows(self, i):
        first, size = self.groups[i]
        half, na, nb = split_of(size, self.xs)
        mine = first + self.place[3] * half
        return first, half, mine, na, na // self.xs, mine + na, nb

    def plan(self, stage, i):
        z, y, x, c = self.place
        first, half, mine, na, part, b_row, nb = self.rows(i)
        g, recv, final = self.g, self.recv, self.final
        a_in, b_in = pl.ds(self.a_first(i), part), pl.ds(self.b_first(i), nb)
        a_rows, b_rows = rows16(mine + x * part, part), rows16(b_row, nb)
        axis_a, axis_b = ((None, 3), (2, 1), (1, 0), (0, 2), (None, 3))[stage]
        copies_a, copies_b = [], []
        for slot, other, to in self.peers(axis_b) if axis_b is not None else ():
            if stage == 0:
                source = g.at[:, :, rows16(first + other * half, half), :]
                target = recv["core"].at[:, :, pl.ds(self.core_first(i), half), :]
            elif stage == 1:
                source, target = g.at[:, other, b_rows, :], recv["b1"].at[slot, :, b_in, :]
            elif stage == 2:
                source, target = g.at[other, y, b_rows, :], recv["b2"].at[slot, b_in, :]
            elif stage == 3:
                source, target = g.at[z, y, b_rows, :], recv["b3"].at[slot, b_in, :]
            else:
                source, target = final.at[b_rows, :], final.at[b_rows, :]
            copies_b.append((source, target, to))
        for slot, other, to in self.peers(axis_a) if axis_a is not None and na else ():
            if stage == 1:
                source, target = g.at[:, :, rows16(mine + other * part, part), :], recv["a1"].at[slot, :, :, a_in, :]
            elif stage == 2:
                source, target = g.at[:, other, a_rows, :], recv["a2"].at[slot, :, a_in, :]
            else:
                source, target = g.at[other, y, a_rows, :], recv["a3"].at[slot, a_in, :]
            copies_a.append((source, target, to))
        if stage == 4 and na:
            copies_a = [(final.at[a_rows, :], final.at[a_rows, :], to) for to in self.heads()]
        return copies_b, copies_a

    def copies(self, stage, i):
        counts = self.counts(self.sizes)
        first = i * sum(map(sum, counts)) + sum(map(sum, counts[:stage]))
        copies_b, copies_a = self.plan(stage, i)
        made = []
        for copies, extra in ((copies_b, 0), (copies_a, counts[stage][0])):
            for n, (source, target, to) in enumerate(copies):
                index = first + extra + n
                made.append(
                    pltpu.make_async_remote_copy(
                        src_ref=source,
                        dst_ref=target,
                        send_sem=self.send_sems.at[index],
                        recv_sem=self.recv_sems.at[index],
                        device_id=to,
                        device_id_type=MESH,
                    )
                )
        return made

    @staticmethod
    def counts(sizes):
        z, y, x, _ = (size - 1 for size in sizes)
        return ((1, 0), (y, x), (z, y), (x, z), (1, 2 * x + 1))

    @staticmethod
    def semaphores(grid, xs, groups):
        sizes = (*grid, xs, 2)
        return len(groups) * sum(map(sum, Sums.counts(sizes))) + 12 * (max(sizes) - 1) + sum(sizes) + 2 * xs

    def claim(self, *groups):
        steps = []
        for i in groups:
            if self.stage[i] < self.STAGES:
                steps.append((i, self.stage[i]))
                self.stage[i] += 1
        return steps

    def do(self, steps):
        for i, stage in steps:
            if stage >= 0:
                for copy in self.copies(stage, i):
                    copy.wait_recv()
                self.add(stage, i)
            if stage + 1 < self.STAGES:
                for copy in self.copies(stage + 1, i):
                    copy.start()

    def advance(self, *groups):
        self.do(self.claim(*groups))

    def over(self, i):
        return self.stage[i] == self.STAGES

    def add(self, stage, i):
        z, y, x, c = self.place
        first, half, mine, na, part, b_row, nb = self.rows(i)
        g, recv = self.g, self.recv
        a_in, b_in = pl.ds(self.a_first(i), part), pl.ds(self.b_first(i), nb)
        a_rows, b_rows = rows16(mine + x * part, part), rows16(b_row, nb)

        def total(mine, got):
            value = mine.astype(f32)
            for other in got:
                value = value + other.astype(f32)
            return value.astype(bf)

        if stage == 0:

            def core(block, carry):
                zb, yb = block // self.ys, block % self.ys
                g[zb, yb, rows16(mine, half), :] += recv["core"][zb, yb, pl.ds(self.core_first(i), half), :]
                return carry

            lax.fori_loop(0, self.zs * self.ys, core, 0)
        elif stage == 1:

            def one(zb, carry):
                got = [recv["b1"][slot, zb, b_in, :] for slot in range(self.ys - 1)]
                g[zb, y, b_rows, :] = total(g[zb, y, b_rows, :], got)
                for yb in range(self.ys) if na else ():
                    got = [recv["a1"][slot, zb, yb, a_in, :] for slot in range(self.xs - 1)]
                    g[zb, yb, a_rows, :] = total(g[zb, yb, a_rows, :], got)
                return carry

            lax.fori_loop(0, self.zs, one, 0)
        elif stage == 2:
            g[z, y, b_rows, :] = total(g[z, y, b_rows, :], [recv["b2"][slot, b_in, :] for slot in range(self.zs - 1)])
            if na:

                def two(zb, carry):
                    got = [recv["a2"][slot, zb, a_in, :] for slot in range(self.ys - 1)]
                    g[zb, y, a_rows, :] = total(g[zb, y, a_rows, :], got)
                    return carry

                lax.fori_loop(0, self.zs, two, 0)
        elif stage == 3:
            got = [recv["b3"][slot, b_in, :] for slot in range(self.xs - 1)]
            self.final[b_rows, :] = total(g[z, y, b_rows, :], got)
            if na:
                got = [recv["a3"][slot, a_in, :] for slot in range(self.zs - 1)]
                self.final[a_rows, :] = total(g[z, y, a_rows, :], got)

    def small_copies(self, k, axis, held, got):
        most = max(self.sizes) - 1
        base = len(self.groups) * sum(map(sum, self.counts(self.sizes)))
        made = []
        for slot, other, to in self.peers(axis):
            index = base + (k * 4 + axis) * most + slot
            made.append(
                pltpu.make_async_remote_copy(
                    src_ref=held.at[axis],
                    dst_ref=got.at[self.got_first(axis) + slot],
                    send_sem=self.send_sems.at[index],
                    recv_sem=self.recv_sems.at[index],
                    device_id=to,
                    device_id_type=MESH,
                )
            )
        return made

    def got_first(self, axis):
        return sum(size - 1 for size in self.sizes[:axis])

    def small_send(self, k, axis, held, got):
        self.small.append((k, axis, held, got))
        for copy in self.small_copies(k, axis, held, got):
            copy.start()

    def small_add(self, k, axis, held, got):
        for copy in self.small_copies(k, axis, held, got):
            copy.wait_recv()
        size, me = self.sizes[axis], self.place[axis]
        total = None
        for n in range(size):
            value = held[axis]
            for slot in range(size - 1):
                value = jnp.where(lax.rem(me - slot - 1 + size, size) == n, got[self.got_first(axis) + slot], value)
            total = value if total is None else total + value
        held[axis - 1 if axis else 4] = total

    def early_plan(self, step, held, got):
        z, y, x, c = self.place
        half = held.shape[2] // 2
        part = half // self.xs
        mine = pl.ds(pl.multiple_of(c * half + x * part, 128), part)
        if step == 4:
            return [
                (held.at[0, :, pl.ds(pl.multiple_of(other * half, 128), half)], got.at[0], to)
                for _, other, to in self.peers(3)
            ]
        if step == 3:
            return [
                (
                    held.at[0, :, pl.ds(pl.multiple_of(c * half + other * part, 128), part)],
                    got.at[1 + slot, :, pl.ds(0, part)],
                    to,
                )
                for slot, other, to in self.peers(2)
            ]
        if step == 0:
            return [(held.at[2, :, mine], held.at[2, :, mine], to) for to in self.heads()]
        first = self.xs + (0 if step == 2 else self.ys - 1)
        return [
            (held.at[2 - step, :, mine], got.at[first + slot, :, pl.ds(0, part)], to)
            for slot, _, to in self.peers(step - 1)
        ]

    def early_copies(self, step, held, got):
        counts = (2 * self.xs - 1, self.zs - 1, self.ys - 1, self.xs - 1, 1)
        base = len(self.groups) * sum(map(sum, self.counts(self.sizes))) + 12 * (max(self.sizes) - 1) + sum(counts[:step])
        return [
            pltpu.make_async_remote_copy(
                src_ref=source,
                dst_ref=target,
                send_sem=self.send_sems.at[base + n],
                recv_sem=self.recv_sems.at[base + n],
                device_id=to,
                device_id_type=MESH,
            )
            for n, (source, target, to) in enumerate(self.early_plan(step, held, got))
        ]

    def early_next(self, step, held, got):
        z, y, x, c = self.place
        half = held.shape[2] // 2
        part = half // self.xs
        mine = pl.ds(pl.multiple_of(c * half + x * part, 128), part)
        if step < 5:
            for copy in self.early_copies(step, held, got):
                copy.wait_recv()
        if step == 4:
            held[0, :, pl.ds(pl.multiple_of(c * half, 128), half)] += got[0]
        elif step == 3:
            for slot in range(self.xs - 1):
                held[0, :, mine] += got[1 + slot, :, 0:part]
        elif step in (1, 2):
            axis = step - 1
            size, me = self.sizes[axis], self.place[axis]
            first = self.xs + (0 if step == 2 else self.ys - 1)
            total = None
            for n in range(size):
                value = held[2 - step, :, mine]
                for slot in range(size - 1):
                    value = jnp.where(lax.rem(me - slot - 1 + size, size) == n, got[first + slot, :, 0:part], value)
                total = value if total is None else total + value
            held[3 - step, :, mine] = total
        if step:
            for copy in self.early_copies(step - 1, held, got):
                copy.start()

    def early_sent(self, held, got):
        for step in range(5):
            for copy in self.early_copies(step, held, got):
                copy.wait_send()

    def small_next(self, k, axis, held, got):
        self.small_add(k, axis, held, got)
        if axis:
            self.small_send(k, axis - 1, held, got)

    def finish(self):
        for i in range(len(self.groups)):
            for stage in range(self.STAGES):
                for copy in self.copies(stage, i):
                    copy.wait_send()
        for small in self.small:
            for copy in self.small_copies(*small):
                copy.wait_send()


def recv_shapes(grid, xs, groups, height):
    zs, ys = grid
    na = sum(split_of(size, xs)[1] for _, size in groups) // xs
    nb = sum(split_of(size, xs)[2] for _, size in groups)
    na = max(na, 16)
    return {
        "core": (zs, ys, max(groups[3][0], height - groups[3][0]) // 2, 256),
        "a1": (xs - 1, zs, ys, na, 256),
        "b1": (ys - 1, zs, nb, 256),
        "a2": (ys - 1, zs, na, 256),
        "b2": (zs - 1, nb, 256),
        "a3": (zs - 1, na, 256),
        "b3": (xs - 1, nb, 256),
    }


SMALL = 16


def last_kernel(share, wide_share, final_far, early_far, late_far, xgrad_in, cell_in, *refs):
    far, refs = refs[:13], refs[13:]
    near, (final_ref, early_ref, late_ref, in_sems, out_sems) = refs[:13], refs[13:]
    rows = xgrad_in.shape[0]
    step = rows // 3
    arriving = [
        pltpu.make_async_copy(source, target, in_sems.at[k])
        for k, (source, target) in enumerate(
            ((final_far, final_ref), (early_far, early_ref), (late_far, late_ref), (cell_in, near[1]))
        )
    ]
    leaving = [pltpu.make_async_copy(near[k], far[k], out_sems.at[k]) for k in range(1, 13)]
    parts = [pl.ds(step * k, step) for k in range(3)]
    inward = [pltpu.make_async_copy(xgrad_in.at[p, :], near[0].at[p, :], in_sems.at[4 + k]) for k, p in enumerate(parts)]
    outward = [pltpu.make_async_copy(near[0].at[p, :], far[0].at[p, :], out_sems.at[13 + k]) for k, p in enumerate(parts)]
    for copy in (arriving[0], *inward, *arriving[1:]):
        copy.start()
    starts, _, _ = offsets(share, wide_share)

    def spread(k, name, tiles, size):
        for n in range(tiles):
            part, m = name, n
            if name in ("left", "glu") and n >= tiles // 2:
                part, m = ("left2" if name == "left" else "glu1"), n - tiles // 2
            first = starts[part] + m * size
            near[k][:, 256 * n : 256 * n + 256] = final_ref[first : first + size, :].astype(f32)
        leaving[k - 1].start()

    arriving[0].wait()
    spread(5, "left", 8, share)
    spread(11, "up", 8, share)
    for a, b in zip(inward, outward):
        a.wait()
        b.start()
    spread(12, "down", 2, wide_share)
    spread(9, "qkv", 6, share)
    arriving[3].wait()
    leaving[0].start()
    spread(4, "glu", 4, share)
    spread(8, "point", 1, wide_share)
    for k in range(3):
        first = starts["conv"] + k * share
        near[6][k] = final_ref[first : first + share, :].astype(f32)
    leaving[5].start()
    spread(10, "out", 2, share)
    arriving[1].wait()
    arriving[2].wait()
    near[2][0:2, :] = late_ref[0:2, :]
    near[2][2:4, :] = early_ref[10:12, 0:D]
    near[3][...] = early_ref[9:10, :]
    near[7][...] = early_ref[0:9, :]
    for k in (2, 3, 7):
        leaving[k - 1].start()
    for copy in (*leaving, *outward):
        copy.wait()


def local(
    grid,
    xs,
    cell_input,
    lengths,
    pair_ids,
    cotangent,
    norm_gains,
    wide_gain,
    w_glu,
    w_left,
    w_conv3,
    w_depth,
    w_point,
    w_qkv,
    w_out,
    w_up,
    w_down,
):
    zs, ys = grid
    dp = zs * ys
    share, wide_share = 512 // dp, 2048 // dp
    rows = cell_input.shape[0]
    sents = lengths.shape[0]
    starts, groups, height = offsets(share, wide_share)
    wg = wide_gain.reshape(FF // 128, 128)
    shape = jax.ShapeDtypeStruct
    params = pltpu.CompilerParams(vmem_limit_bytes=62 << 20)
    kept = kept_shapes(sents)
    anywhere = pl.BlockSpec(memory_space=pl.ANY)
    most = zs + ys + xs - 2
    counting = Sums.semaphores(grid, xs, ())
    front = pl.pallas_call(
        functools.partial(front_kernel, sents, grid, xs),
        out_shape=[shape((rows, D), bf)] + list(kept.values()),
        in_specs=[smem(), smem(), vmem(), anywhere] + [vmem()] * 2 + [anywhere] * 3 + [vmem()] + [anywhere] * 5,
        out_specs=[anywhere] * (1 + len(kept)),
        scratch_shapes=[pltpu.VMEM(v, bf) for v in (*WEIGHTS, (rows, D))]
        + [pltpu.SemaphoreType.DMA((9,)), pltpu.VMEM((rows, D), bf)]
        + [pltpu.VMEM(v.shape, v.dtype) for v in kept.values()]
        + [
            pltpu.SemaphoreType.DMA((len(kept) + 1, sents)),
            pltpu.VMEM((16, FF), f32),
            pltpu.VMEM((SEQ, D), f32),
            pltpu.VMEM((PAD, D), f32),
            pltpu.VMEM((SEQ, FF), f32),
            pltpu.VMEM((SEQ, HALF), f32),
            pltpu.VMEM((SEQ, 3 * D), bf),
            pltpu.SemaphoreType.DMA((counting,)),
            pltpu.SemaphoreType.DMA((counting,)),
            pltpu.VMEM((5, 8, 128), f32),
            pltpu.VMEM((most, 8, 128), f32),
            pltpu.VMEM((sents, 8, 128), f32),
        ],
        compiler_params=pltpu.CompilerParams(vmem_limit_bytes=62 << 20, collective_id=1, has_side_effects=True),
        name="front",
    )(lengths, pair_ids, cell_input, cotangent, norm_gains, wg, w_glu, w_left, w_conv3, w_depth, w_point, w_qkv, w_out, w_up, w_down)
    cell, arrays = front[0], front[1:]
    recv = recv_shapes(grid, xs, groups, height)
    semaphores = Sums.semaphores(grid, xs, groups)
    input_grad, final, early, late = pl.pallas_call(
        functools.partial(back_kernel, sents, grid, xs, tuple(recv)),
        out_shape=[shape((rows, D), f32), shape((height, 256), bf), shape((SMALL, FF), f32), shape((8, D), f32)],
        in_specs=[vmem()] * 2 + [anywhere] * 3 + [vmem()] + [anywhere] * (2 + len(kept)),
        out_specs=[anywhere] * 4,
        scratch_shapes=[pltpu.VMEM(v, bf) for v in (*recv.values(), *WEIGHTS[:5])]
        + [
            pltpu.SemaphoreType.DMA((40,)),
            pltpu.SemaphoreType.DMA((semaphores,)),
            pltpu.SemaphoreType.DMA((semaphores,)),
            pltpu.VMEM((zs, ys, height, 256), bf),
            pltpu.VMEM((height, 256), bf),
            pltpu.VMEM((3, SMALL, FF), f32),
            pltpu.VMEM((most, SMALL, FF // 2), f32),
            pltpu.VMEM((5, 8, D), f32),
            pltpu.VMEM((most, 8, D), f32),
            pltpu.VMEM((rows, FF), bf),
            pltpu.VMEM((rows, FF), bf),
            pltpu.VMEM((rows, 3 * D), bf),
            pltpu.VMEM((sents, HEADS, SEQ, SEQ), bf),
            pltpu.VMEM((rows, D), f32),
            pltpu.VMEM((rows, D), bf),
            pltpu.VMEM((rows, D), bf),
            pltpu.VMEM((rows, D), bf),
            pltpu.VMEM((D, rows), bf),
            pltpu.VMEM((D, rows), bf),
            pltpu.VMEM((3 * D, rows), bf),
            pltpu.VMEM((rows, HALF), bf),
            pltpu.VMEM((rows, 8), f32),
            pltpu.VMEM((sents * 8, D), f32),
            pltpu.VMEM((2, 16, PAD, 128), f32),
            pltpu.VMEM((16, FF), f32),
            pltpu.VMEM((3 * D, SEQ), bf),
            pltpu.VMEM((16, PAD, 128), f32),
            pltpu.VMEM((SEQ, FF), f32),
            pltpu.VMEM((9, 8, FF), f32),
            pltpu.VMEM((SEQ, 128), f32),
            pltpu.VMEM((SEQ, 128), f32),
            pltpu.VMEM((PAD, HALF), f32),
            pltpu.VMEM((32, D), f32),
        ],
        compiler_params=pltpu.CompilerParams(vmem_limit_bytes=63 << 20, collective_id=0, has_side_effects=True),
        name="back",
    )(norm_gains, wg, w_glu, w_left, w_conv3, w_depth, w_point, w_qkv, *arrays)
    results = [
        shape((rows, D), f32),
        shape((rows, D), bf),
        shape((4, D), f32),
        shape((1, FF), f32),
        shape((share, 2 * D), f32),
        shape((share, FF), f32),
        shape((3, share, HALF), f32),
        shape((9, FF), f32),
        shape((wide_share, HALF), f32),
        shape((share, 3 * D), f32),
        shape((share, D), f32),
        shape((share, FF), f32),
        shape((wide_share, D), f32),
    ]
    input_grad, cell_output, norms, gain, glu, left, conv, depth, point, qkv, out, up, down = pl.pallas_call(
        functools.partial(last_kernel, share, wide_share),
        out_shape=results,
        in_specs=[anywhere] * 5,
        out_specs=[anywhere] * 13,
        scratch_shapes=[pltpu.VMEM(v.shape, v.dtype) for v in results]
        + [
            pltpu.VMEM((height, 256), bf),
            pltpu.VMEM((SMALL, FF), f32),
            pltpu.VMEM((8, D), f32),
            pltpu.SemaphoreType.DMA((8,)),
            pltpu.SemaphoreType.DMA((16,)),
        ],
        compiler_params=params,
        name="last",
    )(final, early, late, input_grad, cell)
    return cell_output, input_grad, norms, gain.reshape(FF), glu, left, conv, depth, point, qkv, out, up, down


def solution(mesh):
    dp, head = mesh.shape["dp"], mesh.shape["head"]
    ys = 2 ** ((dp.bit_length() - 1) // 2)
    grid = (dp // ys, ys)
    xs = head // 2
    row = P(("dp", "head"), None)
    in_specs = (row, P(("dp", "head")), P(("dp", "head")), row) + (P(),) * 11
    share = P("dp", None)
    out_specs = (row, row, P(), P(), share, share, P(None, "dp", None), P(), share, share, share, share, share)
    return jax.shard_map(
        functools.partial(local, grid, xs), mesh=mesh, in_specs=in_specs, out_specs=out_specs, check_vma=False
    )
```

```python
import functools

import jax
import jax.numpy as jnp
from jax import lax
from jax.experimental import pallas as pl
from jax.experimental.pallas import tpu as pltpu
from jax.sharding import PartitionSpec as P

HEADS = 8
DH = 64
SEQ = 256
PAIRS = 4
D = 512
FF = 2048
HALF = 256
PAD = SEQ + 16
EPS = 1e-05
MESH = pl.DeviceIdType.MESH
bf = jnp.bfloat16
f32 = jnp.float32
GELU_A = 0.7978845608028654
GELU_B = 0.7978845608028654 * 0.044715
CH = 32


def nn(a, b):
    return lax.dot_general(a, b, (((1,), (0,)), ((), ())), preferred_element_type=f32)


def nt(a, b):
    return lax.dot_general(a, b, (((1,), (1,)), ((), ())), preferred_element_type=f32)


def tn(a, b):
    return lax.dot_general(a, b, (((0,), (0,)), ((), ())), preferred_element_type=f32)


def gelu_both(v):
    square = v * v
    t = jnp.tanh(v * (GELU_A + GELU_B * square))
    half = 0.5 + 0.5 * t
    slope = half + (0.5 * v) * (1.0 - t * t) * (GELU_A + (3.0 * GELU_B) * square)
    return v * half, slope


def sigmoid(v):
    return 0.5 + 0.5 * jnp.tanh(0.5 * v)


def fold8(v):
    total = v[0:8]
    for i in range(1, v.shape[0] // 8):
        total = total + v[8 * i : 8 * i + 8]
    return total


def norm(v):
    centred = v - jnp.mean(v, axis=-1, keepdims=True)
    rstd = lax.rsqrt(jnp.mean(centred * centred, axis=-1, keepdims=True) + EPS)
    return centred, rstd


def norm_back(g, low, gain, inverse, rstd):
    gy = g * gain
    m1 = jnp.mean(gy, axis=-1, keepdims=True)
    m2 = jnp.mean(g * low, axis=-1, keepdims=True)
    return rstd * (gy - m1 - (low * inverse) * m2)


def at(s, first, size):
    return pl.ds(pl.multiple_of(s * SEQ + first, size), size)


def one_row(ref):
    return jnp.concatenate([ref[j : j + 1, :] for j in range(ref.shape[0])], axis=1).astype(f32)


def row_of(first, size):
    return first + lax.broadcasted_iota(jnp.int32, (size, 1), 0)


KEPT = (
    "a", "b", "e", "f", "rstd", "sig", "u", "dgl", "dgr", "m",
    "depth", "qkvt", "pt", "mixt", "up", "gup", "ga", "gmixt", "gain_f", "gl", "gal",
)


def kept_shapes(sents):
    rows = sents * SEQ
    shape = jax.ShapeDtypeStruct
    return {
        "a": shape((rows, D), bf),
        "b": shape((rows, D), bf),
        "e": shape((rows, D), bf),
        "f": shape((rows, D), bf),
        "rstd": shape((rows, 8), f32),
        "sig": shape((rows, D), bf),
        "u": shape((rows, D), bf),
        "dgl": shape((rows, FF), bf),
        "dgr": shape((rows, HALF), bf),
        "m": shape((sents, 16, PAD, 128), f32),
        "depth": shape((8, sents, SEQ, 256), bf),
        "qkvt": shape((3 * D, rows), bf),
        "pt": shape((sents, HEADS, SEQ, SEQ), bf),
        "mixt": shape((D, rows), bf),
        "up": shape((rows, FF), bf),
        "gup": shape((rows, FF), bf),
        "ga": shape((rows, D), f32),
        "gmixt": shape((D, rows), bf),
        "gain_f": shape((sents * 8, D), f32),
        "gl": shape((rows, D), bf),
        "gal": shape((rows, D), bf),
    }


def part_of(name, s):
    if name in ("m", "pt"):
        return (s,)
    if name == "depth":
        return (slice(None), s)
    if name in ("qkvt", "mixt", "gmixt"):
        return (slice(None), pl.ds(pl.multiple_of(s * SEQ, SEQ), SEQ))
    if name == "gain_f":
        return (pl.ds(pl.multiple_of(s * 8, 8), 8),)
    return (pl.ds(pl.multiple_of(s * SEQ, SEQ), SEQ),)


WEIGHTS = ((D, 2 * D), (D, FF), (3, D, HALF), (FF, HALF), (D, 3 * D), (D, D), (D, FF), (FF, D))


def front_kernel(
    sents,
    grid,
    xs,
    len_ref,
    pair_ref,
    x_ref,
    cot_ref,
    gains_ref,
    wg_ref,
    wglu,
    wleft,
    wconv,
    wdepth,
    wpoint,
    wqkv,
    wout,
    wup,
    wdown,
    out_far,
    *refs,
):
    far, refs = dict(zip(KEPT, refs)), refs[len(KEPT) :]
    held, refs = refs[: len(WEIGHTS) + 1], refs[len(WEIGHTS) + 1 :]
    weights = (wglu, wleft, wconv, wpoint, wqkv, wout, wup, wdown, cot_ref)
    load_sems, out_ref, refs = refs[0], refs[1], refs[2:]
    load = [pltpu.make_async_copy(w, h, load_sems.at[k]) for k, (w, h) in enumerate(zip(weights, held))]
    for copy in load[:3]:
        copy.start()
    wglu, wleft, wconv, wpoint, wqkv, wout, wup, wdown, cot_ref = held
    near, refs = dict(zip(KEPT, refs)), refs[len(KEPT) :]
    ship_sems, wp_ref, xf_ref, bs_ref, wide_ref, sep_ref, qkv_ref = refs[:7]
    send_sems, recv_sems, count_ref, count_got, fac_ref = refs[7:]
    sums = Sums(grid, xs, (), None, None, None, send_sems, recv_sems)
    others = sums.greet(False)
    lane = lax.broadcasted_iota(jnp.int32, (8, 128), 1)
    counts = jnp.zeros((8, 128), f32)
    for s in range(sents):
        counts = counts + jnp.where(lane == pair_ref[s], len_ref[s].astype(f32), 0.0)
    count_ref[3] = counts

    def count_next(axis):
        if axis < 4:
            sums.small_add(0, axis, count_ref, count_got)
        else:
            sums.greeted(others)
        if axis:
            for copy in sums.small_copies(0, axis - 1, count_ref, count_got):
                copy.start()
        else:
            counts = count_ref[4]
            total = jnp.sum(counts, axis=1, keepdims=True)
            for k in range(sents):
                mine = jnp.sum(jnp.where(lane == pair_ref[k], counts, 0.0), axis=1, keepdims=True)
                fac_ref[k] = jnp.broadcast_to(total / (PAIRS * mine), (8, 128))

    (a_ref, b_ref, e_ref, f_ref, rstd_ref, sig_ref, u_ref, dgl_ref, dgr_ref, m_ref) = [near[n] for n in KEPT[:10]]
    (depth_ref, qkvt_ref, pt_ref, mixt_ref, up_ref, gup_ref, ga_ref, gmixt_ref, gain_f_ref, gl_ref, gal_ref) = [near[n] for n in KEPT[10:]]

    def shipment(name, s):
        k = KEPT.index(name)
        where = part_of(name, s)
        return pltpu.make_async_copy(near[name].at[where], far[name].at[where], ship_sems.at[k, s])

    def leave(s):
        return pltpu.make_async_copy(out_ref.at[at(s, 0, SEQ), :], out_far.at[at(s, 0, SEQ), :], ship_sems.at[len(KEPT), s])

    def ship(s, *names):
        for name in names:
            shipment(name, s).start()

    wp_ref[0:9, :] = wdepth[...].astype(f32) * one_row(wg_ref)
    gain_f_ref[...] = jnp.zeros_like(gain_f_ref)
    zero8 = jnp.zeros((8, 128), f32)

    def sentence(s, carry):
        length = len_ref[s]

        def loaded(*which, then=(), axis=None):
            @pl.when(s == 0)
            def _():
                for k in which:
                    load[k].wait()
                for k in then:
                    load[k].start()
                if axis is not None:
                    count_next(axis)

        gains = gains_ref[...].astype(f32)
        rows = at(s, 0, SEQ)
        for c in range(0, SEQ, CH):
            cen, rstd = norm(x_ref[at(s, c, CH), :].astype(f32))
            a_ref[at(s, c, CH), :] = (cen * rstd * gains[0:1]).astype(bf)
            rstd_ref[at(s, c, CH), 0:1] = rstd
        a_low = a_ref[rows, :]
        loaded(0, then=(3, 4), axis=4)
        for n in range(2):
            cols = slice(256 * n, 256 * n + 256)
            gcols = slice(512 + 256 * n, 768 + 256 * n)
            value = nn(a_low, wglu[:, cols])
            gate = nn(a_low, wglu[:, gcols])
            for c in range(0, SEQ, CH):
                sig = sigmoid(gate[c : c + CH])
                mixed = value[c : c + CH] * sig
                xf_ref[c : c + CH, cols] = x_ref[at(s, c, CH), cols].astype(f32) + mixed
                sig_ref[at(s, c, CH), cols] = sig.astype(bf)
                u_ref[at(s, c, CH), cols] = (mixed * (1.0 - sig)).astype(bf)
        ship(s, "a", "sig", "u")
        for c in range(0, SEQ, CH):
            cen, rstd = norm(xf_ref[c : c + CH, :])
            rstd = jnp.where(row_of(c, CH) < length, rstd, 0.0)
            b_low = cen * rstd * gains[1:2]
            b_ref[at(s, c, CH), :] = b_low.astype(bf)
            rstd_ref[at(s, c, CH), 1:2] = rstd
            bs_ref[8 + c : 8 + c + CH, :] = b_low
        b_low = b_ref[rows, :]
        bs_ref[0:8, :] = jnp.zeros((8, D), f32)
        bs_ref[8 + SEQ : 16 + SEQ, :] = jnp.zeros((8, D), f32)
        loaded(1, 2, then=(5, 6, 7, 8), axis=3)
        right = (
            nn(bs_ref[7 : 7 + SEQ, :].astype(bf), wconv[0])
            + nn(b_low, wconv[1])
            + nn(bs_ref[9 : 9 + SEQ, :].astype(bf), wconv[2])
        )
        for n in range(8):
            cols = slice(256 * n, 256 * n + 256)
            left = nn(b_low, wleft[:, cols])
            for c in range(0, SEQ, CH):
                hidden, slope = gelu_both(left[c : c + CH])
                dgl_ref[at(s, c, CH), cols] = slope.astype(bf)
                if n == 0:
                    extra, slope = gelu_both(right[c : c + CH])
                    dgr_ref[at(s, c, CH), :] = slope.astype(bf)
                    hidden = hidden + extra
                wide_ref[c : c + CH, cols] = hidden
        ship(s, "b", "dgl", "dgr")
        for j in range(16):
            m_ref[s, j, 0:8, :] = zero8
            m_ref[s, j, 8 + SEQ : PAD, :] = zero8
        for c in range(0, SEQ, 8):
            mean = jnp.mean(wide_ref[c : c + 8, :], axis=-1, keepdims=True)
            cen = wide_ref[c : c + 8, :] - mean
            rstd = lax.rsqrt(jnp.mean(cen * cen, axis=-1, keepdims=True) + EPS)
            rstd = jnp.where(row_of(c, 8) < length, rstd, 0.0)
            rstd_ref[at(s, c, 8), 2:3] = rstd
            for j in range(16):
                m_ref[s, j, 8 + c : 16 + c, :] = cen[:, 128 * j : 128 * j + 128] * rstd
        for j in range(16):
            cols = slice(128 * j, 128 * j + 128)
            taps = [wp_ref[o : o + 1, cols] for o in range(9)]
            for c in range(0, SEQ, CH):
                total = m_ref[s, j, c + 4 : c + 4 + CH, :] * taps[0]
                for o in range(1, 9):
                    total = total + m_ref[s, j, c + 4 + o : c + 4 + o + CH, :] * taps[o]
                depth_ref[j // 2, s, c : c + CH, 128 * (j % 2) : 128 * (j % 2) + 128] = total.astype(bf)
        ship(s, "m", "depth")
        loaded(3, axis=2)
        depth = jnp.concatenate([depth_ref[n, s] for n in range(8)], axis=1)
        sep_ref[...] = nn(depth, wpoint[...])
        for c in range(0, SEQ, CH):
            conv = xf_ref[c : c + CH, :]
            conv = jnp.concatenate([conv[:, :HALF] + sep_ref[c : c + CH, :], conv[:, HALF:]], axis=1)
            xf_ref[c : c + CH, :] = conv
            cen, rstd = norm(conv)
            e_ref[at(s, c, CH), :] = (cen * rstd * gains[2:3]).astype(bf)
            rstd_ref[at(s, c, CH), 3:4] = rstd
        e_low = e_ref[rows, :]
        loaded(4)
        for n in range(6):
            cols = slice(256 * n, 256 * n + 256)
            part = nn(e_low, wqkv[:, cols]).astype(bf)
            qkv_ref[:, cols] = part
            qkvt_ref[cols, at(s, 0, SEQ)] = part.T
        ship(s, "e", "qkvt")
        bias = jnp.where(row_of(0, SEQ) < jnp.maximum(length, 1), 0.0, -1e30)
        for h in range(HEADS):
            base = 3 * DH * h
            key = qkv_ref[:, base + DH : base + 2 * DH] * jnp.asarray(DH**-0.5, bf)
            query_t = qkvt_ref[base : base + DH, at(s, 0, SEQ)]
            value_t = qkvt_ref[base + 2 * DH : base + 3 * DH, at(s, 0, SEQ)]
            for q in range(0, SEQ, 128):
                scores = nn(key, query_t[:, q : q + 128]) + bias
                scores = jnp.exp(scores - jnp.max(scores, axis=0, keepdims=True))
                scores = scores * (1.0 / jnp.sum(scores, axis=0, keepdims=True))
                pt_ref[s, h, :, q : q + 128] = scores.astype(bf)
            mixt_ref[DH * h : DH * h + DH, at(s, 0, SEQ)] = nn(value_t, pt_ref[s, h]).astype(bf)
        ship(s, "pt", "mixt")
        loaded(5, axis=1)
        for n in range(2):
            cols = slice(256 * n, 256 * n + 256)
            xf_ref[:, cols] += tn(mixt_ref[:, at(s, 0, SEQ)], wout[:, cols])
        for c in range(0, SEQ, CH):
            cen, rstd = norm(xf_ref[c : c + CH, :])
            f_ref[at(s, c, CH), :] = (cen * rstd * gains[3:4]).astype(bf)
            rstd_ref[at(s, c, CH), 4:5] = rstd
        f_low = f_ref[rows, :]
        loaded(6)
        for n in range(8):
            cols = slice(256 * n, 256 * n + 256)
            up = nn(f_low, wup[:, cols])
            for c in range(0, SEQ, CH):
                low, slope = gelu_both(up[c : c + CH])
                up_ref[at(s, c, CH), cols] = low.astype(bf)
                gup_ref[at(s, c, CH), cols] = slope.astype(bf)
        loaded(7, 8, axis=0)
        for n in range(2):
            cols = slice(256 * n, 256 * n + 256)
            down = nn(up_ref[rows, :], wdown[:, cols])
            out_ref[rows, cols] = (xf_ref[:, cols] + down).astype(bf)
        ship(s, "f", "rstd", "up")
        leave(s).start()
        for c in range(0, SEQ, CH):
            weight = jnp.where(row_of(c, CH) < length, fac_ref[s, 0:1, 0:1], 0.0)
            g_out = cot_ref[at(s, c, CH), :].astype(f32) * weight
            ga_ref[at(s, c, CH), :] = g_out
            gl_ref[at(s, c, CH), :] = g_out.astype(bf)
        g_low = gl_ref[rows, :]
        for n in range(8):
            cols = slice(256 * n, 256 * n + 256)
            back = nt(g_low, wdown[cols, :])
            gup_ref[rows, cols] = (back * gup_ref[rows, cols].astype(f32)).astype(bf)
        ship(s, "gup", "gl")
        for n in range(2):
            cols = slice(256 * n, 256 * n + 256)
            wide_ref[:, cols] = nt(gup_ref[rows, :], wup[cols, :])
        inverse = 1.0 / gains[3:4]
        for c in range(0, SEQ, CH):
            g_f = wide_ref[c : c + CH, 0:D]
            low = f_ref[at(s, c, CH), :].astype(f32)
            gain_f_ref[pl.ds(pl.multiple_of(s * 8, 8), 8), :] += fold8(g_f * low)
            back = norm_back(g_f, low, gains[3:4], inverse, rstd_ref[at(s, c, CH), 4:5])
            ga_ref[at(s, c, CH), :] += back
        gal_ref[rows, :] = ga_ref[rows, :].astype(bf)
        ship(s, "ga", "gal")
        gmixt_ref[:, at(s, 0, SEQ)] = nt(wout[...], gal_ref[rows, :]).astype(bf)
        ship(s, "gmixt", "gain_f")
        return carry

    lax.fori_loop(0, sents, sentence, 0)

    def landed(s, carry):
        for name in KEPT:
            shipment(name, s).wait()
        leave(s).wait()
        return carry

    lax.fori_loop(0, sents, landed, 0)
    for axis in range(4):
        for copy in sums.small_copies(0, axis, count_ref, count_got):
            copy.wait_send()


def vmem():
    return pl.BlockSpec(memory_space=pltpu.VMEM)


def smem():
    return pl.BlockSpec(memory_space=pltpu.SMEM)


def offsets(share, wide_share):
    sizes = (
        ("up", 8 * share, True),
        ("down", 2 * wide_share, True),
        ("out", 2 * share, False),
        ("qkv", 6 * share, True),
        ("point", wide_share, True),
        ("left", 4 * share, True),
        ("left2", 4 * share, True),
        ("conv", 3 * share, True),
        ("glu", 2 * share, True),
        ("glu1", 2 * share, True),
    )
    first, starts, groups, begin = 0, {}, [], 0
    for name, size, ends in sizes:
        starts[name] = first
        first += size
        if ends:
            first = -(-first // 32) * 32
            groups.append((begin, first - begin))
            begin = first
    return starts, groups, first


def put(g_ref, grid, tile, first, share, wide, chunk=0):
    _, ys = grid
    for part in range(tile.shape[1] // 256):
        for k in range(512 // share):
            block = chunk * (512 // share) + k
            piece = tile[k * share : (k + 1) * share, 256 * part : 256 * part + 256]
            rows = pl.ds(pl.multiple_of(first + part * share, 16), share)
            g_ref[block // ys, block % ys, rows, :] = piece.astype(bf)


SCHEDULE = {
    "u3": (0,),
    "d3": (1,),
    "o": (0,),
    "a1a": (1,),
    "q0": (0,),
    "q2": (2,),
    "p1": (1,),
    "p2": (2,),
    "p3": (3,),
    "w0b": (0,),
    "w0c": (3,),
    "w1c": (1,),
    "w2b": (0,),
    "w2c": (2,),
    "l1": (4, 3, 1,),
    "l2": (0,),
    "l3": (5,),
    "c": (6, 4, 1,),
    "i0": (5, 2,),
    "i1": (6,),
    "i2": (3, 4,),
    "g0": (7,),
    "g1": (8,),
    "r0": (5, 7,),
    "r1": (8, 2, 6,),
    "r2": (3, 4,),
    "e0": (5,),
    "e1": (7, -1, 2,),
    "e2": (3, 8, 6,),
    "z": (-1, 4, -2, 5, -1, 4, 7, -2, 5, 8, 6, -2, 6, -1, 7, 8, -1, -2, 7, 8,),
}


def back_kernel(
    sents,
    grid,
    xs,
    names,
    gains_ref,
    wg_ref,
    wglu_far,
    wleft_far,
    wconv_far,
    wdepth,
    wpoint_far,
    wqkv_far,
    *refs,
):
    far, refs = dict(zip(KEPT, refs)), refs[len(KEPT) :]
    xgrad_far, final_far, early_far, late_far = refs[:4]
    recv, refs = dict(zip(names, refs[4:])), refs[4 + len(names) :]
    (wglu, wleft, wconv, wpoint, wqkv), refs = refs[:5], refs[5:]
    (
        fetch_sems,
        send_sems,
        recv_sems,
        g_ref,
        final_ref,
        early_ref,
        early_got,
        late_ref,
        late_got,
        first_wide,
        second_wide,
        gqkv_ref,
        squares,
        conv_ref,
        gl_ref,
        fs_ref,
        gas_ref,
        mixt_ref,
        gmixt_ref,
        qkvt_ref,
        dgr_ref,
        rstd_ref,
        gain_f_ref,
        m_ref,
        wp_ref,
        gqkvt_ref,
        gd_ref,
        wide_ref,
        taps_ref,
        s1_ref,
        s2_ref,
        right_ref,
        gain_ref,
    ) = refs
    e_ref = gas_ref
    gr_refs = (gl_ref.at[:, 0:HALF], gl_ref.at[:, HALF:D], fs_ref.at[:, 0:HALF])
    sep_ref = fs_ref.at[:, HALF:D]
    up_ref = gleft_ref = dgl_ref = first_wide
    gup_ref = second_wide
    a_ref, b_ref, sig_ref, u_ref = [second_wide.at[:, D * k : D * k + D] for k in range(4)]
    gg_ref = gqkv_ref
    pt_ref, depth_view = squares, squares.reshape(8, sents, SEQ, 256)
    where = dict(
        a=a_ref, b=b_ref, e=e_ref, f=fs_ref, rstd=rstd_ref, sig=sig_ref, u=u_ref, dgl=first_wide, dgr=dgr_ref,
        qkvt=qkvt_ref, mixt=mixt_ref, up=first_wide, gup=second_wide, ga=conv_ref, gmixt=gmixt_ref, gain_f=gain_f_ref,
        pt=squares, depth=depth_view, gl=gl_ref, gal=gas_ref, wglu=wglu, wleft=wleft, wconv=wconv, wpoint=wpoint, wqkv=wqkv,
    )
    far.update(wglu=wglu_far, wleft=wleft_far, wconv=wconv_far, wpoint=wpoint_far, wqkv=wqkv_far)
    order = (
        "gmixt", "qkvt", "pt", "f", "gup", "gal", "ga", "gl", "up", "gain_f", "rstd", "mixt", "wqkv", "wpoint", "dgr",
        "wleft", "wconv", "wglu", "e", "b", "a", "sig", "u", "dgl", "depth",
    )

    def wide_tile(i):
        return pl.ds(pl.multiple_of(i * 512, 512), 512)

    def fetch(name):
        return pltpu.make_async_copy(far[name], where[name], fetch_sems.at[order.index(name)])

    def start(*names):
        for name in names:
            fetch(name).start()

    def wait(*names):
        for name in names:
            fetch(name).wait()

    def fetch_tile(name, i):
        tile = wide_tile(i)
        sem = fetch_sems.at[len(order) + 6 + (4 if name == "up" else 0) + i]
        return pltpu.make_async_copy(far[name].at[:, tile], where[name].at[:, tile], sem)

    def fetch_m(s):
        return pltpu.make_async_copy(far["m"].at[s], m_ref.at[s % 2], fetch_sems.at[len(order) + s % 2])

    start("f")
    for i in range(4):
        fetch_tile("gup", i).start()
    share, wide_share = 512 // (grid[0] * grid[1]), 2048 // (grid[0] * grid[1])
    starts, groups, _ = offsets(share, wide_share)
    sums = Sums(grid, xs, groups, g_ref, final_ref, recv, send_sems, recv_sems)
    sums.greeted(sums.greet())
    small_step = {-1: 4, -2: 3}

    def claim(name):
        steps = []
        for i in SCHEDULE.get(name, ()):
            if i >= 0:
                steps += sums.claim(i)
            elif small_step[i] >= 0:
                steps.append((i, small_step[i]))
                small_step[i] -= 1
        return steps

    def do(steps):
        for i, stage in steps:
            if i >= 0:
                sums.do([(i, stage)])
            elif i == -1:
                sums.early_next(stage, early_ref, early_got)
            else:
                sums.small_next(2, stage, late_ref, late_got)

    def point(name):
        do(claim(name))

    def loop(name, first, last, body, parts=""):
        claims = {(k, part): claim(f"{name}{k}{part}") for k in range(first, last) for part in parts or ("",)}

        def within(k, part):
            for n in range(first, last):
                if claims[n, part]:
                    pl.when(k == n)(functools.partial(do, claims[n, part]))

        def round(k, carry):
            body(k, within)
            if not parts:
                within(k, "")
            return carry

        lax.fori_loop(first, last, round, 0)

    wp_ref[0:9, :] = wdepth[...].astype(f32) * one_row(wg_ref)
    gain_ref[...] = jnp.zeros_like(gain_ref)
    taps_ref[...] = jnp.zeros_like(taps_ref)

    wait("f")
    start("gl")
    for i in range(4):
        fetch_tile("up", i).start()
    start("mixt", "gal", "gain_f")

    def grad_up(i, within):
        fetch_tile("gup", i).wait()
        tile = tn(fs_ref[...], gup_ref[:, wide_tile(i)])
        put(g_ref, grid, tile, starts["up"] + i * 2 * share, share, False)

    loop("u", 0, 4, grad_up)
    wait("gl")
    start("gmixt", "qkvt", "pt", "b", "a", "sig", "u")

    def grad_down(i, within):
        fetch_tile("up", i).wait()
        put(g_ref, grid, tn(up_ref[:, wide_tile(i)], gl_ref[...]), starts["down"], wide_share, True, i)

    loop("d", 0, 4, grad_down)
    wait("gal", "mixt", "gain_f")
    start("dgl", "wqkv", "ga", "rstd")
    put(g_ref, grid, nn(mixt_ref[...], gas_ref[...]), starts["out"], share, False)
    start("e", "wpoint", "dgr")
    point("o")

    for s in range(sents):
        gain_ref[24:32, :] += gain_f_ref[8 * s : 8 * s + 8, :]
    wait("gmixt", "qkvt", "pt")

    def attend(s, within):
        rows = at(s, 0, SEQ)
        for h in range(HEADS):
            base = 3 * DH * h
            g_o = gmixt_ref[DH * h : DH * h + DH, rows]
            query_t = qkvt_ref[base : base + DH, rows]
            key_t = qkvt_ref[base + DH : base + 2 * DH, rows]
            value = qkvt_ref[base + 2 * DH : base + 3 * DH, rows].T
            probs = pt_ref[s, h]
            halves = []
            for q in range(0, SEQ, 128):
                part = probs[:, q : q + 128].astype(f32)
                back = nn(value, g_o[:, q : q + 128])
                both = part * back
                halves.append((both - part * jnp.sum(both, axis=0, keepdims=True)).astype(bf))
            g_scores = jnp.concatenate(halves, axis=1)
            gqkvt_ref[base : base + DH, :] = (nn(key_t, g_scores) * DH**-0.5).astype(bf)
            gqkvt_ref[base + DH : base + 2 * DH, :] = (nt(query_t, g_scores) * DH**-0.5).astype(bf)
            gqkvt_ref[base + 2 * DH : base + 3 * DH, :] = nt(g_o, probs).astype(bf)
            if h % 4 == 3:
                within(s, "ab"[h // 4])
        for n in range(6):
            cols = slice(256 * n, 256 * n + 256)
            gqkv_ref[rows, cols] = gqkvt_ref[cols, :].T

    loop("a", 0, sents, attend, "ab")
    start("depth")
    fetch_m(0).start()
    if sents > 1:
        fetch_m(1).start()
    wait("e")

    def grad_qkv(i, within):
        put(g_ref, grid, tn(e_ref[...], gqkv_ref[:, wide_tile(i)]), starts["qkv"] + i * 2 * share, share, False)

    loop("q", 0, 3, grad_qkv)

    def attention_input(s, within):
        gains = gains_ref[...].astype(f32)
        inverse = 1.0 / gains[2:3]
        rows = at(s, 0, SEQ)
        for n in range(2):
            cols = slice(256 * n, 256 * n + 256)
            wide_ref[:, cols] = nt(gqkv_ref[rows, :], wqkv[cols, :])
        for c in range(0, SEQ, CH):
            part = at(s, c, CH)
            g_e = wide_ref[c : c + CH, 0:D]
            low = e_ref[part, :].astype(f32)
            gain_ref[16:24, :] += fold8(g_e * low)
            g_conv = conv_ref[part, :] + norm_back(g_e, low, gains[2:3], inverse, rstd_ref[part, 3:4])
            conv_ref[part, :] = g_conv
            sep_ref[part, :] = g_conv[:, :HALF].astype(bf)

    wait("wqkv", "ga", "rstd")
    loop("n", 0, sents, attention_input)
    wait("depth")

    def grad_point(i, within):
        depth = [depth_view[2 * i + k].reshape(sents * SEQ, 256) for k in range(2)]
        put(g_ref, grid, tn(jnp.concatenate(depth, axis=1), sep_ref[...]), starts["point"], wide_share, True, i)

    loop("p", 0, 4, grad_point)
    start("wleft", "wconv", "wglu")
    wait("b", "a", "sig", "u", "dgr", "dgl", "wpoint")

    zero8 = jnp.zeros((8, 128), f32)

    def g_depth(rows):
        for n in range(8):
            back = nt(sep_ref[rows, :], wpoint[256 * n : 256 * n + 256, :])
            for k in range(2):
                gd_ref[2 * n + k, 8 : 8 + SEQ, :] = back[:, 128 * k : 128 * k + 128]

    def wide(s, within):
        rows = at(s, 0, SEQ)
        slot = s % 2
        fetch_m(s).wait()
        g_depth(rows)
        within(s, "a")
        for j in range(16):
            gd_ref[j, 0:8, :] = zero8
            gd_ref[j, 8 + SEQ : PAD, :] = zero8
            cols = slice(128 * j, 128 * j + 128)
            taps = [wp_ref[o : o + 1, cols] for o in range(9)]
            for c in range(0, SEQ, CH):
                total = gd_ref[j, c + 12 : c + 12 + CH, :] * taps[0]
                for o in range(1, 9):
                    total = total + gd_ref[j, c + 12 - o : c + 12 - o + CH, :] * taps[o]
                wide_ref[c : c + CH, cols] = total
                mine = m_ref[slot, j, c + 8 : c + 8 + CH, :]
                if j == 0:
                    s1_ref[c : c + CH, :] = total
                    s2_ref[c : c + CH, :] = total * mine
                else:
                    s1_ref[c : c + CH, :] += total
                    s2_ref[c : c + CH, :] += total * mine
        within(s, "b")
        right_ref[0:8, :] = jnp.zeros((8, HALF), f32)
        right_ref[8 + SEQ : PAD, :] = jnp.zeros((8, HALF), f32)
        for c in range(0, SEQ, CH):
            part = at(s, c, CH)
            rstd = rstd_ref[part, 2:3]
            m1 = jnp.sum(s1_ref[c : c + CH, :], axis=-1, keepdims=True) * (rstd / FF)
            m2 = jnp.sum(s2_ref[c : c + CH, :], axis=-1, keepdims=True) * (rstd / FF)
            for j in range(16):
                cols = slice(128 * j, 128 * j + 128)
                g_h = wide_ref[c : c + CH, cols] * rstd - m1 - m_ref[slot, j, c + 8 : c + 8 + CH, :] * m2
                gleft_ref[part, cols] = (g_h * dgl_ref[part, cols].astype(f32)).astype(bf)
                if j < 2:
                    right_ref[8 + c : 8 + c + CH, cols] = g_h * dgr_ref[part, cols].astype(f32)

        @pl.when(s + 2 < sents)
        def _():
            fetch_m(s + 2).start()

        for k in range(3):
            gr_refs[k][rows, :] = right_ref[9 - k : 9 - k + SEQ, :].astype(bf)
        within(s, "c")

    loop("w", 0, sents, wide, "abc")
    for i in range(4):
        put(g_ref, grid, tn(b_ref[...], gleft_ref[:, 512 * i : 512 * i + 512]), starts[("left", "left2")[i // 2]] + i % 2 * 2 * share, share, False)
        point(f"l{i}")
    for k in range(3):
        put(g_ref, grid, tn(b_ref[...], gr_refs[k][...]), starts["conv"] + k * share, share, False)
    point("c")

    def inputs(s, within):
        gains = gains_ref[...].astype(f32)
        rows = at(s, 0, SEQ)
        for n in range(2):
            cols = slice(256 * n, 256 * n + 256)
            g_b = nt(gleft_ref[rows, :], wleft[cols, :])
            for k in range(3):
                g_b = g_b + nt(gr_refs[k][rows, :], wconv[k, cols, :])
            wide_ref[:, cols] = g_b
        inverse = 1.0 / gains[1:2]
        for c in range(0, SEQ, CH):
            part = at(s, c, CH)
            g_b = wide_ref[c : c + CH, 0:D]
            low = b_ref[part, :].astype(f32)
            gain_ref[8:16, :] += fold8(g_b * low)
            g_glu = conv_ref[part, :] + norm_back(g_b, low, gains[1:2], inverse, rstd_ref[part, 1:2])
            conv_ref[part, :] = g_glu
            gg_ref[part, 0:D] = (g_glu * sig_ref[part, :].astype(f32)).astype(bf)
            gg_ref[part, D : 2 * D] = (g_glu * u_ref[part, :].astype(f32)).astype(bf)

    def inputs_end(s, within):
        gains = gains_ref[...].astype(f32)
        rows = at(s, 0, SEQ)
        for n in range(2):
            cols = slice(256 * n, 256 * n + 256)
            wide_ref[:, cols] = nt(gg_ref[rows, 0 : 2 * D], wglu[cols, :])
        inverse = 1.0 / gains[0:1]
        for c in range(0, SEQ, CH):
            part = at(s, c, CH)
            g_a = wide_ref[c : c + CH, 0:D]
            low = a_ref[part, :].astype(f32)
            gain_ref[0:8, :] += fold8(g_a * low)
            conv_ref[part, :] += norm_back(g_a, low, gains[0:1], inverse, rstd_ref[part, 0:1])

    wait("wleft", "wconv", "wglu")
    loop("i", 0, sents, inputs)
    for i in range(2):
        put(g_ref, grid, tn(a_ref[...], gg_ref[:, 512 * i : 512 * i + 512]), starts[("glu", "glu1")[i]], share, False)
        point(f"g{i}")
    def tap_sums(i, within):
        s = sents - 1 - i

        @pl.when(i >= 2)
        def _():
            fetch_m(s).wait()

        @pl.when(i >= 1)
        def _():
            g_depth(at(s, 0, SEQ))

        for j in range(16):
            cols = slice(128 * j, 128 * j + 128)
            lines = [taps_ref[o, :, cols] for o in range(9)]
            for c in range(0, SEQ, CH):
                back = gd_ref[j, c + 8 : c + 8 + CH, :]
                for o in range(9):
                    lines[o] = lines[o] + fold8(m_ref[s % 2, j, c + 4 + o : c + 4 + o + CH, :] * back)
            for o in range(9):
                taps_ref[o, :, cols] = lines[o]

        @pl.when(s >= 2)
        def _():
            fetch_m(s - 2).start()

    loop("r", 0, sents, tap_sums)
    wide_gain = one_row(wg_ref)
    total = jnp.zeros((1, FF), f32)
    for o in range(9):
        lines = jnp.sum(taps_ref[o], axis=0, keepdims=True)
        total = total + lines * wdepth[o : o + 1, :].astype(f32)
        early_ref[0, o : o + 1, :] = lines * wide_gain
    early_ref[0, 9:10, :] = total
    early_ref[0, 10:16, :] = jnp.zeros((6, FF), f32)

    def gain_row(i):
        return jnp.sum(gain_ref[8 * i : 8 * i + 8, :], axis=0, keepdims=True) / gains_ref[i : i + 1, :].astype(f32)

    early_ref[0, 10:11, 0:D] = gain_row(2)
    early_ref[0, 11:12, 0:D] = gain_row(3)
    sums.early_next(5, early_ref, early_got)
    point("t")

    loop("e", 0, sents, inputs_end)
    leave = pltpu.make_async_copy(conv_ref, xgrad_far, fetch_sems.at[len(order) + 2])
    leave.start()
    late_ref[3] = jnp.zeros((8, D), f32)
    late_ref[3, 0:1, :] = gain_row(0)
    late_ref[3, 1:2, :] = gain_row(1)
    sums.small_send(2, 3, late_ref, late_got)
    point("z")
    for _ in range(sums.STAGES + 1):
        sums.advance(*range(len(groups)))
    for i in small_step:
        while small_step[i] >= 0:
            do([(i, small_step[i])])
            small_step[i] -= 1
    ends = (final_ref, final_far), (early_ref.at[2], early_far), (late_ref.at[4], late_far)
    ends = [pltpu.make_async_copy(*pair, fetch_sems.at[len(order) + 3 + k]) for k, pair in enumerate(ends)]
    for copy in ends:
        copy.start()
    sums.finish()
    sums.early_sent(early_ref, early_got)
    leave.wait()
    for copy in ends:
        copy.wait()


def coordinates(ys):
    dp, head = lax.axis_index("dp"), lax.axis_index("head")
    return dp // ys, dp % ys, head // 2, head % 2


def device(ys, z, y, x, c):
    return (z * ys + y, x * 2 + c)


def rows16(first, size):
    return pl.ds(pl.multiple_of(first, 16), size)


def split_of(size, xs):
    half = size // 2
    first = (half // (32 * xs)) * 16 * xs
    return half, first, half - first


class Sums:
    STAGES = 5

    def __init__(self, grid, xs, groups, g_ref, final_ref, recv, send_sems, recv_sems):
        self.zs, self.ys = grid
        self.xs = xs
        self.sizes = (*grid, xs, 2)
        self.groups = groups
        self.g, self.final = g_ref, final_ref
        self.recv = recv
        self.send_sems, self.recv_sems = send_sems, recv_sems
        self.place = coordinates(self.ys)
        self.stage = [-1] * len(groups)
        self.small = []

    def peers(self, axis):
        size = self.sizes[axis]
        for step in range(1, size):
            to = list(self.place)
            to[axis] = lax.rem(to[axis] + step, size)
            yield step - 1, to[axis], device(self.ys, *to)

    def heads(self):
        z, y, x, c = self.place
        for dx in range(self.xs):
            for dc in range(2):
                if dx or dc:
                    yield device(self.ys, z, y, lax.rem(x + dx, self.xs), lax.rem(c + dc, 2))

    def greet(self, heads=True):
        others = [to for axis in range(2 if heads else 4) for _, _, to in self.peers(axis)]
        others += self.heads() if heads else []
        for to in others:
            pl.semaphore_signal(pltpu.get_barrier_semaphore(), inc=1, device_id=to, device_id_type=MESH)
        return len(others)

    def greeted(self, total):
        pl.semaphore_wait(pltpu.get_barrier_semaphore(), total)

    def core_first(self, i):
        return (self.groups[i][0] - (self.groups[3][0] if i > 2 else 0)) // 2

    def a_first(self, i):
        return sum(split_of(size, self.xs)[1] // self.xs for _, size in self.groups[:i])

    def b_first(self, i):
        return sum(split_of(size, self.xs)[2] for _, size in self.groups[:i])

    def rows(self, i):
        first, size = self.groups[i]
        half, na, nb = split_of(size, self.xs)
        mine = first + self.place[3] * half
        return first, half, mine, na, na // self.xs, mine + na, nb

    def plan(self, stage, i):
        z, y, x, c = self.place
        first, half, mine, na, part, b_row, nb = self.rows(i)
        g, recv, final = self.g, self.recv, self.final
        a_in, b_in = pl.ds(self.a_first(i), part), pl.ds(self.b_first(i), nb)
        a_rows, b_rows = rows16(mine + x * part, part), rows16(b_row, nb)
        axis_a, axis_b = ((None, 3), (2, 1), (1, 0), (0, 2), (None, 3))[stage]
        copies_a, copies_b = [], []
        for slot, other, to in self.peers(axis_b) if axis_b is not None else ():
            if stage == 0:
                source = g.at[:, :, rows16(first + other * half, half), :]
                target = recv["core"].at[:, :, pl.ds(self.core_first(i), half), :]
            elif stage == 1:
                source, target = g.at[:, other, b_rows, :], recv["b1"].at[slot, :, b_in, :]
            elif stage == 2:
                source, target = g.at[other, y, b_rows, :], recv["b2"].at[slot, b_in, :]
            elif stage == 3:
                source, target = g.at[z, y, b_rows, :], recv["b3"].at[slot, b_in, :]
            else:
                source, target = final.at[b_rows, :], final.at[b_rows, :]
            copies_b.append((source, target, to))
        for slot, other, to in self.peers(axis_a) if axis_a is not None and na else ():
            if stage == 1:
                source, target = g.at[:, :, rows16(mine + other * part, part), :], recv["a1"].at[slot, :, :, a_in, :]
            elif stage == 2:
                source, target = g.at[:, other, a_rows, :], recv["a2"].at[slot, :, a_in, :]
            else:
                source, target = g.at[other, y, a_rows, :], recv["a3"].at[slot, a_in, :]
            copies_a.append((source, target, to))
        if stage == 4 and na:
            copies_a = [(final.at[a_rows, :], final.at[a_rows, :], to) for to in self.heads()]
        return copies_b, copies_a

    def copies(self, stage, i):
        counts = self.counts(self.sizes)
        first = i * sum(map(sum, counts)) + sum(map(sum, counts[:stage]))
        copies_b, copies_a = self.plan(stage, i)
        made = []
        for copies, extra in ((copies_b, 0), (copies_a, counts[stage][0])):
            for n, (source, target, to) in enumerate(copies):
                index = first + extra + n
                made.append(
                    pltpu.make_async_remote_copy(
                        src_ref=source,
                        dst_ref=target,
                        send_sem=self.send_sems.at[index],
                        recv_sem=self.recv_sems.at[index],
                        device_id=to,
                        device_id_type=MESH,
                    )
                )
        return made

    @staticmethod
    def counts(sizes):
        z, y, x, _ = (size - 1 for size in sizes)
        return ((1, 0), (y, x), (z, y), (x, z), (1, 2 * x + 1))

    @staticmethod
    def semaphores(grid, xs, groups):
        sizes = (*grid, xs, 2)
        return len(groups) * sum(map(sum, Sums.counts(sizes))) + 12 * (max(sizes) - 1) + sum(sizes) + 2 * xs

    def claim(self, *groups):
        steps = []
        for i in groups:
            if self.stage[i] < self.STAGES:
                steps.append((i, self.stage[i]))
                self.stage[i] += 1
        return steps

    def do(self, steps):
        for i, stage in steps:
            if stage >= 0:
                for copy in self.copies(stage, i):
                    copy.wait_recv()
                self.add(stage, i)
            if stage + 1 < self.STAGES:
                for copy in self.copies(stage + 1, i):
                    copy.start()

    def advance(self, *groups):
        self.do(self.claim(*groups))

    def over(self, i):
        return self.stage[i] == self.STAGES

    def add(self, stage, i):
        z, y, x, c = self.place
        first, half, mine, na, part, b_row, nb = self.rows(i)
        g, recv = self.g, self.recv
        a_in, b_in = pl.ds(self.a_first(i), part), pl.ds(self.b_first(i), nb)
        a_rows, b_rows = rows16(mine + x * part, part), rows16(b_row, nb)

        def total(mine, got):
            value = mine.astype(f32)
            for other in got:
                value = value + other.astype(f32)
            return value.astype(bf)

        if stage == 0:

            def core(block, carry):
                zb, yb = block // self.ys, block % self.ys
                g[zb, yb, rows16(mine, half), :] += recv["core"][zb, yb, pl.ds(self.core_first(i), half), :]
                return carry

            lax.fori_loop(0, self.zs * self.ys, core, 0)
        elif stage == 1:

            def one(zb, carry):
                got = [recv["b1"][slot, zb, b_in, :] for slot in range(self.ys - 1)]
                g[zb, y, b_rows, :] = total(g[zb, y, b_rows, :], got)
                for yb in range(self.ys) if na else ():
                    got = [recv["a1"][slot, zb, yb, a_in, :] for slot in range(self.xs - 1)]
                    g[zb, yb, a_rows, :] = total(g[zb, yb, a_rows, :], got)
                return carry

            lax.fori_loop(0, self.zs, one, 0)
        elif stage == 2:
            g[z, y, b_rows, :] = total(g[z, y, b_rows, :], [recv["b2"][slot, b_in, :] for slot in range(self.zs - 1)])
            if na:

                def two(zb, carry):
                    got = [recv["a2"][slot, zb, a_in, :] for slot in range(self.ys - 1)]
                    g[zb, y, a_rows, :] = total(g[zb, y, a_rows, :], got)
                    return carry

                lax.fori_loop(0, self.zs, two, 0)
        elif stage == 3:
            got = [recv["b3"][slot, b_in, :] for slot in range(self.xs - 1)]
            self.final[b_rows, :] = total(g[z, y, b_rows, :], got)
            if na:
                got = [recv["a3"][slot, a_in, :] for slot in range(self.zs - 1)]
                self.final[a_rows, :] = total(g[z, y, a_rows, :], got)

    def small_copies(self, k, axis, held, got):
        most = max(self.sizes) - 1
        base = len(self.groups) * sum(map(sum, self.counts(self.sizes)))
        made = []
        for slot, other, to in self.peers(axis):
            index = base + (k * 4 + axis) * most + slot
            made.append(
                pltpu.make_async_remote_copy(
                    src_ref=held.at[axis],
                    dst_ref=got.at[self.got_first(axis) + slot],
                    send_sem=self.send_sems.at[index],
                    recv_sem=self.recv_sems.at[index],
                    device_id=to,
                    device_id_type=MESH,
                )
            )
        return made

    def got_first(self, axis):
        return sum(size - 1 for size in self.sizes[:axis])

    def small_send(self, k, axis, held, got):
        self.small.append((k, axis, held, got))
        for copy in self.small_copies(k, axis, held, got):
            copy.start()

    def small_add(self, k, axis, held, got):
        for copy in self.small_copies(k, axis, held, got):
            copy.wait_recv()
        size, me = self.sizes[axis], self.place[axis]
        total = None
        for n in range(size):
            value = held[axis]
            for slot in range(size - 1):
                value = jnp.where(lax.rem(me - slot - 1 + size, size) == n, got[self.got_first(axis) + slot], value)
            total = value if total is None else total + value
        held[axis - 1 if axis else 4] = total

    def early_plan(self, step, held, got):
        z, y, x, c = self.place
        half = held.shape[2] // 2
        part = half // self.xs
        mine = pl.ds(pl.multiple_of(c * half + x * part, 128), part)
        if step == 4:
            return [
                (held.at[0, :, pl.ds(pl.multiple_of(other * half, 128), half)], got.at[0], to)
                for _, other, to in self.peers(3)
            ]
        if step == 3:
            return [
                (
                    held.at[0, :, pl.ds(pl.multiple_of(c * half + other * part, 128), part)],
                    got.at[1 + slot, :, pl.ds(0, part)],
                    to,
                )
                for slot, other, to in self.peers(2)
            ]
        if step == 0:
            return [(held.at[2, :, mine], held.at[2, :, mine], to) for to in self.heads()]
        first = self.xs + (0 if step == 2 else self.ys - 1)
        return [
            (held.at[2 - step, :, mine], got.at[first + slot, :, pl.ds(0, part)], to)
            for slot, _, to in self.peers(step - 1)
        ]

    def early_copies(self, step, held, got):
        counts = (2 * self.xs - 1, self.zs - 1, self.ys - 1, self.xs - 1, 1)
        base = len(self.groups) * sum(map(sum, self.counts(self.sizes))) + 12 * (max(self.sizes) - 1) + sum(counts[:step])
        return [
            pltpu.make_async_remote_copy(
                src_ref=source,
                dst_ref=target,
                send_sem=self.send_sems.at[base + n],
                recv_sem=self.recv_sems.at[base + n],
                device_id=to,
                device_id_type=MESH,
            )
            for n, (source, target, to) in enumerate(self.early_plan(step, held, got))
        ]

    def early_next(self, step, held, got):
        z, y, x, c = self.place
        half = held.shape[2] // 2
        part = half // self.xs
        mine = pl.ds(pl.multiple_of(c * half + x * part, 128), part)
        if step < 5:
            for copy in self.early_copies(step, held, got):
                copy.wait_recv()
        if step == 4:
            held[0, :, pl.ds(pl.multiple_of(c * half, 128), half)] += got[0]
        elif step == 3:
            for slot in range(self.xs - 1):
                held[0, :, mine] += got[1 + slot, :, 0:part]
        elif step in (1, 2):
            axis = step - 1
            size, me = self.sizes[axis], self.place[axis]
            first = self.xs + (0 if step == 2 else self.ys - 1)
            total = None
            for n in range(size):
                value = held[2 - step, :, mine]
                for slot in range(size - 1):
                    value = jnp.where(lax.rem(me - slot - 1 + size, size) == n, got[first + slot, :, 0:part], value)
                total = value if total is None else total + value
            held[3 - step, :, mine] = total
        if step:
            for copy in self.early_copies(step - 1, held, got):
                copy.start()

    def early_sent(self, held, got):
        for step in range(5):
            for copy in self.early_copies(step, held, got):
                copy.wait_send()

    def small_next(self, k, axis, held, got):
        self.small_add(k, axis, held, got)
        if axis:
            self.small_send(k, axis - 1, held, got)

    def finish(self):
        for i in range(len(self.groups)):
            for stage in range(self.STAGES):
                for copy in self.copies(stage, i):
                    copy.wait_send()
        for small in self.small:
            for copy in self.small_copies(*small):
                copy.wait_send()


def recv_shapes(grid, xs, groups, height):
    zs, ys = grid
    na = sum(split_of(size, xs)[1] for _, size in groups) // xs
    nb = sum(split_of(size, xs)[2] for _, size in groups)
    na = max(na, 16)
    return {
        "core": (zs, ys, max(groups[3][0], height - groups[3][0]) // 2, 256),
        "a1": (xs - 1, zs, ys, na, 256),
        "b1": (ys - 1, zs, nb, 256),
        "a2": (ys - 1, zs, na, 256),
        "b2": (zs - 1, nb, 256),
        "a3": (zs - 1, na, 256),
        "b3": (xs - 1, nb, 256),
    }


SMALL = 16


def last_kernel(share, wide_share, final_far, early_far, late_far, xgrad_in, cell_in, *refs):
    far, refs = refs[:13], refs[13:]
    near, (final_ref, early_ref, late_ref, in_sems, out_sems) = refs[:13], refs[13:]
    rows = xgrad_in.shape[0]
    step = rows // 3
    arriving = [
        pltpu.make_async_copy(source, target, in_sems.at[k])
        for k, (source, target) in enumerate(
            ((final_far, final_ref), (early_far, early_ref), (late_far, late_ref), (cell_in, near[1]))
        )
    ]
    leaving = [pltpu.make_async_copy(near[k], far[k], out_sems.at[k]) for k in range(1, 13)]
    parts = [pl.ds(step * k, step) for k in range(3)]
    inward = [pltpu.make_async_copy(xgrad_in.at[p, :], near[0].at[p, :], in_sems.at[4 + k]) for k, p in enumerate(parts)]
    outward = [pltpu.make_async_copy(near[0].at[p, :], far[0].at[p, :], out_sems.at[13 + k]) for k, p in enumerate(parts)]
    for copy in (arriving[0], *inward, *arriving[1:]):
        copy.start()
    starts, _, _ = offsets(share, wide_share)

    def spread(k, name, tiles, size):
        for n in range(tiles):
            part, m = name, n
            if name in ("left", "glu") and n >= tiles // 2:
                part, m = ("left2" if name == "left" else "glu1"), n - tiles // 2
            first = starts[part] + m * size
            near[k][:, 256 * n : 256 * n + 256] = final_ref[first : first + size, :].astype(f32)
        leaving[k - 1].start()

    arriving[0].wait()
    spread(5, "left", 8, share)
    spread(11, "up", 8, share)
    for a, b in zip(inward, outward):
        a.wait()
        b.start()
    spread(12, "down", 2, wide_share)
    spread(9, "qkv", 6, share)
    arriving[3].wait()
    leaving[0].start()
    spread(4, "glu", 4, share)
    spread(8, "point", 1, wide_share)
    for k in range(3):
        first = starts["conv"] + k * share
        near[6][k] = final_ref[first : first + share, :].astype(f32)
    leaving[5].start()
    spread(10, "out", 2, share)
    arriving[1].wait()
    arriving[2].wait()
    near[2][0:2, :] = late_ref[0:2, :]
    near[2][2:4, :] = early_ref[10:12, 0:D]
    near[3][...] = early_ref[9:10, :]
    near[7][...] = early_ref[0:9, :]
    for k in (2, 3, 7):
        leaving[k - 1].start()
    for copy in (*leaving, *outward):
        copy.wait()


def local(
    grid,
    xs,
    cell_input,
    lengths,
    pair_ids,
    cotangent,
    norm_gains,
    wide_gain,
    w_glu,
    w_left,
    w_conv3,
    w_depth,
    w_point,
    w_qkv,
    w_out,
    w_up,
    w_down,
):
    zs, ys = grid
    dp = zs * ys
    share, wide_share = 512 // dp, 2048 // dp
    rows = cell_input.shape[0]
    sents = lengths.shape[0]
    starts, groups, height = offsets(share, wide_share)
    wg = wide_gain.reshape(FF // 128, 128)
    shape = jax.ShapeDtypeStruct
    params = pltpu.CompilerParams(vmem_limit_bytes=62 << 20)
    kept = kept_shapes(sents)
    anywhere = pl.BlockSpec(memory_space=pl.ANY)
    most = zs + ys + xs - 2
    counting = Sums.semaphores(grid, xs, ())
    front = pl.pallas_call(
        functools.partial(front_kernel, sents, grid, xs),
        out_shape=[shape((rows, D), bf)] + list(kept.values()),
        in_specs=[smem(), smem(), vmem(), anywhere] + [vmem()] * 2 + [anywhere] * 3 + [vmem()] + [anywhere] * 5,
        out_specs=[anywhere] * (1 + len(kept)),
        scratch_shapes=[pltpu.VMEM(v, bf) for v in (*WEIGHTS, (rows, D))]
        + [pltpu.SemaphoreType.DMA((9,)), pltpu.VMEM((rows, D), bf)]
        + [pltpu.VMEM(v.shape, v.dtype) for v in kept.values()]
        + [
            pltpu.SemaphoreType.DMA((len(kept) + 1, sents)),
            pltpu.VMEM((16, FF), f32),
            pltpu.VMEM((SEQ, D), f32),
            pltpu.VMEM((PAD, D), f32),
            pltpu.VMEM((SEQ, FF), f32),
            pltpu.VMEM((SEQ, HALF), f32),
            pltpu.VMEM((SEQ, 3 * D), bf),
            pltpu.SemaphoreType.DMA((counting,)),
            pltpu.SemaphoreType.DMA((counting,)),
            pltpu.VMEM((5, 8, 128), f32),
            pltpu.VMEM((most, 8, 128), f32),
            pltpu.VMEM((sents, 8, 128), f32),
        ],
        compiler_params=pltpu.CompilerParams(vmem_limit_bytes=62 << 20, collective_id=1, has_side_effects=True),
        name="front",
    )(lengths, pair_ids, cell_input, cotangent, norm_gains, wg, w_glu, w_left, w_conv3, w_depth, w_point, w_qkv, w_out, w_up, w_down)
    cell, arrays = front[0], front[1:]
    recv = recv_shapes(grid, xs, groups, height)
    semaphores = Sums.semaphores(grid, xs, groups)
    input_grad, final, early, late = pl.pallas_call(
        functools.partial(back_kernel, sents, grid, xs, tuple(recv)),
        out_shape=[shape((rows, D), f32), shape((height, 256), bf), shape((SMALL, FF), f32), shape((8, D), f32)],
        in_specs=[vmem()] * 2 + [anywhere] * 3 + [vmem()] + [anywhere] * (2 + len(kept)),
        out_specs=[anywhere] * 4,
        scratch_shapes=[pltpu.VMEM(v, bf) for v in (*recv.values(), *WEIGHTS[:5])]
        + [
            pltpu.SemaphoreType.DMA((40,)),
            pltpu.SemaphoreType.DMA((semaphores,)),
            pltpu.SemaphoreType.DMA((semaphores,)),
            pltpu.VMEM((zs, ys, height, 256), bf),
            pltpu.VMEM((height, 256), bf),
            pltpu.VMEM((3, SMALL, FF), f32),
            pltpu.VMEM((most, SMALL, FF // 2), f32),
            pltpu.VMEM((5, 8, D), f32),
            pltpu.VMEM((most, 8, D), f32),
            pltpu.VMEM((rows, FF), bf),
            pltpu.VMEM((rows, FF), bf),
            pltpu.VMEM((rows, 3 * D), bf),
            pltpu.VMEM((sents, HEADS, SEQ, SEQ), bf),
            pltpu.VMEM((rows, D), f32),
            pltpu.VMEM((rows, D), bf),
            pltpu.VMEM((rows, D), bf),
            pltpu.VMEM((rows, D), bf),
            pltpu.VMEM((D, rows), bf),
            pltpu.VMEM((D, rows), bf),
            pltpu.VMEM((3 * D, rows), bf),
            pltpu.VMEM((rows, HALF), bf),
            pltpu.VMEM((rows, 8), f32),
            pltpu.VMEM((sents * 8, D), f32),
            pltpu.VMEM((2, 16, PAD, 128), f32),
            pltpu.VMEM((16, FF), f32),
            pltpu.VMEM((3 * D, SEQ), bf),
            pltpu.VMEM((16, PAD, 128), f32),
            pltpu.VMEM((SEQ, FF), f32),
            pltpu.VMEM((9, 8, FF), f32),
            pltpu.VMEM((SEQ, 128), f32),
            pltpu.VMEM((SEQ, 128), f32),
            pltpu.VMEM((PAD, HALF), f32),
            pltpu.VMEM((32, D), f32),
        ],
        compiler_params=pltpu.CompilerParams(vmem_limit_bytes=63 << 20, collective_id=0, has_side_effects=True),
        name="back",
    )(norm_gains, wg, w_glu, w_left, w_conv3, w_depth, w_point, w_qkv, *arrays)
    results = [
        shape((rows, D), f32),
        shape((rows, D), bf),
        shape((4, D), f32),
        shape((1, FF), f32),
        shape((share, 2 * D), f32),
        shape((share, FF), f32),
        shape((3, share, HALF), f32),
        shape((9, FF), f32),
        shape((wide_share, HALF), f32),
        shape((share, 3 * D), f32),
        shape((share, D), f32),
        shape((share, FF), f32),
        shape((wide_share, D), f32),
    ]
    input_grad, cell_output, norms, gain, glu, left, conv, depth, point, qkv, out, up, down = pl.pallas_call(
        functools.partial(last_kernel, share, wide_share),
        out_shape=results,
        in_specs=[anywhere] * 5,
        out_specs=[anywhere] * 13,
        scratch_shapes=[pltpu.VMEM(v.shape, v.dtype) for v in results]
        + [
            pltpu.VMEM((height, 256), bf),
            pltpu.VMEM((SMALL, FF), f32),
            pltpu.VMEM((8, D), f32),
            pltpu.SemaphoreType.DMA((8,)),
            pltpu.SemaphoreType.DMA((16,)),
        ],
        compiler_params=params,
        name="last",
    )(final, early, late, input_grad, cell)
    return cell_output, input_grad, norms, gain.reshape(FF), glu, left, conv, depth, point, qkv, out, up, down


def solution(mesh):
    dp, head = mesh.shape["dp"], mesh.shape["head"]
    ys = 2 ** ((dp.bit_length() - 1) // 2)
    grid = (dp // ys, ys)
    xs = head // 2
    row = P(("dp", "head"), None)
    in_specs = (row, P(("dp", "head")), P(("dp", "head")), row) + (P(),) * 11
    share = P("dp", None)
    out_specs = (row, row, P(), P(), share, share, P(None, "dp", None), P(), share, share, share, share, share)
    return jax.shard_map(
        functools.partial(local, grid, xs), mesh=mesh, in_specs=in_specs, out_specs=out_specs, check_vma=False
    )
```
